32 devices in a mesh: row: 8 (over z, y), col: 4 (over x, core).
Axes of the slice: x: 2, y: 2, z: 4, core: 2. Of those that a mesh axis runs over, the one named last changes fastest.
Arguments:
- image: bfloat16 [32, 512, 512], P(None, 'row', 'col'), may hold values from -6 to 6
- weight: bfloat16 [3, 3, 32, 32], replicated, may hold values from -0.375 to 0.375
- bias: float32 [32], replicated, may hold values from -3 to 3
- cotangent: bfloat16 [32, 512, 512], P(None, 'row', 'col'), may hold values from -60 to 60
Outputs:
- activation: bfloat16 [32, 512, 512], P(None, 'row', 'col')
- grad_image: bfloat16 [32, 512, 512], P(None, 'row', 'col')
- grad_weight: float32 [3, 3, 32, 32], replicated
- grad_bias: float32 [32], replicated
The draws below stay inside these ranges and needn't reach their ends.
All inputs are finite; a program needn't handle non-finite values.
Results may differ from the reference program's by a relative error of at most 0.0065.
Values may be sent and summed in bfloat16 or wider, within the bound.
No kernel may reach another device: no remote copies, remote signals or barrier semaphores. Data moves between devices by JAX's collectives and lax.ppermute only.
A program may use at most 64 MiB of HBM per device.

```python
import math
import jax
import jax.numpy as jnp
from jax import lax

FEATURE_CHANNELS = 32
DILATION_PIXELS = 16
REGION_HEIGHT = 512
REGION_WIDTH = 512


def draw_cotangent(key, part):
    first, second = jax.random.split(jax.random.fold_in(key, 17))
    rows_pos = jnp.arange(REGION_HEIGHT, dtype=jnp.float32) / REGION_HEIGHT
    cols_pos = jnp.arange(REGION_WIDTH, dtype=jnp.float32) / REGION_WIDTH
    noise = jnp.clip(jax.random.normal(first, (FEATURE_CHANNELS, REGION_HEIGHT, REGION_WIDTH), jnp.float32), -6.0, 6.0)
    ramp = 3.0 ** (rows_pos[:, None] + cols_pos[None, :])
    rough = jnp.exp(jax.random.uniform(second, (FEATURE_CHANNELS, REGION_HEIGHT, REGION_WIDTH), jnp.float32, -0.35, 0.35))
    return (noise * ramp[None, :, :] * rough * 0.7).astype(jnp.bfloat16)


def shard_levels(own_key, extent, shards, low, largest):
    factor_of, own = 1.0, jax.random.fold_in(own_key, 6)
    for dim, parts in shards:
        draws = jnp.exp(jax.random.uniform(jax.random.fold_in(own, dim), (parts,), jnp.float32, low / len(shards), largest / len(shards)))
        factor_of = factor_of * jnp.repeat(draws, extent[dim] // parts).reshape([-1 if axis == dim else 1 for axis in range(len(extent))])
    return factor_of


def bell_draw(rng, extent, spread, limit, shards=(), kind=jnp.bfloat16):
    level = shard_levels(rng, extent, shards, -0.22, 0.18) if shards else 1.0
    entries = jax.random.normal(rng, extent, jnp.float32) * spread * level
    return jnp.minimum(jnp.maximum(entries, -limit), limit).astype(kind)


def setup_inputs(seed: int = 0) -> dict:
    streams_of = jax.random.split(jax.random.key(seed), 5)
    image = bell_draw(streams_of[0], (FEATURE_CHANNELS, REGION_HEIGHT, REGION_WIDTH), 1.0, 6.0, ((1, 8), (2, 4)))
    weight = bell_draw(streams_of[1], (3, 3, FEATURE_CHANNELS, FEATURE_CHANNELS), (9 * FEATURE_CHANNELS) ** -0.5, 0.375)
    bias = bell_draw(streams_of[2], (FEATURE_CHANNELS,), 0.5, 3.0, (), jnp.float32)
    cotangent = draw_cotangent(jax.random.fold_in(streams_of[4], 71), 0)
    return {"image": image, "weight": weight, "bias": bias, "cotangent": cotangent}


def gelu_pair(preact):
    coef = 0.7978845608
    cube = preact * preact * preact
    tval = jnp.tanh(coef * (preact + 0.044715 * cube))
    value = 0.5 * preact * (1.0 + tval)
    slope_val = 0.5 * (1.0 + tval) + 0.5 * preact * (1.0 - tval * tval) * coef * (1.0 + 3.0 * 0.044715 * preact * preact)
    return (value, slope_val)

def window(source, row_offset, column_offset):
    start_row = DILATION_PIXELS + row_offset * DILATION_PIXELS
    start_column = DILATION_PIXELS + column_offset * DILATION_PIXELS
    piece = source[:, start_row:start_row + REGION_HEIGHT, start_column:start_column + REGION_WIDTH]
    return piece.reshape(FEATURE_CHANNELS, REGION_HEIGHT * REGION_WIDTH)

def reference(image, weight, bias, cotangent):
    padded_input = jnp.pad(image, ((0, 0), (DILATION_PIXELS, DILATION_PIXELS), (DILATION_PIXELS, DILATION_PIXELS)))
    preact = jnp.zeros((FEATURE_CHANNELS, REGION_HEIGHT * REGION_WIDTH), jnp.float32) + bias.astype(jnp.float32)[:, None]
    for row_offset in (-1, 0, 1):
        for column_offset in (-1, 0, 1):
            preact = preact + jnp.dot(weight[row_offset + 1, column_offset + 1], window(padded_input, row_offset, column_offset), preferred_element_type=jnp.float32)
    value, slope_val = gelu_pair(preact)
    activation = value.astype(jnp.bfloat16).reshape(FEATURE_CHANNELS, REGION_HEIGHT, REGION_WIDTH)
    cot_flat = cotangent.reshape(FEATURE_CHANNELS, REGION_HEIGHT * REGION_WIDTH).astype(jnp.float32)
    preact_gradient = (cot_flat * slope_val).astype(jnp.bfloat16)
    scale = 1.0 / math.sqrt(REGION_HEIGHT * REGION_WIDTH)
    taps = []
    for row_offset in (-1, 0, 1):
        line = []
        for column_offset in (-1, 0, 1):
            line.append(jnp.dot(preact_gradient, window(padded_input, row_offset, column_offset).T, preferred_element_type=jnp.float32) * scale)
        taps.append(jnp.stack(line))
    grad_weight = jnp.stack(taps)
    grad_bias = lax.optimization_barrier(jnp.sum(preact_gradient.astype(jnp.float32), axis=1)) * scale
    padded_gradient = jnp.pad(preact_gradient.reshape(FEATURE_CHANNELS, REGION_HEIGHT, REGION_WIDTH), ((0, 0), (DILATION_PIXELS, DILATION_PIXELS), (DILATION_PIXELS, DILATION_PIXELS)))
    total = jnp.zeros((FEATURE_CHANNELS, REGION_HEIGHT * REGION_WIDTH), jnp.float32)
    for row_offset in (-1, 0, 1):
        for column_offset in (-1, 0, 1):
            total = total + jnp.dot(weight[row_offset + 1, column_offset + 1].T, window(padded_gradient, -row_offset, -column_offset), preferred_element_type=jnp.float32)
    grad_image = total.astype(jnp.bfloat16).reshape(FEATURE_CHANNELS, REGION_HEIGHT, REGION_WIDTH)
    return (activation, grad_image, grad_weight, grad_bias)
```

```python
import math

import jax
import jax.numpy as jnp
from jax import lax
from jax.sharding import PartitionSpec as P

DILATION_PIXELS = 16


def from_behind(value, axis, steps):
    count = lax.axis_size(axis)
    initial, last = (max(0, -steps), min(count, count - steps))
    return lax.ppermute(value, axis, [(source, source + steps) for source in range(initial, last)])


def gelu_pair(preact):
    coef = 0.7978845608
    cube = preact * preact * preact
    tval = jnp.tanh(coef * (preact + 0.044715 * cube))
    value = 0.5 * preact * (1.0 + tval)
    slope_val = 0.5 * (1.0 + tval) + 0.5 * preact * (1.0 - tval * tval) * coef * (
        1.0 + 3.0 * 0.044715 * preact * preact
    )
    return (value, slope_val)


def extended(local_block):
    row_count = local_block.shape[1]
    column_count = local_block.shape[2]
    upper_neighbour = from_behind(local_block[:, row_count - DILATION_PIXELS :, :], "row", 1)
    lower_neighbour = from_behind(local_block[:, :DILATION_PIXELS, :], "row", -1)
    tall_block = jnp.concatenate([upper_neighbour, local_block, lower_neighbour], axis=1)
    left_margin = from_behind(tall_block[:, :, column_count - DILATION_PIXELS :], "col", 1)
    right_margin = from_behind(tall_block[:, :, :DILATION_PIXELS], "col", -1)
    return jnp.concatenate([left_margin, tall_block, right_margin], axis=2)


def tap_view(ext, row_offset, column_offset, row_count, column_count):
    start_row = DILATION_PIXELS + row_offset * DILATION_PIXELS
    start_column = DILATION_PIXELS + column_offset * DILATION_PIXELS
    return ext[:, start_row : start_row + row_count, start_column : start_column + column_count]


def row_stack(ext, row_offset, sign_flip, row_count, column_count):
    return jnp.concatenate(
        [
            tap_view(
                ext, sign_flip * row_offset, sign_flip * column_offset, row_count, column_count
            )
            for column_offset in (-1, 0, 1)
        ],
        axis=0,
    )


def shards(image, weight, bias, cotangent):
    row_count = image.shape[1]
    column_count = image.shape[2]
    channels = image.shape[0]
    height_all = row_count * lax.axis_size("row")
    width_all = column_count * lax.axis_size("col")
    scale = 1.0 / math.sqrt(height_all * width_all)
    image_ext = extended(image)
    preact = jnp.zeros(image.shape, jnp.float32) + bias[:, None, None]
    for row_offset in (-1, 0, 1):
        weight_row = jnp.transpose(weight[row_offset + 1], (1, 0, 2)).reshape(
            channels, 3 * channels
        )
        stacked = row_stack(image_ext, row_offset, 1, row_count, column_count)
        preact = preact + jnp.einsum(
            "ok,krq->orq", weight_row, stacked, preferred_element_type=jnp.float32
        )
    value, slope_val = gelu_pair(preact)
    activation = value.astype(jnp.bfloat16)
    preact_gradient = (cotangent.astype(jnp.float32) * slope_val).astype(jnp.bfloat16)
    taps = []
    for row_offset in (-1, 0, 1):
        stacked = row_stack(image_ext, row_offset, 1, row_count, column_count)
        joined = (
            jnp.einsum("orq,krq->ok", preact_gradient, stacked, preferred_element_type=jnp.float32)
            * scale
        )
        taps.append(jnp.transpose(joined.reshape(channels, 3, channels), (1, 0, 2)))
    local_weight = jnp.stack(taps)
    local_bias = jnp.sum(preact_gradient.astype(jnp.float32), axis=(1, 2)) * scale
    count = local_weight.size + local_bias.size
    terms = jnp.concatenate([local_weight.reshape(-1), local_bias])
    terms = jnp.pad(terms, (0, -count % 1024)).reshape(-1, 128)
    summed = jnp.sum(lax.all_gather(terms, ("row", "col")), axis=0).reshape(-1)
    grad_weight = summed[: local_weight.size].reshape(local_weight.shape)
    grad_bias = summed[local_weight.size : count]
    grad_ext = extended(preact_gradient)
    total = jnp.zeros(image.shape, jnp.float32)
    for row_offset in (-1, 0, 1):
        weight_row = weight[row_offset + 1].reshape(3 * channels, channels)
        stacked = row_stack(grad_ext, row_offset, -1, row_count, column_count)
        total = total + jnp.einsum(
            "kc,krq->crq", weight_row, stacked, preferred_element_type=jnp.float32
        )
    grad_image = total.astype(jnp.bfloat16)
    return (activation, grad_image, grad_weight, grad_bias)


def solution(mesh):
    return jax.shard_map(
        shards,
        mesh=mesh,
        in_specs=(P(None, "row", "col"), P(), P(), P(None, "row", "col")),
        out_specs=(P(None, "row", "col"), P(None, "row", "col"), P(), P()),
        check_vma=False,
    )
```

```python
import math

import jax
import jax.numpy as jnp
from jax import lax
from jax.sharding import PartitionSpec as P

DILATION_PIXELS = 16


def from_behind(value, axis, steps):
    count = lax.axis_size(axis)
    initial, last = (max(0, -steps), min(count, count - steps))
    return lax.ppermute(value, axis, [(source, source + steps) for source in range(initial, last)])


def pair_sum(value, axis):
    count = lax.axis_size(axis)
    if count & (count - 1):
        return lax.psum(value, axis)
    step = 1
    while step < count:
        value = value + lax.ppermute(value, axis, [(place, place ^ step) for place in range(count)])
        step *= 2
    return value


def gelu_pair(preact):
    coef = 0.7978845608
    cube = preact * preact * preact
    tval = jnp.tanh(coef * (preact + 0.044715 * cube))
    value = 0.5 * preact * (1.0 + tval)
    slope_val = 0.5 * (1.0 + tval) + 0.5 * preact * (1.0 - tval * tval) * coef * (
        1.0 + 3.0 * 0.044715 * preact * preact
    )
    return (value, slope_val)


def extended(local_block):
    row_count = local_block.shape[1]
    column_count = local_block.shape[2]
    upper_neighbour = from_behind(local_block[:, row_count - DILATION_PIXELS :, :], "row", 1)
    lower_neighbour = from_behind(local_block[:, :DILATION_PIXELS, :], "row", -1)
    tall_block = jnp.concatenate([upper_neighbour, local_block, lower_neighbour], axis=1)
    left_margin = from_behind(tall_block[:, :, column_count - DILATION_PIXELS :], "col", 1)
    right_margin = from_behind(tall_block[:, :, :DILATION_PIXELS], "col", -1)
    return jnp.concatenate([left_margin, tall_block, right_margin], axis=2)


def tap_view(ext, row_offset, column_offset, row_count, column_count):
    start_row = DILATION_PIXELS + row_offset * DILATION_PIXELS
    start_column = DILATION_PIXELS + column_offset * DILATION_PIXELS
    return ext[:, start_row : start_row + row_count, start_column : start_column + column_count]


def row_stack(ext, row_offset, sign_flip, row_count, column_count):
    return jnp.concatenate(
        [
            tap_view(
                ext, sign_flip * row_offset, sign_flip * column_offset, row_count, column_count
            )
            for column_offset in (-1, 0, 1)
        ],
        axis=0,
    )


def shards(image, weight, bias, cotangent):
    row_count = image.shape[1]
    column_count = image.shape[2]
    channels = image.shape[0]
    height_all = row_count * lax.axis_size("row")
    width_all = column_count * lax.axis_size("col")
    scale = 1.0 / math.sqrt(height_all * width_all)
    image_ext = extended(image)
    preact = jnp.zeros(image.shape, jnp.float32) + bias[:, None, None]
    for row_offset in (-1, 0, 1):
        weight_row = jnp.transpose(weight[row_offset + 1], (1, 0, 2)).reshape(
            channels, 3 * channels
        )
        stacked = row_stack(image_ext, row_offset, 1, row_count, column_count)
        preact = preact + jnp.einsum(
            "ok,krq->orq", weight_row, stacked, preferred_element_type=jnp.float32
        )
    value, slope_val = gelu_pair(preact)
    activation = value.astype(jnp.bfloat16)
    preact_gradient = (cotangent.astype(jnp.float32) * slope_val).astype(jnp.bfloat16)
    taps = []
    for row_offset in (-1, 0, 1):
        stacked = row_stack(image_ext, row_offset, 1, row_count, column_count)
        joined = (
            jnp.einsum("orq,krq->ok", preact_gradient, stacked, preferred_element_type=jnp.float32)
            * scale
        )
        taps.append(jnp.transpose(joined.reshape(channels, 3, channels), (1, 0, 2)))
    local_weight = jnp.stack(taps)
    local_bias = jnp.sum(preact_gradient.astype(jnp.float32), axis=(1, 2)) * scale
    count = local_weight.size + local_bias.size
    terms = jnp.concatenate([local_weight.reshape(-1), local_bias])
    terms = jnp.pad(terms, (0, -count % 1024)).reshape(-1, 128)
    summed = pair_sum(pair_sum(terms, "col"), "row").reshape(-1)
    grad_weight = summed[: local_weight.size].reshape(local_weight.shape)
    grad_bias = summed[local_weight.size : count]
    grad_ext = extended(preact_gradient)
    total = jnp.zeros(image.shape, jnp.float32)
    for row_offset in (-1, 0, 1):
        weight_row = weight[row_offset + 1].reshape(3 * channels, channels)
        stacked = row_stack(grad_ext, row_offset, -1, row_count, column_count)
        total = total + jnp.einsum(
            "kc,krq->crq", weight_row, stacked, preferred_element_type=jnp.float32
        )
    grad_image = total.astype(jnp.bfloat16)
    return (activation, grad_image, grad_weight, grad_bias)


def solution(mesh):
    return jax.shard_map(
        shards,
        mesh=mesh,
        in_specs=(P(None, "row", "col"), P(), P(), P(None, "row", "col")),
        out_specs=(P(None, "row", "col"), P(None, "row", "col"), P(), P()),
        check_vma=False,
    )
```

```python
import functools
import math

import jax
import jax.numpy as jnp
from jax import lax
from jax.experimental import pallas as pl
from jax.experimental.pallas import tpu as pltpu
from jax.sharding import PartitionSpec as P

DILATION = 16
VMEM_BYTES = 16 * 2**20


def from_behind(value, axis, steps):
    count = lax.axis_size(axis)
    initial, last = (max(0, -steps), min(count, count - steps))
    return lax.ppermute(value, axis, [(source, source + steps) for source in range(initial, last)])


def add_pairs(value, axes):
    other = None
    for axis in axes:
        count = lax.axis_size(axis)
        step = 1
        while step < count:
            value = value if other is None else value + other
            other = lax.ppermute(value, axis, [(place, place ^ step) for place in range(count)])
            step *= 2
    return value, jnp.zeros_like(value) if other is None else other


def gelu_pair(preact):
    coef = 0.7978845608
    square = preact * preact
    tval = jnp.tanh(coef * (preact + 0.044715 * (square * preact)))
    half = 0.5 * (1.0 + tval)
    slope_val = half + 0.5 * preact * (1.0 - tval * tval) * coef * (1.0 + 3.0 * 0.044715 * square)
    return (preact * half, slope_val)


def lane_of(shape):
    return lax.broadcasted_iota(jnp.int32, shape, len(shape) - 1)


def pack_group(rows):
    half = len(rows) // 2
    width = rows[0].shape[-1]
    lane = lane_of(rows[0].shape)
    pair = lane // (2 * DILATION)
    front = lane % (2 * DILATION) < DILATION

    def joined(part):
        total = pltpu.roll(part[0], DILATION, 1)
        for k in range(1, half):
            total = jnp.where(pair == k, pltpu.roll(part[k], DILATION + 2 * DILATION * k, 1), total)
        return total

    low, high = joined(rows[:half]), joined(rows[half:])
    first = jnp.where(front, pltpu.roll(low, width - DILATION, 1), high)
    last = jnp.where(front, low, pltpu.roll(high, DILATION, 1))
    return first, last


def unpack_group(from_left, from_right, count):
    half = count // 2
    width = from_left.shape[-1]
    front = lane_of(from_left.shape) % (2 * DILATION) < DILATION
    low = jnp.where(front, from_right, pltpu.roll(from_left, DILATION, 1))
    high = jnp.where(front, pltpu.roll(from_right, width - DILATION, 1), from_left)
    return [
        pltpu.roll(low if k < half else high, (width - DILATION - 2 * DILATION * (k % half)) % width, 1)
        for k in range(count)
    ]


def pack_rows(block, store, first_group):
    pieces = block.shape[-1] // DILATION
    for group in range(block.shape[0] // pieces):
        first, last = pack_group([block[group * pieces + k] for k in range(pieces)])
        store(first_group + group, first, last)


def own_kernel(image_ref, rows_ref, rims_ref):
    count = image_ref.shape[1] // DILATION
    groups = rims_ref.shape[1] // count

    def store(place, first, last):
        rims_ref[0, place] = first
        rims_ref[1, place] = last

    def body(block, carry):
        start = pl.multiple_of(block * DILATION, DILATION)
        rows = jnp.swapaxes(image_ref[:, pl.ds(start, DILATION), :], 0, 1)
        rows_ref[pl.ds(start, DILATION)] = rows
        pack_rows(rows, store, block * groups)
        return carry

    lax.fori_loop(0, count, body, 0)


def rim_kernel(swap, upper_ref, lower_ref, rims_ref, first_ref, last_ref, *rows_refs):
    own = rims_ref.shape[1]
    groups = (first_ref.shape[0] - own) // 2
    first_ref[groups : groups + own] = rims_ref[0]
    last_ref[groups : groups + own] = rims_ref[1]

    def store(place, first, last):
        first_ref[place] = first
        last_ref[place] = last

    for index, ref in enumerate((upper_ref, lower_ref)):
        rows = jnp.swapaxes(ref[...], 0, 1) if swap else ref[...]
        if swap:
            rows_refs[0][index] = rows
        pack_rows(rows, store, index * (groups + own))


def spread(rows_of, left_ref, right_ref, stack_ref, block, group_start):
    channels, width = left_ref.shape[1:]
    pieces = width // DILATION
    lane = lane_of((channels, width))
    for group in range(DILATION // pieces):
        rims = unpack_group(left_ref[group_start + group], right_ref[group_start + group], pieces)
        for k in range(pieces):
            row = group * pieces + k
            value = rows_of(row)
            columns = slice(row * width, (row + 1) * width)
            before = jnp.where(lane < DILATION, rims[k], pltpu.roll(value, DILATION, 1))
            after = jnp.where(lane >= width - DILATION, rims[k], pltpu.roll(value, width - DILATION, 1))
            stack_ref[block, 0:channels, columns] = before
            stack_ref[block, channels : 2 * channels, columns] = value
            stack_ref[block, 2 * channels : 3 * channels, columns] = after


def spread_all(own_ref, upper_of, lower_of, left_ref, right_ref, stack_ref):
    count = own_ref.shape[0] // DILATION
    groups = left_ref.shape[0] // (count + 2)
    spread(upper_of, left_ref, right_ref, stack_ref, 0, 0)

    def body(block, carry):
        spread(
            lambda row: own_ref[block * DILATION + row],
            left_ref, right_ref, stack_ref, block + 1, (block + 1) * groups,
        )
        return carry

    lax.fori_loop(0, count, body, 0)
    spread(lower_of, left_ref, right_ref, stack_ref, count + 1, (count + 1) * groups)


def forward_kernel(
    scale, own_ref, outer_ref, left_ref, right_ref, cotangent_ref, weight_ref, bias_ref,
    activation_ref, grad_ref, upper_ref, lower_ref, rims_ref, terms_ref, stack_ref, sum_ref,
):
    height, channels, width = own_ref.shape
    count = height // DILATION
    groups = rims_ref.shape[1] // count
    spread_all(
        own_ref, lambda row: outer_ref[0, row], lambda row: outer_ref[1, row], left_ref, right_ref, stack_ref
    )
    terms_ref[...] = jnp.zeros_like(terms_ref)
    sum_ref[...] = jnp.zeros_like(sum_ref)
    depth = 9 * channels

    def store(place, first, last):
        rims_ref[0, place] = first
        rims_ref[1, place] = last

    def body(block, carry):
        start = pl.multiple_of(block * DILATION, DILATION)
        stacked = stack_ref[pl.ds(block, 3)].reshape(depth, DILATION * width)
        preact = jnp.dot(weight_ref[...], stacked, preferred_element_type=jnp.float32)
        cotangent = jnp.swapaxes(cotangent_ref[:, pl.ds(start, DILATION), :], 0, 1)
        bias = jnp.broadcast_to(bias_ref[...], (channels, width))
        values, grads = [], []
        total = sum_ref[...]
        for row in range(DILATION):
            value, slope_val = gelu_pair(preact[:, row * width : (row + 1) * width] + bias)
            values.append(value.astype(jnp.bfloat16))
            grad = (cotangent[row].astype(jnp.float32) * slope_val).astype(jnp.bfloat16)
            grads.append(grad)
            total = total + grad.astype(jnp.float32)
            grad_ref[start + row] = grad
        sum_ref[...] = total
        activation_ref[:, pl.ds(start, DILATION), :] = jnp.swapaxes(jnp.stack(values), 0, 1)
        terms_ref[:, :depth] += lax.dot_general(
            jnp.concatenate(grads, axis=1), stacked, (((1,), (1,)), ((), ())),
            preferred_element_type=jnp.float32,
        )
        pack_rows(grads_stack(grads), store, block * groups)
        return carry

    lax.fori_loop(0, count, body, 0)
    upper_ref[...] = grad_ref[:DILATION]
    lower_ref[...] = grad_ref[height - DILATION :]
    terms_ref[:, :depth] = terms_ref[:, :depth] * scale
    sums = jnp.sum(sum_ref[...], axis=1, keepdims=True) * scale
    terms_ref[:, depth:] = jnp.broadcast_to(sums, (channels, terms_ref.shape[1] - depth))


def grads_stack(grads):
    return jnp.stack(grads)


def backward_kernel(
    own_ref, upper_ref, lower_ref, left_ref, right_ref, weight_ref, out_ref, stack_ref
):
    height, channels, width = own_ref.shape
    spread_all(
        own_ref, lambda row: upper_ref[row], lambda row: lower_ref[row], left_ref, right_ref, stack_ref
    )

    def body(block, carry):
        start = pl.multiple_of(block * DILATION, DILATION)
        stacked = stack_ref[pl.ds(block, 3)].reshape(9 * channels, DILATION * width)
        total = jnp.dot(weight_ref[...], stacked, preferred_element_type=jnp.float32).astype(jnp.bfloat16)
        rows = jnp.stack([total[:, row * width : (row + 1) * width] for row in range(DILATION)])
        out_ref[:, pl.ds(start, DILATION), :] = jnp.swapaxes(rows, 0, 1)
        return carry

    lax.fori_loop(0, height // DILATION, body, 0)


def finish_kernel(one_ref, other_ref, weight_ref, bias_ref):
    total = one_ref[...] + other_ref[...]
    channels = total.shape[0]
    for tap in range(9):
        weight_ref[tap // 3, tap % 3] = total[:, tap * channels : (tap + 1) * channels]
    flipped = jnp.transpose(total[:, total.shape[1] - 128 :])
    bias_ref[...] = flipped[127:128, :channels]


def call(kernel, out_shapes, operands, scratch=(), flops=0):
    size = sum(math.prod(x.shape) * jnp.dtype(x.dtype).itemsize for x in (*operands, *out_shapes))
    return pl.pallas_call(
        kernel,
        out_shape=out_shapes,
        scratch_shapes=list(scratch),
        compiler_params=pltpu.CompilerParams(vmem_limit_bytes=VMEM_BYTES),
        cost_estimate=pl.CostEstimate(flops=flops, bytes_accessed=size, transcendentals=0),
    )(*operands)


def shards(image, weight, bias, cotangent):
    channels, height, width = image.shape
    bf16, f32 = jnp.bfloat16, jnp.float32
    scale = 1.0 / math.sqrt(height * lax.axis_size("row") * width * lax.axis_size("col"))
    shape = jax.ShapeDtypeStruct
    pieces = width // DILATION
    own_groups, all_groups = height // pieces, (height + 2 * DILATION) // pieces
    depth = 9 * channels
    stack = pltpu.VMEM((height // DILATION + 2, 3 * channels, DILATION * width), bf16)
    edge = shape((DILATION, channels, width), bf16)
    packed = shape((all_groups, channels, width), bf16)
    own_rims = shape((2, own_groups, channels, width), bf16)
    rows = shape((height, channels, width), bf16)
    flops = 2 * depth * channels * height * width

    upper = from_behind(image[:, height - DILATION :, :], "row", 1)
    lower = from_behind(image[:, :DILATION, :], "row", -1)
    image_rows, rims = call(own_kernel, (rows, own_rims), (image,))
    forward_weight = jnp.transpose(weight, (2, 0, 1, 3)).reshape(channels, depth)
    backward_weight = jnp.transpose(weight[::-1, ::-1], (3, 0, 1, 2)).reshape(channels, depth)
    first, last, outer = call(
        functools.partial(rim_kernel, True),
        (packed, packed, shape((2, DILATION, channels, width), bf16)),
        (upper, lower, rims),
    )
    left = from_behind(last, "col", 1)
    right = from_behind(first, "col", -1)
    activation, grads, top, bottom, rims, terms = call(
        functools.partial(forward_kernel, scale),
        (
            shape(image.shape, bf16), rows, edge, edge, own_rims,
            shape((channels, -(-(depth + 1) // 128) * 128), f32),
        ),
        (image_rows, outer, left, right, cotangent, forward_weight, bias[:, None]),
        (stack, pltpu.VMEM((channels, width), f32)),
        2 * flops,
    )
    upper = from_behind(bottom, "row", 1)
    lower = from_behind(top, "row", -1)
    first, last = call(functools.partial(rim_kernel, False), (packed, packed), (upper, lower, rims))
    left = from_behind(last, "col", 1)
    right = from_behind(first, "col", -1)
    (grad_image,) = call(
        backward_kernel,
        (shape(image.shape, bf16),),
        (grads, upper, lower, left, right, backward_weight),
        (stack,),
        flops,
    )
    one, other = add_pairs(terms, ("col", "row"))
    grad_weight, grad_bias = call(
        finish_kernel, (shape(weight.shape, f32), shape((1, channels), f32)), (one, other)
    )
    return (activation, grad_image, grad_weight, grad_bias.reshape(channels))


def solution(mesh):
    return jax.shard_map(
        shards,
        mesh=mesh,
        in_specs=(P(None, "row", "col"), P(), P(), P(None, "row", "col")),
        out_specs=(P(None, "row", "col"), P(None, "row", "col"), P(), P()),
        check_vma=False,
    )
```

```python
import functools
import math

import jax
import jax.numpy as jnp
from jax import lax
from jax.experimental import pallas as pl
from jax.experimental.pallas import tpu as pltpu
from jax.sharding import PartitionSpec as P

DILATION = 16
VMEM_BYTES = 16 * 2**20


def swap_pairs(value, axis, first):
    pairs = []
    for place in range(first, lax.axis_size(axis) - 1, 2):
        pairs += [(place, place + 1), (place + 1, place)]
    return lax.ppermute(value, axis, pairs)


def add_pairs(value, axes):
    other = None
    for axis in axes:
        count = lax.axis_size(axis)
        step = 1
        while step < count:
            value = value if other is None else value + other
            other = lax.ppermute(value, axis, [(place, place ^ step) for place in range(count)])
            step *= 2
    return value, jnp.zeros_like(value) if other is None else other


def gelu_pair(preact):
    coef = 0.7978845608
    square = preact * preact
    tval = jnp.tanh(coef * (preact + 0.044715 * (square * preact)))
    half = 0.5 * (1.0 + tval)
    slope_val = half + 0.5 * preact * (1.0 - tval * tval) * coef * (1.0 + 3.0 * 0.044715 * square)
    return (preact * half, slope_val)


def lane_of(shape):
    return lax.broadcasted_iota(jnp.int32, shape, len(shape) - 1)


def pack_group(rows):
    half = len(rows) // 2
    width = rows[0].shape[-1]
    lane = lane_of(rows[0].shape)
    pair = lane // (2 * DILATION)
    front = lane % (2 * DILATION) < DILATION

    def joined(part):
        total = pltpu.roll(part[0], DILATION, 1)
        for k in range(1, half):
            total = jnp.where(pair == k, pltpu.roll(part[k], DILATION + 2 * DILATION * k, 1), total)
        return total

    low, high = joined(rows[:half]), joined(rows[half:])
    first = jnp.where(front, pltpu.roll(low, width - DILATION, 1), high)
    last = jnp.where(front, low, pltpu.roll(high, DILATION, 1))
    return first, last


def unpack_group(from_left, from_right, count):
    half = count // 2
    width = from_left.shape[-1]
    front = lane_of(from_left.shape) % (2 * DILATION) < DILATION
    low = jnp.where(front, from_right, pltpu.roll(from_left, DILATION, 1))
    high = jnp.where(front, pltpu.roll(from_right, width - DILATION, 1), from_left)
    return [
        pltpu.roll(low if k < half else high, (width - DILATION - 2 * DILATION * (k % half)) % width, 1)
        for k in range(count)
    ]


def pack_rows(block, store, first_group):
    pieces = block.shape[-1] // DILATION
    for group in range(block.shape[0] // pieces):
        first, last = pack_group([block[group * pieces + k] for k in range(pieces)])
        store(first_group + group, first, last)


def own_kernel(image_ref, rows_ref, rims_ref):
    count = image_ref.shape[1] // DILATION
    groups = rims_ref.shape[1] // count

    def store(place, first, last):
        rims_ref[0, place] = first
        rims_ref[1, place] = last

    def body(block, carry):
        start = pl.multiple_of(block * DILATION, DILATION)
        rows = jnp.swapaxes(image_ref[:, pl.ds(start, DILATION), :], 0, 1)
        rows_ref[pl.ds(start, DILATION)] = rows
        pack_rows(rows, store, block * groups)
        return carry

    lax.fori_loop(0, count, body, 0)


def rim_kernel(swap, odd_ref, one_ref, two_ref, rims_ref, send_one_ref, send_two_ref, outer_ref):
    own = rims_ref.shape[1]
    groups = (send_one_ref.shape[0] - own) // 2
    odd_row, odd_column = odd_ref[0] == 1, odd_ref[1] == 1
    send_one_ref[groups : groups + own] = rims_ref[1 - odd_ref[1]]
    send_two_ref[groups : groups + own] = rims_ref[odd_ref[1]]

    def store(place, first, last):
        send_one_ref[place] = jnp.where(odd_column, first, last)
        send_two_ref[place] = jnp.where(odd_column, last, first)

    one, two = one_ref[...], two_ref[...]
    for index, rows in enumerate((jnp.where(odd_row, one, two), jnp.where(odd_row, two, one))):
        rows = jnp.swapaxes(rows, 0, 1) if swap else rows
        outer_ref[index] = rows
        pack_rows(rows, store, index * (groups + own))


def spread(rows_of, odd, one_ref, two_ref, stack_ref, block, group_start):
    channels, width = one_ref.shape[1:]
    pieces = width // DILATION
    lane = lane_of((channels, width))
    for group in range(DILATION // pieces):
        one, two = one_ref[group_start + group], two_ref[group_start + group]
        rims = unpack_group(jnp.where(odd, one, two), jnp.where(odd, two, one), pieces)
        for k in range(pieces):
            row = group * pieces + k
            value = rows_of(row)
            columns = slice(row * width, (row + 1) * width)
            before = jnp.where(lane < DILATION, rims[k], pltpu.roll(value, DILATION, 1))
            after = jnp.where(lane >= width - DILATION, rims[k], pltpu.roll(value, width - DILATION, 1))
            stack_ref[block, 0:channels, columns] = before
            stack_ref[block, channels : 2 * channels, columns] = value
            stack_ref[block, 2 * channels : 3 * channels, columns] = after


def spread_all(odd_ref, own_ref, outer_ref, one_ref, two_ref, stack_ref):
    count = own_ref.shape[0] // DILATION
    groups = one_ref.shape[0] // (count + 2)
    odd = odd_ref[1] == 1
    spread(lambda row: outer_ref[0, row], odd, one_ref, two_ref, stack_ref, 0, 0)

    def body(block, carry):
        spread(
            lambda row: own_ref[block * DILATION + row],
            odd, one_ref, two_ref, stack_ref, block + 1, (block + 1) * groups,
        )
        return carry

    lax.fori_loop(0, count, body, 0)
    spread(lambda row: outer_ref[1, row], odd, one_ref, two_ref, stack_ref, count + 1, (count + 1) * groups)


def forward_kernel(
    scale, odd_ref, own_ref, outer_ref, one_ref, two_ref, cotangent_ref, weight_ref, bias_ref,
    activation_ref, grad_ref, send_one_ref, send_two_ref, rims_ref, terms_ref, stack_ref, sum_ref,
):
    height, channels, width = own_ref.shape
    count = height // DILATION
    groups = rims_ref.shape[1] // count
    spread_all(odd_ref, own_ref, outer_ref, one_ref, two_ref, stack_ref)
    terms_ref[...] = jnp.zeros_like(terms_ref)
    sum_ref[...] = jnp.zeros_like(sum_ref)
    depth = 9 * channels

    def store(place, first, last):
        rims_ref[0, place] = first
        rims_ref[1, place] = last

    def body(block, carry):
        start = pl.multiple_of(block * DILATION, DILATION)
        stacked = stack_ref[pl.ds(block, 3)].reshape(depth, DILATION * width)
        preact = jnp.dot(weight_ref[...], stacked, preferred_element_type=jnp.float32)
        cotangent = jnp.swapaxes(cotangent_ref[:, pl.ds(start, DILATION), :], 0, 1)
        bias = jnp.broadcast_to(bias_ref[...], (channels, width))
        values, grads = [], []
        total = sum_ref[...]
        for row in range(DILATION):
            value, slope_val = gelu_pair(preact[:, row * width : (row + 1) * width] + bias)
            values.append(value.astype(jnp.bfloat16))
            grad = (cotangent[row].astype(jnp.float32) * slope_val).astype(jnp.bfloat16)
            grads.append(grad)
            total = total + grad.astype(jnp.float32)
            grad_ref[start + row] = grad
        sum_ref[...] = total
        activation_ref[:, pl.ds(start, DILATION), :] = jnp.swapaxes(jnp.stack(values), 0, 1)
        terms_ref[:, :depth] += lax.dot_general(
            jnp.concatenate(grads, axis=1), stacked, (((1,), (1,)), ((), ())),
            preferred_element_type=jnp.float32,
        )
        pack_rows(jnp.stack(grads), store, block * groups)
        return carry

    lax.fori_loop(0, count, body, 0)
    end = height - DILATION
    send_one_ref[...] = grad_ref[pl.ds((1 - odd_ref[0]) * end, DILATION)]
    send_two_ref[...] = grad_ref[pl.ds(odd_ref[0] * end, DILATION)]
    terms_ref[:, :depth] = terms_ref[:, :depth] * scale
    sums = jnp.sum(sum_ref[...], axis=1, keepdims=True) * scale
    terms_ref[:, depth:] = jnp.broadcast_to(sums, (channels, terms_ref.shape[1] - depth))


def backward_kernel(
    odd_ref, own_ref, outer_ref, one_ref, two_ref, weight_ref, out_ref, stack_ref
):
    height, channels, width = own_ref.shape
    spread_all(odd_ref, own_ref, outer_ref, one_ref, two_ref, stack_ref)

    def body(block, carry):
        start = pl.multiple_of(block * DILATION, DILATION)
        stacked = stack_ref[pl.ds(block, 3)].reshape(9 * channels, DILATION * width)
        total = jnp.dot(weight_ref[...], stacked, preferred_element_type=jnp.float32).astype(jnp.bfloat16)
        rows = jnp.stack([total[:, row * width : (row + 1) * width] for row in range(DILATION)])
        out_ref[:, pl.ds(start, DILATION), :] = jnp.swapaxes(rows, 0, 1)
        return carry

    lax.fori_loop(0, height // DILATION, body, 0)


def finish_kernel(one_ref, other_ref, weight_ref, bias_ref):
    total = one_ref[...] + other_ref[...]
    channels = total.shape[0]
    for tap in range(9):
        weight_ref[tap // 3, tap % 3] = total[:, tap * channels : (tap + 1) * channels]
    flipped = jnp.transpose(total[:, total.shape[1] - 128 :])
    bias_ref[...] = flipped[127:128, :channels]


def call(kernel, out_shapes, operands, scratch=(), flops=0, scalars=0):
    whole = pl.BlockSpec(memory_space=pltpu.VMEM)
    size = sum(math.prod(x.shape) * jnp.dtype(x.dtype).itemsize for x in (*operands, *out_shapes))
    return pl.pallas_call(
        kernel,
        out_shape=out_shapes,
        in_specs=[pl.BlockSpec(memory_space=pltpu.SMEM)] * scalars + [whole] * (len(operands) - scalars),
        out_specs=[whole] * len(out_shapes),
        scratch_shapes=list(scratch),
        compiler_params=pltpu.CompilerParams(vmem_limit_bytes=VMEM_BYTES),
        cost_estimate=pl.CostEstimate(flops=flops, bytes_accessed=size, transcendentals=0),
    )(*operands)


def shards(image, weight, bias, cotangent):
    channels, height, width = image.shape
    bf16, f32 = jnp.bfloat16, jnp.float32
    scale = 1.0 / math.sqrt(height * lax.axis_size("row") * width * lax.axis_size("col"))
    shape = jax.ShapeDtypeStruct
    pieces = width // DILATION
    own_groups, all_groups = height // pieces, (height + 2 * DILATION) // pieces
    depth = 9 * channels
    stack = pltpu.VMEM((height // DILATION + 2, 3 * channels, DILATION * width), bf16)
    edge = shape((DILATION, channels, width), bf16)
    packed = shape((all_groups, channels, width), bf16)
    own_rims = shape((2, own_groups, channels, width), bf16)
    rows = shape((height, channels, width), bf16)
    flops = 2 * depth * channels * height * width

    row, column = lax.axis_index("row"), lax.axis_index("col")
    odd = jnp.stack([row % 2, column % 2]).astype(jnp.int32)
    outer = shape((2, DILATION, channels, width), bf16)
    end = height - DILATION

    one = swap_pairs(lax.dynamic_slice_in_dim(image, (1 - odd[0]) * end, DILATION, 1), "row", 0)
    two = swap_pairs(lax.dynamic_slice_in_dim(image, odd[0] * end, DILATION, 1), "row", 1)
    image_rows, rims = call(own_kernel, (rows, own_rims), (image,))
    forward_weight = jnp.transpose(weight, (2, 0, 1, 3)).reshape(channels, depth)
    backward_weight = jnp.transpose(weight[::-1, ::-1], (3, 0, 1, 2)).reshape(channels, depth)
    one, two, image_outer = call(
        functools.partial(rim_kernel, True), (packed, packed, outer), (odd, one, two, rims), scalars=1
    )
    one, two = swap_pairs(one, "col", 0), swap_pairs(two, "col", 1)
    activation, grads, one, two, rims, terms = call(
        functools.partial(forward_kernel, scale),
        (
            shape(image.shape, bf16), rows, edge, edge, own_rims,
            shape((channels, -(-(depth + 1) // 128) * 128), f32),
        ),
        (odd, image_rows, image_outer, one, two, cotangent, forward_weight, bias[:, None]),
        (stack, pltpu.VMEM((channels, width), f32)),
        2 * flops,
        1,
    )
    one, two = swap_pairs(one, "row", 0), swap_pairs(two, "row", 1)
    one, two, grad_outer = call(
        functools.partial(rim_kernel, False), (packed, packed, outer), (odd, one, two, rims), scalars=1
    )
    one, two = swap_pairs(one, "col", 0), swap_pairs(two, "col", 1)
    (grad_image,) = call(
        backward_kernel,
        (shape(image.shape, bf16),),
        (odd, grads, grad_outer, one, two, backward_weight),
        (stack,),
        flops,
        1,
    )
    one, other = add_pairs(terms, ("col", "row"))
    grad_weight, grad_bias = call(
        finish_kernel, (shape(weight.shape, f32), shape((1, channels), f32)), (one, other)
    )
    return (activation, grad_image, grad_weight, grad_bias.reshape(channels))


def solution(mesh):
    return jax.shard_map(
        shards,
        mesh=mesh,
        in_specs=(P(None, "row", "col"), P(), P(), P(None, "row", "col")),
        out_specs=(P(None, "row", "col"), P(None, "row", "col"), P(), P()),
        check_vma=False,
    )
```

```python
import functools
import math

import jax
import jax.numpy as jnp
from jax import lax
from jax.experimental import pallas as pl
from jax.experimental.pallas import tpu as pltpu
from jax.sharding import PartitionSpec as P

DILATION = 16
VMEM_BYTES = 16 * 2**20


def swap_pairs(value, axis, first):
    pairs = []
    for place in range(first, lax.axis_size(axis) - 1, 2):
        pairs += [(place, place + 1), (place + 1, place)]
    return lax.ppermute(value, axis, pairs)


def add_pairs(value, axes):
    other = None
    for axis in axes:
        count = lax.axis_size(axis)
        step = 1
        while step < count:
            value = value if other is None else value + other
            other = lax.ppermute(value, axis, [(place, place ^ step) for place in range(count)])
            step *= 2
    return value, jnp.zeros_like(value) if other is None else other


def gelu_pair(preact):
    coef = 0.7978845608
    square = preact * preact
    tval = jnp.tanh(coef * (preact + 0.044715 * (square * preact)))
    half = 0.5 * (1.0 + tval)
    slope_val = half + 0.5 * preact * (1.0 - tval * tval) * coef * (1.0 + 3.0 * 0.044715 * square)
    return (preact * half, slope_val)


def lane_of(shape):
    return lax.broadcasted_iota(jnp.int32, shape, len(shape) - 1)


def pack_group(rows):
    half = len(rows) // 2
    width = rows[0].shape[-1]
    lane = lane_of(rows[0].shape)
    pair = lane // (2 * DILATION)
    front = lane % (2 * DILATION) < DILATION

    def joined(part):
        total = pltpu.roll(part[0], DILATION, 1)
        for k in range(1, half):
            total = jnp.where(pair == k, pltpu.roll(part[k], DILATION + 2 * DILATION * k, 1), total)
        return total

    low, high = joined(rows[:half]), joined(rows[half:])
    first = jnp.where(front, pltpu.roll(low, width - DILATION, 1), high)
    last = jnp.where(front, low, pltpu.roll(high, DILATION, 1))
    return first, last


def unpack_group(from_left, from_right, count):
    half = count // 2
    width = from_left.shape[-1]
    front = lane_of(from_left.shape) % (2 * DILATION) < DILATION
    low = jnp.where(front, from_right, pltpu.roll(from_left, DILATION, 1))
    high = jnp.where(front, pltpu.roll(from_right, width - DILATION, 1), from_left)
    return [
        pltpu.roll(low if k < half else high, (width - DILATION - 2 * DILATION * (k % half)) % width, 1)
        for k in range(count)
    ]


def pack_rows(block, store, first_group):
    pieces = block.shape[-1] // DILATION
    for group in range(block.shape[0] // pieces):
        first, last = pack_group([block[group * pieces + k] for k in range(pieces)])
        store(first_group + group, first, last)


def either(flag, body, one, two):
    pl.when(flag == 1)(lambda: body(one, two))
    pl.when(flag != 1)(lambda: body(two, one))


def own_kernel(odd_ref, image_ref, bias_ref, *refs):
    weight_refs, (rows_ref, rims_ref, send_ref, wide_ref), ready_refs = refs[:2], refs[2:6], refs[6:]
    height = image_ref.shape[1]
    count = height // DILATION
    groups = rims_ref.shape[1] // count
    start = pl.multiple_of(odd_ref[0] * (height - DILATION), DILATION)
    send_ref[...] = image_ref[:, pl.ds(start, DILATION), :]
    wide_ref[...] = jnp.broadcast_to(bias_ref[...], wide_ref.shape)
    for weight_ref, ready_ref in zip(weight_refs, ready_refs):
        ready_ref[...] = weight_ref[...]

    def store(place, first, last):
        rims_ref[0, place] = first
        rims_ref[1, place] = last

    def body(block, carry):
        start = pl.multiple_of(block * DILATION, DILATION)
        rows = jnp.swapaxes(image_ref[:, pl.ds(start, DILATION), :], 0, 1)
        rows_ref[pl.ds(start, DILATION)] = rows
        pack_rows(rows, store, block * groups)
        return carry

    lax.fori_loop(0, count, body, 0)


def rim_kernel(swap, odd_ref, one_ref, two_ref, rims_ref, send_one_ref, send_two_ref, outer_ref):
    own = rims_ref.shape[1]
    groups = (send_one_ref.shape[0] - own) // 2
    send_one_ref[groups : groups + own] = rims_ref[1 - odd_ref[1]]
    send_two_ref[groups : groups + own] = rims_ref[odd_ref[1]]

    def order(upper_ref, lower_ref):
        for index, ref in enumerate((upper_ref, lower_ref)):
            outer_ref[index] = jnp.swapaxes(ref[...], 0, 1) if swap else ref[...]

    def pack(send_first_ref, send_last_ref):
        def store(place, first, last):
            send_first_ref[place] = first
            send_last_ref[place] = last

        for index in range(2):
            pack_rows(outer_ref[index], store, index * (groups + own))

    either(odd_ref[0], order, one_ref, two_ref)
    either(odd_ref[1], pack, send_one_ref, send_two_ref)


def spread(rows_of, left_ref, right_ref, stack_ref, block, group_start):
    channels, width = left_ref.shape[1:]
    pieces = width // DILATION
    lane = lane_of((channels, width))
    for group in range(DILATION // pieces):
        rims = unpack_group(left_ref[group_start + group], right_ref[group_start + group], pieces)
        for k in range(pieces):
            row = group * pieces + k
            value = rows_of(row)
            columns = slice(row * width, (row + 1) * width)
            before = jnp.where(lane < DILATION, rims[k], pltpu.roll(value, DILATION, 1))
            after = jnp.where(lane >= width - DILATION, rims[k], pltpu.roll(value, width - DILATION, 1))
            stack_ref[block, 0:channels, columns] = before
            stack_ref[block, channels : 2 * channels, columns] = value
            stack_ref[block, 2 * channels : 3 * channels, columns] = after


def spread_all(odd_ref, own_ref, outer_ref, one_ref, two_ref, stack_ref):
    count = own_ref.shape[0] // DILATION
    groups = one_ref.shape[0] // (count + 2)

    def every(left_ref, right_ref):
        spread(lambda row: outer_ref[0, row], left_ref, right_ref, stack_ref, 0, 0)

        def body(block, carry):
            spread(
                lambda row: own_ref[block * DILATION + row],
                left_ref, right_ref, stack_ref, block + 1, (block + 1) * groups,
            )
            return carry

        lax.fori_loop(0, count, body, 0)
        spread(lambda row: outer_ref[1, row], left_ref, right_ref, stack_ref, count + 1, (count + 1) * groups)

    either(odd_ref[1], every, one_ref, two_ref)


def stacked_at(stack_ref, block):
    rows, columns = stack_ref.shape[1:]
    return stack_ref[pl.ds(block, 3)].reshape(3 * rows, columns)


def forward_kernel(
    odd_ref, own_ref, outer_ref, one_ref, two_ref, cotangent_ref, weight_ref, bias_ref,
    activation_ref, grad_ref, send_ref, stack_ref,
):
    height, channels, width = own_ref.shape
    spread_all(odd_ref, own_ref, outer_ref, one_ref, two_ref, stack_ref)

    def body(block, carry):
        start = pl.multiple_of(block * DILATION, DILATION)
        preact = jnp.dot(weight_ref[...], stacked_at(stack_ref, block), preferred_element_type=jnp.float32)
        cotangent = jnp.swapaxes(cotangent_ref[:, pl.ds(start, DILATION), :], 0, 1)
        values = []
        for row in range(DILATION):
            value, slope_val = gelu_pair(preact[:, row * width : (row + 1) * width] + bias_ref[...])
            values.append(value.astype(jnp.bfloat16))
            grad_ref[start + row] = (cotangent[row].astype(jnp.float32) * slope_val).astype(jnp.bfloat16)
        activation_ref[:, pl.ds(start, DILATION), :] = jnp.swapaxes(jnp.stack(values), 0, 1)
        return carry

    lax.fori_loop(0, height // DILATION, body, 0)
    send_ref[...] = grad_ref[pl.ds((1 - odd_ref[0]) * (height - DILATION), DILATION)]


def terms_kernel(scale, odd_ref, grad_ref, stack_ref, send_ref, rims_ref, terms_ref, sum_ref):
    height, channels, width = grad_ref.shape
    count = height // DILATION
    groups = rims_ref.shape[1] // count
    depth = 9 * channels
    send_ref[...] = grad_ref[pl.ds(odd_ref[0] * (height - DILATION), DILATION)]
    terms_ref[...] = jnp.zeros_like(terms_ref)
    sum_ref[...] = jnp.zeros_like(sum_ref)

    def store(place, first, last):
        rims_ref[0, place] = first
        rims_ref[1, place] = last

    def body(block, carry):
        grads = grad_ref[pl.ds(block * DILATION, DILATION)]
        rows = [grads[row] for row in range(DILATION)]
        total = sum_ref[...]
        for row in rows:
            total = total + row.astype(jnp.float32)
        sum_ref[...] = total
        terms_ref[:, :depth] += lax.dot_general(
            jnp.concatenate(rows, axis=1), stacked_at(stack_ref, block), (((1,), (1,)), ((), ())),
            preferred_element_type=jnp.float32,
        )
        pack_rows(grads, store, block * groups)
        return carry

    lax.fori_loop(0, count, body, 0)
    terms_ref[:, :depth] = terms_ref[:, :depth] * scale
    sums = jnp.sum(sum_ref[...], axis=1, keepdims=True) * scale
    terms_ref[:, depth:] = jnp.broadcast_to(sums, (channels, terms_ref.shape[1] - depth))


def backward_kernel(
    odd_ref, own_ref, outer_ref, one_ref, two_ref, weight_ref, out_ref, stack_ref
):
    height, channels, width = own_ref.shape
    spread_all(odd_ref, own_ref, outer_ref, one_ref, two_ref, stack_ref)

    def body(block, carry):
        start = pl.multiple_of(block * DILATION, DILATION)
        total = jnp.dot(
            weight_ref[...], stacked_at(stack_ref, block), preferred_element_type=jnp.float32
        ).astype(jnp.bfloat16)
        rows = jnp.stack([total[:, row * width : (row + 1) * width] for row in range(DILATION)])
        out_ref[:, pl.ds(start, DILATION), :] = jnp.swapaxes(rows, 0, 1)
        return carry

    lax.fori_loop(0, height // DILATION, body, 0)


def finish_kernel(one_ref, other_ref, weight_ref, bias_ref):
    total = one_ref[...] + other_ref[...]
    channels = total.shape[0]
    for tap in range(9):
        weight_ref[tap // 3, tap % 3] = total[:, tap * channels : (tap + 1) * channels]
    flipped = jnp.transpose(total[:, total.shape[1] - 128 :])
    bias_ref[...] = flipped[127:128, :channels]


def call(kernel, out_shapes, operands, scratch=(), flops=0, scalars=0):
    whole = pl.BlockSpec(memory_space=pltpu.VMEM)
    size = sum(math.prod(x.shape) * jnp.dtype(x.dtype).itemsize for x in (*operands, *out_shapes))
    return pl.pallas_call(
        kernel,
        out_shape=out_shapes,
        in_specs=[pl.BlockSpec(memory_space=pltpu.SMEM)] * scalars + [whole] * (len(operands) - scalars),
        out_specs=[whole] * len(out_shapes),
        scratch_shapes=list(scratch),
        compiler_params=pltpu.CompilerParams(vmem_limit_bytes=VMEM_BYTES),
        cost_estimate=pl.CostEstimate(flops=flops, bytes_accessed=size, transcendentals=0),
    )(*operands)


def shards(image, weight, bias, cotangent):
    channels, height, width = image.shape
    bf16, f32 = jnp.bfloat16, jnp.float32
    scale = 1.0 / math.sqrt(height * lax.axis_size("row") * width * lax.axis_size("col"))
    shape = jax.ShapeDtypeStruct
    pieces = width // DILATION
    own_groups, all_groups = height // pieces, (height + 2 * DILATION) // pieces
    depth = 9 * channels
    stack_shape = (height // DILATION + 2, 3 * channels, DILATION * width)
    edge = shape((DILATION, channels, width), bf16)
    packed = shape((all_groups, channels, width), bf16)
    own_rims = shape((2, own_groups, channels, width), bf16)
    outer = shape((2, DILATION, channels, width), bf16)
    rows = shape((height, channels, width), bf16)
    weights = shape((channels, depth), bf16)
    terms = shape((channels, -(-(depth + 1) // 128) * 128), f32)
    flops = 2 * depth * channels * height * width
    odd = jnp.stack([lax.axis_index("row") % 2, lax.axis_index("col") % 2]).astype(jnp.int32)

    rim = lax.dynamic_slice_in_dim(image, (1 - odd[0]) * (height - DILATION), DILATION, 1)
    one = swap_pairs(rim, "row", 0)
    image_rows, rims, rim, wide_bias, forward_weight, backward_weight = call(
        own_kernel,
        (rows, own_rims, shape((channels, DILATION, width), bf16), shape((channels, width), f32), weights, weights),
        (
            odd, image, bias[:, None],
            jnp.transpose(weight, (2, 0, 1, 3)).reshape(channels, depth),
            jnp.transpose(weight[::-1, ::-1], (3, 0, 1, 2)).reshape(channels, depth),
        ),
        scalars=1,
    )
    two = swap_pairs(rim, "row", 1)
    one, two, image_outer = call(
        functools.partial(rim_kernel, True), (packed, packed, outer), (odd, one, two, rims), scalars=1
    )
    one, two = swap_pairs(one, "col", 0), swap_pairs(two, "col", 1)
    activation, grads, rim, stack = call(
        forward_kernel,
        (shape(image.shape, bf16), rows, edge, shape(stack_shape, bf16)),
        (odd, image_rows, image_outer, one, two, cotangent, forward_weight, wide_bias),
        flops=flops,
        scalars=1,
    )
    one = swap_pairs(rim, "row", 0)
    rim, rims, terms = call(
        functools.partial(terms_kernel, scale),
        (edge, own_rims, terms),
        (odd, grads, stack),
        (pltpu.VMEM((channels, width), f32),),
        flops,
        1,
    )
    two = swap_pairs(rim, "row", 1)
    one, two, grad_outer = call(
        functools.partial(rim_kernel, False), (packed, packed, outer), (odd, one, two, rims), scalars=1
    )
    one, two = swap_pairs(one, "col", 0), swap_pairs(two, "col", 1)
    (grad_image,) = call(
        backward_kernel,
        (shape(image.shape, bf16),),
        (odd, grads, grad_outer, one, two, backward_weight),
        (pltpu.VMEM(stack_shape, bf16),),
        flops,
        1,
    )
    one, other = add_pairs(terms, ("col", "row"))
    grad_weight, grad_bias = call(
        finish_kernel, (shape(weight.shape, f32), shape((1, channels), f32)), (one, other)
    )
    return (activation, grad_image, grad_weight, grad_bias.reshape(channels))


def solution(mesh):
    return jax.shard_map(
        shards,
        mesh=mesh,
        in_specs=(P(None, "row", "col"), P(), P(), P(None, "row", "col")),
        out_specs=(P(None, "row", "col"), P(None, "row", "col"), P(), P()),
        check_vma=False,
    )
```

```python
import functools
import math

import jax
import jax.numpy as jnp
from jax import lax
from jax.experimental import pallas as pl
from jax.experimental.pallas import tpu as pltpu
from jax.sharding import PartitionSpec as P

DILATION = 16
VMEM_BYTES = 16 * 2**20


def swap_pairs(value, axis, first):
    pairs = []
    for place in range(first, lax.axis_size(axis) - 1, 2):
        pairs += [(place, place + 1), (place + 1, place)]
    return lax.ppermute(value, axis, pairs)


def add_pairs(value, axes):
    other = None
    for axis in axes:
        count = lax.axis_size(axis)
        step = count // 2
        while step:
            value = value if other is None else value + other
            other = lax.ppermute(value, axis, [(place, place ^ step) for place in range(count)])
            step //= 2
    return value, jnp.zeros_like(value) if other is None else other


def gelu_pair(preact):
    coef = 0.7978845608
    square = preact * preact
    tval = jnp.tanh(coef * (preact + 0.044715 * (square * preact)))
    half = 0.5 * (1.0 + tval)
    slope_val = half + 0.5 * preact * (1.0 - tval * tval) * coef * (1.0 + 3.0 * 0.044715 * square)
    return (preact * half, slope_val)


def lane_of(shape):
    return lax.broadcasted_iota(jnp.int32, shape, len(shape) - 1)


def pack_group(rows):
    half = len(rows) // 2
    width = rows[0].shape[-1]
    lane = lane_of(rows[0].shape)
    pair = lane // (2 * DILATION)
    front = lane % (2 * DILATION) < DILATION

    def joined(part):
        total = pltpu.roll(part[0], DILATION, 1)
        for k in range(1, half):
            total = jnp.where(pair == k, pltpu.roll(part[k], DILATION + 2 * DILATION * k, 1), total)
        return total

    low, high = joined(rows[:half]), joined(rows[half:])
    first = jnp.where(front, pltpu.roll(low, width - DILATION, 1), high)
    last = jnp.where(front, low, pltpu.roll(high, DILATION, 1))
    return first, last


def unpack_group(from_left, from_right, count):
    half = count // 2
    width = from_left.shape[-1]
    front = lane_of(from_left.shape) % (2 * DILATION) < DILATION
    low = jnp.where(front, from_right, pltpu.roll(from_left, DILATION, 1))
    high = jnp.where(front, pltpu.roll(from_right, width - DILATION, 1), from_left)
    return [
        pltpu.roll(low if k < half else high, (width - DILATION - 2 * DILATION * (k % half)) % width, 1)
        for k in range(count)
    ]


def pack_rows(block, store, first_group):
    pieces = block.shape[-1] // DILATION
    for group in range(block.shape[0] // pieces):
        first, last = pack_group([block[group * pieces + k] for k in range(pieces)])
        store(first_group + group, first, last)


def own_kernel(image_ref, rows_ref, rims_ref):
    count = image_ref.shape[1] // DILATION
    groups = rims_ref.shape[1] // count

    def store(place, first, last):
        rims_ref[0, place] = first
        rims_ref[1, place] = last

    def body(block, carry):
        start = pl.multiple_of(block * DILATION, DILATION)
        rows = jnp.swapaxes(image_ref[:, pl.ds(start, DILATION), :], 0, 1)
        rows_ref[pl.ds(start, DILATION)] = rows
        pack_rows(rows, store, block * groups)
        return carry

    lax.fori_loop(0, count, body, 0)


def either(axis, body, one, two):
    odd = lax.axis_index(axis) % 2 == 1
    pl.when(odd)(lambda: body(one, two))
    pl.when(jnp.logical_not(odd))(lambda: body(two, one))


def rim_kernel(swap, one_ref, two_ref, rims_ref, send_one_ref, send_two_ref, outer_ref):
    own = rims_ref.shape[1]
    groups = (send_one_ref.shape[0] - own) // 2

    def order(upper_ref, lower_ref):
        for index, ref in enumerate((upper_ref, lower_ref)):
            outer_ref[index] = jnp.swapaxes(ref[...], 0, 1) if swap else ref[...]

    def pack(send_first_ref, send_last_ref):
        def store(place, first, last):
            send_first_ref[place] = first
            send_last_ref[place] = last

        send_first_ref[groups : groups + own] = rims_ref[0]
        send_last_ref[groups : groups + own] = rims_ref[1]
        for index in range(2):
            pack_rows(outer_ref[index], store, index * (groups + own))

    either("row", order, one_ref, two_ref)
    either("col", pack, send_one_ref, send_two_ref)


def spread(rows_of, left_ref, right_ref, stack_ref, block, group_start):
    channels, width = left_ref.shape[1:]
    pieces = width // DILATION
    lane = lane_of((channels, width))
    for group in range(DILATION // pieces):
        rims = unpack_group(left_ref[group_start + group], right_ref[group_start + group], pieces)
        for k in range(pieces):
            row = group * pieces + k
            value = rows_of(row)
            columns = slice(row * width, (row + 1) * width)
            before = jnp.where(lane < DILATION, rims[k], pltpu.roll(value, DILATION, 1))
            after = jnp.where(lane >= width - DILATION, rims[k], pltpu.roll(value, width - DILATION, 1))
            stack_ref[block, 0:channels, columns] = before
            stack_ref[block, channels : 2 * channels, columns] = value
            stack_ref[block, 2 * channels : 3 * channels, columns] = after


def spread_all(own_ref, outer_ref, one_ref, two_ref, stack_ref):
    count = own_ref.shape[0] // DILATION
    groups = one_ref.shape[0] // (count + 2)

    def every(left_ref, right_ref):
        spread(lambda row: outer_ref[0, row], left_ref, right_ref, stack_ref, 0, 0)

        def body(block, carry):
            spread(
                lambda row: own_ref[block * DILATION + row],
                left_ref, right_ref, stack_ref, block + 1, (block + 1) * groups,
            )
            return carry

        lax.fori_loop(0, count, body, 0)
        spread(lambda row: outer_ref[1, row], left_ref, right_ref, stack_ref, count + 1, (count + 1) * groups)

    either("col", every, one_ref, two_ref)


def forward_kernel(
    scale, own_ref, outer_ref, one_ref, two_ref, cotangent_ref, weight_ref, bias_ref,
    activation_ref, grad_ref, send_one_ref, send_two_ref, rims_ref, terms_ref, stack_ref, sum_ref,
):
    height, channels, width = own_ref.shape
    count = height // DILATION
    groups = rims_ref.shape[1] // count
    spread_all(own_ref, outer_ref, one_ref, two_ref, stack_ref)
    terms_ref[...] = jnp.zeros_like(terms_ref)
    sum_ref[...] = jnp.zeros_like(sum_ref)
    depth = 9 * channels

    def store(place, first, last):
        rims_ref[0, place] = first
        rims_ref[1, place] = last

    def body(block, carry):
        start = pl.multiple_of(block * DILATION, DILATION)
        stacked = stack_ref[pl.ds(block, 3)].reshape(depth, DILATION * width)
        preact = jnp.dot(weight_ref[...], stacked, preferred_element_type=jnp.float32)
        cotangent = jnp.swapaxes(cotangent_ref[:, pl.ds(start, DILATION), :], 0, 1)
        bias = jnp.broadcast_to(bias_ref[...], (channels, width))
        values, grads = [], []
        total = sum_ref[...]
        for row in range(DILATION):
            value, slope_val = gelu_pair(preact[:, row * width : (row + 1) * width] + bias)
            values.append(value.astype(jnp.bfloat16))
            grad = (cotangent[row].astype(jnp.float32) * slope_val).astype(jnp.bfloat16)
            grads.append(grad)
            total = total + grad.astype(jnp.float32)
            grad_ref[start + row] = grad
        sum_ref[...] = total
        activation_ref[:, pl.ds(start, DILATION), :] = jnp.swapaxes(jnp.stack(values), 0, 1)
        terms_ref[:, :depth] += lax.dot_general(
            jnp.concatenate(grads, axis=1), stacked, (((1,), (1,)), ((), ())),
            preferred_element_type=jnp.float32,
        )
        pack_rows(jnp.stack(grads), store, block * groups)
        return carry

    lax.fori_loop(0, count, body, 0)
    end = height - DILATION
    odd = lax.axis_index("row") % 2
    send_one_ref[...] = grad_ref[pl.ds((1 - odd) * end, DILATION)]
    send_two_ref[...] = grad_ref[pl.ds(odd * end, DILATION)]
    terms_ref[:, :depth] = terms_ref[:, :depth] * scale
    sums = jnp.sum(sum_ref[...], axis=1, keepdims=True) * scale
    terms_ref[:, depth:] = jnp.broadcast_to(sums, (channels, terms_ref.shape[1] - depth))


def backward_kernel(
    own_ref, outer_ref, one_ref, two_ref, weight_ref, out_ref, stack_ref
):
    height, channels, width = own_ref.shape
    spread_all(own_ref, outer_ref, one_ref, two_ref, stack_ref)

    def body(block, carry):
        start = pl.multiple_of(block * DILATION, DILATION)
        stacked = stack_ref[pl.ds(block, 3)].reshape(9 * channels, DILATION * width)
        total = jnp.dot(weight_ref[...], stacked, preferred_element_type=jnp.float32).astype(jnp.bfloat16)
        rows = jnp.stack([total[:, row * width : (row + 1) * width] for row in range(DILATION)])
        out_ref[:, pl.ds(start, DILATION), :] = jnp.swapaxes(rows, 0, 1)
        return carry

    lax.fori_loop(0, height // DILATION, body, 0)


def finish_kernel(one_ref, other_ref, weight_ref, bias_ref):
    total = one_ref[...] + other_ref[...]
    channels = total.shape[0]
    for tap in range(9):
        weight_ref[tap // 3, tap % 3] = total[:, tap * channels : (tap + 1) * channels]
    flipped = jnp.transpose(total[:, total.shape[1] - 128 :])
    bias_ref[...] = flipped[127:128, :channels]


def call(kernel, out_shapes, operands, scratch=(), flops=0):
    whole = pl.BlockSpec(memory_space=pltpu.VMEM)
    size = sum(math.prod(x.shape) * jnp.dtype(x.dtype).itemsize for x in (*operands, *out_shapes))
    return pl.pallas_call(
        kernel,
        out_shape=out_shapes,
        in_specs=[whole] * len(operands),
        out_specs=[whole] * len(out_shapes),
        scratch_shapes=list(scratch),
        compiler_params=pltpu.CompilerParams(vmem_limit_bytes=VMEM_BYTES),
        cost_estimate=pl.CostEstimate(flops=flops, bytes_accessed=size, transcendentals=0),
    )(*operands)


def shards(image, weight, bias, cotangent):
    channels, height, width = image.shape
    bf16, f32 = jnp.bfloat16, jnp.float32
    scale = 1.0 / math.sqrt(height * lax.axis_size("row") * width * lax.axis_size("col"))
    shape = jax.ShapeDtypeStruct
    pieces = width // DILATION
    own_groups, all_groups = height // pieces, (height + 2 * DILATION) // pieces
    depth = 9 * channels
    stack = pltpu.VMEM((height // DILATION + 2, 3 * channels, DILATION * width), bf16)
    edge = shape((DILATION, channels, width), bf16)
    packed = shape((all_groups, channels, width), bf16)
    own_rims = shape((2, own_groups, channels, width), bf16)
    rows = shape((height, channels, width), bf16)
    flops = 2 * depth * channels * height * width

    odd = lax.axis_index("row") % 2
    outer = shape((2, DILATION, channels, width), bf16)
    end = height - DILATION

    one = swap_pairs(lax.dynamic_slice_in_dim(image, (1 - odd) * end, DILATION, 1), "row", 0)
    two = swap_pairs(lax.dynamic_slice_in_dim(image, odd * end, DILATION, 1), "row", 1)
    image_rows, rims = call(own_kernel, (rows, own_rims), (image,))
    forward_weight = jnp.transpose(weight, (2, 0, 1, 3)).reshape(channels, depth)
    backward_weight = jnp.transpose(weight[::-1, ::-1], (3, 0, 1, 2)).reshape(channels, depth)
    one, two, image_outer = call(
        functools.partial(rim_kernel, True), (packed, packed, outer), (one, two, rims)
    )
    one, two = swap_pairs(one, "col", 0), swap_pairs(two, "col", 1)
    activation, grads, one, two, rims, terms = call(
        functools.partial(forward_kernel, scale),
        (
            shape(image.shape, bf16), rows, edge, edge, own_rims,
            shape((channels, -(-(depth + 1) // 128) * 128), f32),
        ),
        (image_rows, image_outer, one, two, cotangent, forward_weight, bias[:, None]),
        (stack, pltpu.VMEM((channels, width), f32)),
        2 * flops,
    )
    one, two = swap_pairs(one, "row", 0), swap_pairs(two, "row", 1)
    one, two, grad_outer = call(
        functools.partial(rim_kernel, False), (packed, packed, outer), (one, two, rims)
    )
    one, two = swap_pairs(one, "col", 0), swap_pairs(two, "col", 1)
    (grad_image,) = call(
        backward_kernel,
        (shape(image.shape, bf16),),
        (grads, grad_outer, one, two, backward_weight),
        (stack,),
        flops,
    )
    one, other = add_pairs(terms, ("row", "col"))
    grad_weight, grad_bias = call(
        finish_kernel, (shape(weight.shape, f32), shape((1, channels), f32)), (one, other)
    )
    return (activation, grad_image, grad_weight, grad_bias.reshape(channels))


def solution(mesh):
    return jax.shard_map(
        shards,
        mesh=mesh,
        in_specs=(P(None, "row", "col"), P(), P(), P(None, "row", "col")),
        out_specs=(P(None, "row", "col"), P(None, "row", "col"), P(), P()),
        check_vma=False,
    )
```

```python
import functools
import math

import jax
import jax.numpy as jnp
from jax import lax
from jax.experimental import pallas as pl
from jax.experimental.pallas import tpu as pltpu
from jax.sharding import PartitionSpec as P

DILATION = 16
VMEM_BYTES = 16 * 2**20


def swap_pairs(value, axis, first):
    pairs = []
    for place in range(first, lax.axis_size(axis) - 1, 2):
        pairs += [(place, place + 1), (place + 1, place)]
    return lax.ppermute(value, axis, pairs)


def add_pairs(value, near_axis, far_axis):
    near, far = lax.axis_size(near_axis), lax.axis_size(far_axis)
    steps = [(near_axis, 2**k) for k in range(near.bit_length() - 1)]
    steps += [(far_axis, 2**k) for k in reversed(range(far.bit_length() - 1))]
    other = jnp.zeros_like(value)
    for place, (axis, step) in enumerate(steps):
        value = value + other if place else value
        other = lax.ppermute(value, axis, [(at, at ^ step) for at in range(lax.axis_size(axis))])
    return value, other


def gelu_pair(preact):
    coef = 0.7978845608
    square = preact * preact
    tval = jnp.tanh(coef * (preact + 0.044715 * (square * preact)))
    half = 0.5 * (1.0 + tval)
    slope_val = half + 0.5 * preact * (1.0 - tval * tval) * coef * (1.0 + 3.0 * 0.044715 * square)
    return (preact * half, slope_val)


def lane_of(shape):
    return lax.broadcasted_iota(jnp.int32, shape, len(shape) - 1)


def pack_group(rows):
    half = len(rows) // 2
    width = rows[0].shape[-1]
    lane = lane_of(rows[0].shape)
    pair = lane // (2 * DILATION)
    front = lane % (2 * DILATION) < DILATION

    def joined(part):
        total = pltpu.roll(part[0], DILATION, 1)
        for k in range(1, half):
            total = jnp.where(pair == k, pltpu.roll(part[k], DILATION + 2 * DILATION * k, 1), total)
        return total

    low, high = joined(rows[:half]), joined(rows[half:])
    first = jnp.where(front, pltpu.roll(low, width - DILATION, 1), high)
    last = jnp.where(front, low, pltpu.roll(high, DILATION, 1))
    return first, last


def unpack_group(from_left, from_right, count):
    half = count // 2
    width = from_left.shape[-1]
    front = lane_of(from_left.shape) % (2 * DILATION) < DILATION
    low = jnp.where(front, from_right, pltpu.roll(from_left, DILATION, 1))
    high = jnp.where(front, pltpu.roll(from_right, width - DILATION, 1), from_left)
    return [
        pltpu.roll(low if k < half else high, (width - DILATION - 2 * DILATION * (k % half)) % width, 1)
        for k in range(count)
    ]


def pack_rows(block, store, first_group):
    pieces = block.shape[-1] // DILATION
    for group in range(block.shape[0] // pieces):
        first, last = pack_group([block[group * pieces + k] for k in range(pieces)])
        store(first_group + group, first, last)


def own_kernel(image_ref, rows_ref, rims_ref):
    count = image_ref.shape[1] // DILATION
    groups = rims_ref.shape[1] // count

    def store(place, first, last):
        rims_ref[0, place] = first
        rims_ref[1, place] = last

    def body(block, carry):
        start = pl.multiple_of(block * DILATION, DILATION)
        rows = jnp.swapaxes(image_ref[:, pl.ds(start, DILATION), :], 0, 1)
        rows_ref[pl.ds(start, DILATION)] = rows
        pack_rows(rows, store, block * groups)
        return carry

    lax.fori_loop(0, count, body, 0)


def either(axis, body, one, two):
    odd = lax.axis_index(axis) % 2 == 1
    pl.when(odd)(lambda: body(one, two))
    pl.when(jnp.logical_not(odd))(lambda: body(two, one))


def rim_kernel(swap, one_ref, two_ref, rims_ref, send_one_ref, send_two_ref, outer_ref):
    own = rims_ref.shape[1]
    groups = (send_one_ref.shape[0] - own) // 2

    def order(upper_ref, lower_ref):
        for index, ref in enumerate((upper_ref, lower_ref)):
            outer_ref[index] = jnp.swapaxes(ref[...], 0, 1) if swap else ref[...]

    def pack(send_first_ref, send_last_ref):
        def store(place, first, last):
            send_first_ref[place] = first
            send_last_ref[place] = last

        send_first_ref[groups : groups + own] = rims_ref[0]
        send_last_ref[groups : groups + own] = rims_ref[1]
        for index in range(2):
            pack_rows(outer_ref[index], store, index * (groups + own))

    either("row", order, one_ref, two_ref)
    either("col", pack, send_one_ref, send_two_ref)


def spread(rows_of, left_ref, right_ref, stack_ref, block, group_start):
    channels, width = left_ref.shape[1:]
    pieces = width // DILATION
    lane = lane_of((channels, width))
    for group in range(DILATION // pieces):
        rims = unpack_group(left_ref[group_start + group], right_ref[group_start + group], pieces)
        for k in range(pieces):
            row = group * pieces + k
            value = rows_of(row)
            columns = slice(row * width, (row + 1) * width)
            before = jnp.where(lane < DILATION, rims[k], pltpu.roll(value, DILATION, 1))
            after = jnp.where(lane >= width - DILATION, rims[k], pltpu.roll(value, width - DILATION, 1))
            stack_ref[block, 0:channels, columns] = before
            stack_ref[block, channels : 2 * channels, columns] = value
            stack_ref[block, 2 * channels : 3 * channels, columns] = after


def spread_all(own_ref, outer_ref, one_ref, two_ref, stack_ref):
    count = own_ref.shape[0] // DILATION
    groups = one_ref.shape[0] // (count + 2)

    def every(left_ref, right_ref):
        spread(lambda row: outer_ref[0, row], left_ref, right_ref, stack_ref, 0, 0)

        def body(block, carry):
            spread(
                lambda row: own_ref[block * DILATION + row],
                left_ref, right_ref, stack_ref, block + 1, (block + 1) * groups,
            )
            return carry

        lax.fori_loop(0, count, body, 0)
        spread(lambda row: outer_ref[1, row], left_ref, right_ref, stack_ref, count + 1, (count + 1) * groups)

    either("col", every, one_ref, two_ref)


def forward_kernel(
    scale, own_ref, outer_ref, one_ref, two_ref, cotangent_ref, weight_ref, bias_ref,
    activation_ref, grad_ref, send_one_ref, send_two_ref, rims_ref, terms_ref, stack_ref, sum_ref,
):
    height, channels, width = own_ref.shape
    count = height // DILATION
    groups = rims_ref.shape[1] // count
    spread_all(own_ref, outer_ref, one_ref, two_ref, stack_ref)
    terms_ref[...] = jnp.zeros_like(terms_ref)
    sum_ref[...] = jnp.zeros_like(sum_ref)
    depth = 9 * channels

    def store(place, first, last):
        rims_ref[0, place] = first
        rims_ref[1, place] = last

    def body(block, carry):
        start = pl.multiple_of(block * DILATION, DILATION)
        stacked = stack_ref[pl.ds(block, 3)].reshape(depth, DILATION * width)
        preact = jnp.dot(weight_ref[...], stacked, preferred_element_type=jnp.float32)
        cotangent = jnp.swapaxes(cotangent_ref[:, pl.ds(start, DILATION), :], 0, 1)
        bias = jnp.broadcast_to(bias_ref[...], (channels, width))
        values, grads = [], []
        total = sum_ref[...]
        for row in range(DILATION):
            value, slope_val = gelu_pair(preact[:, row * width : (row + 1) * width] + bias)
            values.append(value.astype(jnp.bfloat16))
            grad = (cotangent[row].astype(jnp.float32) * slope_val).astype(jnp.bfloat16)
            grads.append(grad)
            total = total + grad.astype(jnp.float32)
            grad_ref[start + row] = grad
        sum_ref[...] = total
        activation_ref[:, pl.ds(start, DILATION), :] = jnp.swapaxes(jnp.stack(values), 0, 1)
        terms_ref[:, :depth] += lax.dot_general(
            jnp.concatenate(grads, axis=1), stacked, (((1,), (1,)), ((), ())),
            preferred_element_type=jnp.float32,
        )
        pack_rows(jnp.stack(grads), store, block * groups)
        return carry

    lax.fori_loop(0, count, body, 0)
    end = height - DILATION
    odd = lax.axis_index("row") % 2
    send_one_ref[...] = grad_ref[pl.ds((1 - odd) * end, DILATION)]
    send_two_ref[...] = grad_ref[pl.ds(odd * end, DILATION)]
    terms_ref[:, :depth] = terms_ref[:, :depth] * scale
    sums = jnp.sum(sum_ref[...], axis=1, keepdims=True) * scale
    terms_ref[:, depth:] = jnp.broadcast_to(sums, (channels, terms_ref.shape[1] - depth))


def backward_kernel(
    own_ref, outer_ref, one_ref, two_ref, weight_ref, out_ref, stack_ref
):
    height, channels, width = own_ref.shape
    spread_all(own_ref, outer_ref, one_ref, two_ref, stack_ref)

    def body(block, carry):
        start = pl.multiple_of(block * DILATION, DILATION)
        stacked = stack_ref[pl.ds(block, 3)].reshape(9 * channels, DILATION * width)
        total = jnp.dot(weight_ref[...], stacked, preferred_element_type=jnp.float32).astype(jnp.bfloat16)
        rows = jnp.stack([total[:, row * width : (row + 1) * width] for row in range(DILATION)])
        out_ref[:, pl.ds(start, DILATION), :] = jnp.swapaxes(rows, 0, 1)
        return carry

    lax.fori_loop(0, height // DILATION, body, 0)


def finish_kernel(one_ref, other_ref, weight_ref, bias_ref):
    total = one_ref[...] + other_ref[...]
    channels = total.shape[0]
    for tap in range(9):
        weight_ref[tap // 3, tap % 3] = total[:, tap * channels : (tap + 1) * channels]
    flipped = jnp.transpose(total[:, total.shape[1] - 128 :])
    bias_ref[...] = flipped[127:128, :channels]


def call(kernel, out_shapes, operands, scratch=(), flops=0):
    whole = pl.BlockSpec(memory_space=pltpu.VMEM)
    size = sum(math.prod(x.shape) * jnp.dtype(x.dtype).itemsize for x in (*operands, *out_shapes))
    return pl.pallas_call(
        kernel,
        out_shape=out_shapes,
        in_specs=[whole] * len(operands),
        out_specs=[whole] * len(out_shapes),
        scratch_shapes=list(scratch),
        compiler_params=pltpu.CompilerParams(vmem_limit_bytes=VMEM_BYTES),
        cost_estimate=pl.CostEstimate(flops=flops, bytes_accessed=size, transcendentals=0),
    )(*operands)


def shards(image, weight, bias, cotangent):
    channels, height, width = image.shape
    bf16, f32 = jnp.bfloat16, jnp.float32
    scale = 1.0 / math.sqrt(height * lax.axis_size("row") * width * lax.axis_size("col"))
    shape = jax.ShapeDtypeStruct
    pieces = width // DILATION
    own_groups, all_groups = height // pieces, (height + 2 * DILATION) // pieces
    depth = 9 * channels
    stack = pltpu.VMEM((height // DILATION + 2, 3 * channels, DILATION * width), bf16)
    edge = shape((DILATION, channels, width), bf16)
    packed = shape((all_groups, channels, width), bf16)
    own_rims = shape((2, own_groups, channels, width), bf16)
    rows = shape((height, channels, width), bf16)
    flops = 2 * depth * channels * height * width

    odd = lax.axis_index("row") % 2
    outer = shape((2, DILATION, channels, width), bf16)
    end = height - DILATION

    one = swap_pairs(lax.dynamic_slice_in_dim(image, (1 - odd) * end, DILATION, 1), "row", 0)
    two = swap_pairs(lax.dynamic_slice_in_dim(image, odd * end, DILATION, 1), "row", 1)
    image_rows, rims = call(own_kernel, (rows, own_rims), (image,))
    forward_weight = jnp.transpose(weight, (2, 0, 1, 3)).reshape(channels, depth)
    backward_weight = jnp.transpose(weight[::-1, ::-1], (3, 0, 1, 2)).reshape(channels, depth)
    one, two, image_outer = call(
        functools.partial(rim_kernel, True), (packed, packed, outer), (one, two, rims)
    )
    two, one = swap_pairs(two, "col", 1), swap_pairs(one, "col", 0)
    activation, grads, one, two, rims, terms = call(
        functools.partial(forward_kernel, scale),
        (
            shape(image.shape, bf16), rows, edge, edge, own_rims,
            shape((channels, -(-(depth + 1) // 128) * 128), f32),
        ),
        (image_rows, image_outer, one, two, cotangent, forward_weight, bias[:, None]),
        (stack, pltpu.VMEM((channels, width), f32)),
        2 * flops,
    )
    one, two = swap_pairs(one, "row", 0), swap_pairs(two, "row", 1)
    one, two, grad_outer = call(
        functools.partial(rim_kernel, False), (packed, packed, outer), (one, two, rims)
    )
    two, one = swap_pairs(two, "col", 1), swap_pairs(one, "col", 0)
    (grad_image,) = call(
        backward_kernel,
        (shape(image.shape, bf16),),
        (grads, grad_outer, one, two, backward_weight),
        (stack,),
        flops,
    )
    one, other = add_pairs(terms, "col", "row")
    grad_weight, grad_bias = call(
        finish_kernel, (shape(weight.shape, f32), shape((1, channels), f32)), (one, other)
    )
    return (activation, grad_image, grad_weight, grad_bias.reshape(channels))


def solution(mesh):
    return jax.shard_map(
        shards,
        mesh=mesh,
        in_specs=(P(None, "row", "col"), P(), P(), P(None, "row", "col")),
        out_specs=(P(None, "row", "col"), P(None, "row", "col"), P(), P()),
        check_vma=False,
    )
```

```python
import functools
import math

import jax
import jax.numpy as jnp
from jax import lax
from jax.experimental import pallas as pl
from jax.experimental.pallas import tpu as pltpu
from jax.sharding import PartitionSpec as P

DILATION = 16
VMEM_BYTES = 16 * 2**20


def partners(axis, first):
    places = range(first, lax.axis_size(axis) - 1, 2)
    return [(at, at + 1) for at in places] + [(at + 1, at) for at in places]


def swap_pairs(value, axis, first):
    return lax.ppermute(value, axis, partners(axis, first))


def swap_corners(value, first_row, first_column):
    columns = lax.axis_size("col")
    pairs = [
        (row * columns + column, other_row * columns + other_column)
        for row, other_row in partners("row", first_row)
        for column, other_column in partners("col", first_column)
    ]
    return lax.ppermute(value, ("row", "col"), pairs)


def add_pairs(value, near_axis, far_axis):
    near, far = lax.axis_size(near_axis), lax.axis_size(far_axis)
    steps = [(near_axis, 2**k) for k in range(near.bit_length() - 1)]
    steps += [(far_axis, 2**k) for k in reversed(range(far.bit_length() - 1))]
    other = jnp.zeros_like(value)
    for place, (axis, step) in enumerate(steps):
        value = value + other if place else value
        other = lax.ppermute(value, axis, [(at, at ^ step) for at in range(lax.axis_size(axis))])
    return value, other


def gelu_pair(preact):
    coef = 0.7978845608
    square = preact * preact
    tval = jnp.tanh(coef * (preact + 0.044715 * (square * preact)))
    half = 0.5 * (1.0 + tval)
    slope_val = half + 0.5 * preact * (1.0 - tval * tval) * coef * (1.0 + 3.0 * 0.044715 * square)
    return (preact * half, slope_val)


def lane_of(shape):
    return lax.broadcasted_iota(jnp.int32, shape, len(shape) - 1)


def pack_group(rows):
    half = len(rows) // 2
    width = rows[0].shape[-1]
    lane = lane_of(rows[0].shape)
    pair = lane // (2 * DILATION)
    front = lane % (2 * DILATION) < DILATION

    def joined(part):
        total = pltpu.roll(part[0], DILATION, 1)
        for k in range(1, half):
            total = jnp.where(pair == k, pltpu.roll(part[k], DILATION + 2 * DILATION * k, 1), total)
        return total

    low, high = joined(rows[:half]), joined(rows[half:])
    first = jnp.where(front, pltpu.roll(low, width - DILATION, 1), high)
    last = jnp.where(front, low, pltpu.roll(high, DILATION, 1))
    return first, last


def unpack_group(from_left, from_right, count):
    half = count // 2
    width = from_left.shape[-1]
    front = lane_of(from_left.shape) % (2 * DILATION) < DILATION
    low = jnp.where(front, from_right, pltpu.roll(from_left, DILATION, 1))
    high = jnp.where(front, pltpu.roll(from_right, width - DILATION, 1), from_left)
    return [
        pltpu.roll(low if k < half else high, (width - DILATION - 2 * DILATION * (k % half)) % width, 1)
        for k in range(count)
    ]


def pack_rows(block, store, first_group):
    pieces = block.shape[-1] // DILATION
    for group in range(block.shape[0] // pieces):
        first, last = pack_group([block[group * pieces + k] for k in range(pieces)])
        store(first_group + group, first, last)


def either(axis, body, one, two):
    odd = lax.axis_index(axis) % 2 == 1
    pl.when(odd)(lambda: body(one, two))
    pl.when(jnp.logical_not(odd))(lambda: body(two, one))


def send_rims(rims_ref, one_ref, two_ref, corner_one_ref, corner_two_ref):
    odd_row, odd_column = lax.axis_index("row") % 2, lax.axis_index("col") % 2
    groups = corner_one_ref.shape[0]
    start = (1 - odd_row) * (one_ref.shape[0] - groups)
    one_ref[...] = rims_ref[1 - odd_column]
    two_ref[...] = rims_ref[odd_column]
    corner_one_ref[...] = rims_ref[1 - odd_column, pl.ds(start, groups)]
    corner_two_ref[...] = rims_ref[odd_column, pl.ds(start, groups)]


def own_kernel(image_ref, rows_ref, one_ref, two_ref, corner_one_ref, corner_two_ref, rims_ref):
    count = image_ref.shape[1] // DILATION
    groups = rims_ref.shape[1] // count

    def store(place, first, last):
        rims_ref[0, place] = first
        rims_ref[1, place] = last

    def body(block, carry):
        start = pl.multiple_of(block * DILATION, DILATION)
        rows = jnp.swapaxes(image_ref[:, pl.ds(start, DILATION), :], 0, 1)
        rows_ref[pl.ds(start, DILATION)] = rows
        pack_rows(rows, store, block * groups)
        return carry

    lax.fori_loop(0, count, body, 0)
    send_rims(rims_ref, one_ref, two_ref, corner_one_ref, corner_two_ref)


def join_kernel(swap, rows_ref, edge_ref, one_ref, two_ref, corner_one_ref, corner_two_ref, out_ref, near_ref):
    odd = lax.axis_index("row") % 2
    groups = (out_ref.shape[0] - DILATION) // 2
    start = odd * (one_ref.shape[0] - groups)
    out_ref[:DILATION] = rows_ref[pl.ds(odd * (rows_ref.shape[0] - DILATION), DILATION)]
    out_ref[DILATION : DILATION + groups] = one_ref[pl.ds(start, groups)]
    out_ref[DILATION + groups :] = two_ref[pl.ds(start, groups)]
    near_ref[:DILATION] = jnp.swapaxes(edge_ref[...], 0, 1) if swap else edge_ref[...]
    near_ref[DILATION : DILATION + groups] = corner_one_ref[...]
    near_ref[DILATION + groups :] = corner_two_ref[...]


def spread(rows_of, left_of, right_of, stack_ref, block, channels, width):
    pieces = width // DILATION
    lane = lane_of((channels, width))
    for group in range(DILATION // pieces):
        rims = unpack_group(left_of(group), right_of(group), pieces)
        for k in range(pieces):
            row = group * pieces + k
            value = rows_of(row)
            columns = slice(row * width, (row + 1) * width)
            before = jnp.where(lane < DILATION, rims[k], pltpu.roll(value, DILATION, 1))
            after = jnp.where(lane >= width - DILATION, rims[k], pltpu.roll(value, width - DILATION, 1))
            stack_ref[block, 0:channels, columns] = before
            stack_ref[block, channels : 2 * channels, columns] = value
            stack_ref[block, 2 * channels : 3 * channels, columns] = after


def spread_all(own_ref, near_ref, far_ref, one_ref, two_ref, stack_ref):
    height, channels, width = own_ref.shape
    count = height // DILATION
    groups = (near_ref.shape[0] - DILATION) // 2
    near = jnp.where(lax.axis_index("row") % 2 == 1, 0, count + 1)
    place = functools.partial(spread, stack_ref=stack_ref, channels=channels, width=width)

    def every(left, right):
        (left_ref, left_start), (right_ref, right_start) = left, right

        def body(block, carry):
            place(
                lambda row: own_ref[block * DILATION + row],
                lambda group: left_ref[block * groups + group],
                lambda group: right_ref[block * groups + group],
                block=block + 1,
            )
            return carry

        lax.fori_loop(0, count, body, 0)
        for edge_ref, block in ((near_ref, near), (far_ref, count + 1 - near)):
            place(
                lambda row, edge_ref=edge_ref: edge_ref[row],
                lambda group, edge_ref=edge_ref: edge_ref[left_start + group],
                lambda group, edge_ref=edge_ref: edge_ref[right_start + group],
                block=block,
            )

    either("col", every, (one_ref, DILATION), (two_ref, DILATION + groups))


def forward_kernel(
    scale, own_ref, near_ref, far_ref, one_ref, two_ref, cotangent_ref, weight_ref, bias_ref,
    activation_ref, grad_ref, rim_ref, send_one_ref, send_two_ref, send_corner_one_ref, send_corner_two_ref,
    terms_ref, stack_ref, sum_ref, rims_ref,
):
    height, channels, width = own_ref.shape
    count = height // DILATION
    groups = rims_ref.shape[1] // count
    spread_all(own_ref, near_ref, far_ref, one_ref, two_ref, stack_ref)
    terms_ref[...] = jnp.zeros_like(terms_ref)
    sum_ref[...] = jnp.zeros_like(sum_ref)
    depth = 9 * channels

    def store(place, first, last):
        rims_ref[0, place] = first
        rims_ref[1, place] = last

    def body(block, carry):
        start = pl.multiple_of(block * DILATION, DILATION)
        stacked = stack_ref[pl.ds(block, 3)].reshape(depth, DILATION * width)
        preact = jnp.dot(weight_ref[...], stacked, preferred_element_type=jnp.float32)
        cotangent = jnp.swapaxes(cotangent_ref[:, pl.ds(start, DILATION), :], 0, 1)
        bias = jnp.broadcast_to(bias_ref[...], (channels, width))
        values, grads = [], []
        total = sum_ref[...]
        for row in range(DILATION):
            value, slope_val = gelu_pair(preact[:, row * width : (row + 1) * width] + bias)
            values.append(value.astype(jnp.bfloat16))
            grad = (cotangent[row].astype(jnp.float32) * slope_val).astype(jnp.bfloat16)
            grads.append(grad)
            total = total + grad.astype(jnp.float32)
            grad_ref[start + row] = grad
        sum_ref[...] = total
        activation_ref[:, pl.ds(start, DILATION), :] = jnp.swapaxes(jnp.stack(values), 0, 1)
        terms_ref[:, :depth] += lax.dot_general(
            jnp.concatenate(grads, axis=1), stacked, (((1,), (1,)), ((), ())),
            preferred_element_type=jnp.float32,
        )
        pack_rows(jnp.stack(grads), store, block * groups)
        return carry

    lax.fori_loop(0, count, body, 0)
    odd = lax.axis_index("row") % 2
    rim_ref[...] = grad_ref[pl.ds((1 - odd) * (height - DILATION), DILATION)]
    send_rims(rims_ref, send_one_ref, send_two_ref, send_corner_one_ref, send_corner_two_ref)
    terms_ref[:, :depth] = terms_ref[:, :depth] * scale
    sums = jnp.sum(sum_ref[...], axis=1, keepdims=True) * scale
    terms_ref[:, depth:] = jnp.broadcast_to(sums, (channels, terms_ref.shape[1] - depth))


def backward_kernel(
    own_ref, near_ref, far_ref, one_ref, two_ref, weight_ref, out_ref, stack_ref
):
    height, channels, width = own_ref.shape
    spread_all(own_ref, near_ref, far_ref, one_ref, two_ref, stack_ref)

    def body(block, carry):
        start = pl.multiple_of(block * DILATION, DILATION)
        stacked = stack_ref[pl.ds(block, 3)].reshape(9 * channels, DILATION * width)
        total = jnp.dot(weight_ref[...], stacked, preferred_element_type=jnp.float32).astype(jnp.bfloat16)
        rows = jnp.stack([total[:, row * width : (row + 1) * width] for row in range(DILATION)])
        out_ref[:, pl.ds(start, DILATION), :] = jnp.swapaxes(rows, 0, 1)
        return carry

    lax.fori_loop(0, height // DILATION, body, 0)


def finish_kernel(one_ref, other_ref, weight_ref, bias_ref):
    total = one_ref[...] + other_ref[...]
    channels = total.shape[0]
    for tap in range(9):
        weight_ref[tap // 3, tap % 3] = total[:, tap * channels : (tap + 1) * channels]
    flipped = jnp.transpose(total[:, total.shape[1] - 128 :])
    bias_ref[...] = flipped[127:128, :channels]


def call(kernel, out_shapes, operands, scratch=(), flops=0):
    whole = pl.BlockSpec(memory_space=pltpu.VMEM)
    size = sum(math.prod(x.shape) * jnp.dtype(x.dtype).itemsize for x in (*operands, *out_shapes))
    return pl.pallas_call(
        kernel,
        out_shape=out_shapes,
        in_specs=[whole] * len(operands),
        out_specs=[whole] * len(out_shapes),
        scratch_shapes=list(scratch),
        compiler_params=pltpu.CompilerParams(vmem_limit_bytes=VMEM_BYTES),
        cost_estimate=pl.CostEstimate(flops=flops, bytes_accessed=size, transcendentals=0),
    )(*operands)


def shards(image, weight, bias, cotangent):
    channels, height, width = image.shape
    bf16, f32 = jnp.bfloat16, jnp.float32
    scale = 1.0 / math.sqrt(height * lax.axis_size("row") * width * lax.axis_size("col"))
    shape = jax.ShapeDtypeStruct
    pieces = width // DILATION
    own_groups, groups = height // pieces, DILATION // pieces
    depth = 9 * channels
    stack = pltpu.VMEM((height // DILATION + 2, 3 * channels, DILATION * width), bf16)
    rims = pltpu.VMEM((2, own_groups, channels, width), bf16)
    edge = shape((DILATION, channels, width), bf16)
    packed = shape((own_groups, channels, width), bf16)
    corner = shape((groups, channels, width), bf16)
    joint = shape((DILATION + 2 * groups, channels, width), bf16)
    rows = shape((height, channels, width), bf16)
    sums = shape((channels, -(-(depth + 1) // 128) * 128), f32)
    flops = 2 * depth * channels * height * width

    def exchange(swap, rows, rim, one, two, corner_one, corner_two):
        rim = swap_pairs(rim, "row", 0)
        one, two = swap_pairs(one, "col", 0), swap_pairs(two, "col", 1)
        corner_one, corner_two = swap_corners(corner_one, 0, 0), swap_corners(corner_two, 0, 1)
        far, near = call(
            functools.partial(join_kernel, swap), (joint, joint), (rows, rim, one, two, corner_one, corner_two)
        )
        return rows, near, swap_pairs(far, "row", 1), one, two

    even = 1 - lax.axis_index("row") % 2
    rim = lax.dynamic_slice_in_dim(image, even * (height - DILATION), DILATION, 1)
    image_rows, *sent = call(own_kernel, (rows, packed, packed, corner, corner), (image,), (rims,))
    forward_weight = jnp.transpose(weight, (2, 0, 1, 3)).reshape(channels, depth)
    backward_weight = jnp.transpose(weight[::-1, ::-1], (3, 0, 1, 2)).reshape(channels, depth)
    activation, grads, rim, *sent, terms = call(
        functools.partial(forward_kernel, scale),
        (shape(image.shape, bf16), rows, edge, packed, packed, corner, corner, sums),
        (*exchange(True, image_rows, rim, *sent), cotangent, forward_weight, bias[:, None]),
        (stack, pltpu.VMEM((channels, width), f32), rims),
        2 * flops,
    )
    (grad_image,) = call(
        backward_kernel,
        (shape(image.shape, bf16),),
        (*exchange(False, grads, rim, *sent), backward_weight),
        (stack,),
        flops,
    )
    one, other = add_pairs(terms, "col", "row")
    grad_weight, grad_bias = call(
        finish_kernel, (shape(weight.shape, f32), shape((1, channels), f32)), (one, other)
    )
    return (activation, grad_image, grad_weight, grad_bias.reshape(channels))


def solution(mesh):
    return jax.shard_map(
        shards,
        mesh=mesh,
        in_specs=(P(None, "row", "col"), P(), P(), P(None, "row", "col")),
        out_specs=(P(None, "row", "col"), P(None, "row", "col"), P(), P()),
        check_vma=False,
    )
```

```python
import functools
import math

import jax
import jax.numpy as jnp
from jax import lax
from jax.experimental import pallas as pl
from jax.experimental.pallas import tpu as pltpu
from jax.sharding import PartitionSpec as P

DILATION = 16
VMEM_BYTES = 16 * 2**20


def partners(axis, first):
    count = lax.axis_size(axis)
    to = list(range(count))
    for at in range(first, count - 1, 2):
        to[at], to[at + 1] = at + 1, at
    return list(enumerate(to))


def alone(axis, first):
    places = [at for at, other in partners(axis, first) if at == other]
    at = lax.axis_index(axis)
    return functools.reduce(jnp.logical_or, [at == place for place in places]) if places else None


def clear_if(flag, ref):
    if flag is not None:
        @pl.when(flag)
        def _():
            ref[...] = jnp.zeros_like(ref)


def swap_pairs(value, axis, first):
    return lax.ppermute(value, axis, partners(axis, first))


def add_pairs(value, near_axis, far_axis):
    near, far = lax.axis_size(near_axis), lax.axis_size(far_axis)
    steps = [(near_axis, 2**k) for k in range(near.bit_length() - 1)]
    steps += [(far_axis, 2**k) for k in reversed(range(far.bit_length() - 1))]
    other = jnp.zeros_like(value)
    for place, (axis, step) in enumerate(steps):
        value = value + other if place else value
        other = lax.ppermute(value, axis, [(at, at ^ step) for at in range(lax.axis_size(axis))])
    return value, other


def gelu_pair(preact):
    coef = 0.7978845608
    square = preact * preact
    tval = jnp.tanh(coef * (preact + 0.044715 * (square * preact)))
    half = 0.5 * (1.0 + tval)
    slope_val = half + 0.5 * preact * (1.0 - tval * tval) * coef * (1.0 + 3.0 * 0.044715 * square)
    return (preact * half, slope_val)


def lane_of(shape):
    return lax.broadcasted_iota(jnp.int32, shape, len(shape) - 1)


def pack_group(rows):
    half = len(rows) // 2
    width = rows[0].shape[-1]
    lane = lane_of(rows[0].shape)
    pair = lane // (2 * DILATION)
    front = lane % (2 * DILATION) < DILATION

    def joined(part):
        total = pltpu.roll(part[0], DILATION, 1)
        for k in range(1, half):
            total = jnp.where(pair == k, pltpu.roll(part[k], DILATION + 2 * DILATION * k, 1), total)
        return total

    low, high = joined(rows[:half]), joined(rows[half:])
    first = jnp.where(front, pltpu.roll(low, width - DILATION, 1), high)
    last = jnp.where(front, low, pltpu.roll(high, DILATION, 1))
    return first, last


def unpack_group(from_left, from_right, count):
    half = count // 2
    width = from_left.shape[-1]
    front = lane_of(from_left.shape) % (2 * DILATION) < DILATION
    low = jnp.where(front, from_right, pltpu.roll(from_left, DILATION, 1))
    high = jnp.where(front, pltpu.roll(from_right, width - DILATION, 1), from_left)
    return [
        pltpu.roll(low if k < half else high, (width - DILATION - 2 * DILATION * (k % half)) % width, 1)
        for k in range(count)
    ]


def pack_rows(block, store, first_group):
    pieces = block.shape[-1] // DILATION
    for group in range(block.shape[0] // pieces):
        first, last = pack_group([block[group * pieces + k] for k in range(pieces)])
        store(first_group + group, first, last)


def own_kernel(image_ref, rows_ref, rims_ref):
    count = image_ref.shape[1] // DILATION
    groups = rims_ref.shape[1] // count

    def store(place, first, last):
        rims_ref[0, place] = first
        rims_ref[1, place] = last

    def body(block, carry):
        start = pl.multiple_of(block * DILATION, DILATION)
        rows = jnp.swapaxes(image_ref[:, pl.ds(start, DILATION), :], 0, 1)
        rows_ref[pl.ds(start, DILATION)] = rows
        pack_rows(rows, store, block * groups)
        return carry

    lax.fori_loop(0, count, body, 0)


def either(axis, body, one, two):
    odd = lax.axis_index(axis) % 2 == 1
    pl.when(odd)(lambda: body(one, two))
    pl.when(jnp.logical_not(odd))(lambda: body(two, one))


def rim_kernel(swap, one_ref, two_ref, rims_ref, send_one_ref, send_two_ref, outer_ref):
    own = rims_ref.shape[1]
    groups = (send_one_ref.shape[0] - own) // 2

    def order(upper_ref, lower_ref):
        for index, ref in enumerate((upper_ref, lower_ref)):
            outer_ref[index] = jnp.swapaxes(ref[...], 0, 1) if swap else ref[...]

    def pack(send_first_ref, send_last_ref):
        def store(place, first, last):
            send_first_ref[place] = first
            send_last_ref[place] = last

        send_first_ref[groups : groups + own] = rims_ref[0]
        send_last_ref[groups : groups + own] = rims_ref[1]
        for index in range(2):
            pack_rows(outer_ref[index], store, index * (groups + own))

    either("row", order, one_ref, two_ref)
    either("col", pack, send_one_ref, send_two_ref)
    clear_if(alone("col", 0), send_one_ref)
    clear_if(alone("col", 1), send_two_ref)


def spread(rows_of, left_ref, right_ref, stack_ref, block, group_start):
    channels, width = left_ref.shape[1:]
    pieces = width // DILATION
    lane = lane_of((channels, width))
    for group in range(DILATION // pieces):
        rims = unpack_group(left_ref[group_start + group], right_ref[group_start + group], pieces)
        for k in range(pieces):
            row = group * pieces + k
            value = rows_of(row)
            columns = slice(row * width, (row + 1) * width)
            before = jnp.where(lane < DILATION, rims[k], pltpu.roll(value, DILATION, 1))
            after = jnp.where(lane >= width - DILATION, rims[k], pltpu.roll(value, width - DILATION, 1))
            stack_ref[block, 0:channels, columns] = before
            stack_ref[block, channels : 2 * channels, columns] = value
            stack_ref[block, 2 * channels : 3 * channels, columns] = after


def spread_all(own_ref, outer_ref, one_ref, two_ref, stack_ref):
    count = own_ref.shape[0] // DILATION
    groups = one_ref.shape[0] // (count + 2)

    def every(left_ref, right_ref):
        spread(lambda row: outer_ref[0, row], left_ref, right_ref, stack_ref, 0, 0)

        def body(block, carry):
            spread(
                lambda row: own_ref[block * DILATION + row],
                left_ref, right_ref, stack_ref, block + 1, (block + 1) * groups,
            )
            return carry

        lax.fori_loop(0, count, body, 0)
        spread(lambda row: outer_ref[1, row], left_ref, right_ref, stack_ref, count + 1, (count + 1) * groups)

    either("col", every, one_ref, two_ref)


def forward_kernel(
    scale, own_ref, outer_ref, one_ref, two_ref, cotangent_ref, weight_ref, bias_ref,
    activation_ref, grad_ref, send_one_ref, send_two_ref, rims_ref, terms_ref, stack_ref, sum_ref,
):
    height, channels, width = own_ref.shape
    count = height // DILATION
    groups = rims_ref.shape[1] // count
    spread_all(own_ref, outer_ref, one_ref, two_ref, stack_ref)
    terms_ref[...] = jnp.zeros_like(terms_ref)
    sum_ref[...] = jnp.zeros_like(sum_ref)
    depth = 9 * channels

    def store(place, first, last):
        rims_ref[0, place] = first
        rims_ref[1, place] = last

    def body(block, carry):
        start = pl.multiple_of(block * DILATION, DILATION)
        stacked = stack_ref[pl.ds(block, 3)].reshape(depth, DILATION * width)
        preact = jnp.dot(weight_ref[...], stacked, preferred_element_type=jnp.float32)
        cotangent = jnp.swapaxes(cotangent_ref[:, pl.ds(start, DILATION), :], 0, 1)
        bias = jnp.broadcast_to(bias_ref[...], (channels, width))
        values, grads = [], []
        total = sum_ref[...]
        for row in range(DILATION):
            value, slope_val = gelu_pair(preact[:, row * width : (row + 1) * width] + bias)
            values.append(value.astype(jnp.bfloat16))
            grad = (cotangent[row].astype(jnp.float32) * slope_val).astype(jnp.bfloat16)
            grads.append(grad)
            total = total + grad.astype(jnp.float32)
            grad_ref[start + row] = grad
        sum_ref[...] = total
        activation_ref[:, pl.ds(start, DILATION), :] = jnp.swapaxes(jnp.stack(values), 0, 1)
        terms_ref[:, :depth] += lax.dot_general(
            jnp.concatenate(grads, axis=1), stacked, (((1,), (1,)), ((), ())),
            preferred_element_type=jnp.float32,
        )
        pack_rows(jnp.stack(grads), store, block * groups)
        return carry

    lax.fori_loop(0, count, body, 0)
    end = height - DILATION
    odd = lax.axis_index("row") % 2
    send_one_ref[...] = grad_ref[pl.ds((1 - odd) * end, DILATION)]
    send_two_ref[...] = grad_ref[pl.ds(odd * end, DILATION)]
    clear_if(alone("row", 0), send_one_ref)
    clear_if(alone("row", 1), send_two_ref)
    terms_ref[:, :depth] = terms_ref[:, :depth] * scale
    sums = jnp.sum(sum_ref[...], axis=1, keepdims=True) * scale
    terms_ref[:, depth:] = jnp.broadcast_to(sums, (channels, terms_ref.shape[1] - depth))


def backward_kernel(
    own_ref, outer_ref, one_ref, two_ref, weight_ref, out_ref, stack_ref
):
    height, channels, width = own_ref.shape
    spread_all(own_ref, outer_ref, one_ref, two_ref, stack_ref)

    def body(block, carry):
        start = pl.multiple_of(block * DILATION, DILATION)
        stacked = stack_ref[pl.ds(block, 3)].reshape(9 * channels, DILATION * width)
        total = jnp.dot(weight_ref[...], stacked, preferred_element_type=jnp.float32).astype(jnp.bfloat16)
        rows = jnp.stack([total[:, row * width : (row + 1) * width] for row in range(DILATION)])
        out_ref[:, pl.ds(start, DILATION), :] = jnp.swapaxes(rows, 0, 1)
        return carry

    lax.fori_loop(0, height // DILATION, body, 0)


def finish_kernel(one_ref, other_ref, weight_ref, bias_ref):
    total = one_ref[...] + other_ref[...]
    channels = total.shape[0]
    for tap in range(9):
        weight_ref[tap // 3, tap % 3] = total[:, tap * channels : (tap + 1) * channels]
    flipped = jnp.transpose(total[:, total.shape[1] - 128 :])
    bias_ref[...] = flipped[127:128, :channels]


def call(kernel, out_shapes, operands, scratch=(), flops=0):
    whole = pl.BlockSpec(memory_space=pltpu.VMEM)
    size = sum(math.prod(x.shape) * jnp.dtype(x.dtype).itemsize for x in (*operands, *out_shapes))
    return pl.pallas_call(
        kernel,
        out_shape=out_shapes,
        in_specs=[whole] * len(operands),
        out_specs=[whole] * len(out_shapes),
        scratch_shapes=list(scratch),
        compiler_params=pltpu.CompilerParams(vmem_limit_bytes=VMEM_BYTES),
        cost_estimate=pl.CostEstimate(flops=flops, bytes_accessed=size, transcendentals=0),
    )(*operands)


def shards(image, weight, bias, cotangent):
    channels, height, width = image.shape
    bf16, f32 = jnp.bfloat16, jnp.float32
    scale = 1.0 / math.sqrt(height * lax.axis_size("row") * width * lax.axis_size("col"))
    shape = jax.ShapeDtypeStruct
    pieces = width // DILATION
    own_groups, all_groups = height // pieces, (height + 2 * DILATION) // pieces
    depth = 9 * channels
    stack = pltpu.VMEM((height // DILATION + 2, 3 * channels, DILATION * width), bf16)
    edge = shape((DILATION, channels, width), bf16)
    packed = shape((all_groups, channels, width), bf16)
    own_rims = shape((2, own_groups, channels, width), bf16)
    rows = shape((height, channels, width), bf16)
    flops = 2 * depth * channels * height * width

    odd = lax.axis_index("row") % 2
    outer = shape((2, DILATION, channels, width), bf16)
    end = height - DILATION


    def image_rim(start, first):
        rim = lax.dynamic_slice_in_dim(image, start, DILATION, 1)
        flag = alone("row", first)
        return rim if flag is None else jnp.where(flag, jnp.zeros_like(rim), rim)

    one = swap_pairs(image_rim((1 - odd) * end, 0), "row", 0)
    two = swap_pairs(image_rim(odd * end, 1), "row", 1)
    image_rows, rims = call(own_kernel, (rows, own_rims), (image,))
    forward_weight = jnp.transpose(weight, (2, 0, 1, 3)).reshape(channels, depth)
    backward_weight = jnp.transpose(weight[::-1, ::-1], (3, 0, 1, 2)).reshape(channels, depth)
    one, two, image_outer = call(
        functools.partial(rim_kernel, True), (packed, packed, outer), (one, two, rims)
    )
    two, one = swap_pairs(two, "col", 1), swap_pairs(one, "col", 0)
    activation, grads, one, two, rims, terms = call(
        functools.partial(forward_kernel, scale),
        (
            shape(image.shape, bf16), rows, edge, edge, own_rims,
            shape((channels, -(-(depth + 1) // 128) * 128), f32),
        ),
        (image_rows, image_outer, one, two, cotangent, forward_weight, bias[:, None]),
        (stack, pltpu.VMEM((channels, width), f32)),
        2 * flops,
    )
    one, two = swap_pairs(one, "row", 0), swap_pairs(two, "row", 1)
    one, two, grad_outer = call(
        functools.partial(rim_kernel, False), (packed, packed, outer), (one, two, rims)
    )
    two, one = swap_pairs(two, "col", 1), swap_pairs(one, "col", 0)
    (grad_image,) = call(
        backward_kernel,
        (shape(image.shape, bf16),),
        (grads, grad_outer, one, two, backward_weight),
        (stack,),
        flops,
    )
    one, other = add_pairs(terms, "col", "row")
    grad_weight, grad_bias = call(
        finish_kernel, (shape(weight.shape, f32), shape((1, channels), f32)), (one, other)
    )
    return (activation, grad_image, grad_weight, grad_bias.reshape(channels))


def solution(mesh):
    return jax.shard_map(
        shards,
        mesh=mesh,
        in_specs=(P(None, "row", "col"), P(), P(), P(None, "row", "col")),
        out_specs=(P(None, "row", "col"), P(None, "row", "col"), P(), P()),
        check_vma=False,
    )
```

```python
import functools
import math

import jax
import jax.numpy as jnp
from jax import lax
from jax.experimental import pallas as pl
from jax.experimental.pallas import tpu as pltpu
from jax.sharding import PartitionSpec as P

DILATION = 16
VMEM_BYTES = 16 * 2**20


def partners(axis, first):
    count = lax.axis_size(axis)
    to = list(range(count))
    for at in range(first, count - 1, 2):
        to[at], to[at + 1] = at + 1, at
    return list(enumerate(to))


def alone(axis, first):
    places = [at for at, other in partners(axis, first) if at == other]
    at = lax.axis_index(axis)
    return functools.reduce(jnp.logical_or, [at == place for place in places]) if places else None


def clear_if(flag, ref):
    if flag is not None:
        @pl.when(flag)
        def _():
            ref[...] = jnp.zeros_like(ref)


def swap_pairs(value, axis, first):
    other_axis = "col" if axis == "row" else "row"
    columns = lax.axis_size("col")

    def place(at, other):
        row, column = (at, other) if axis == "row" else (other, at)
        return row * columns + column

    pairs = []
    for at, to in partners(axis, first):
        for other, other_to in partners(other_axis, 0):
            pairs.append((place(at, other), place(to, other if to != at else other_to)))
    return lax.ppermute(value, ("row", "col"), pairs)


def add_pairs(value, near_axis, far_axis):
    near, far = lax.axis_size(near_axis), lax.axis_size(far_axis)
    steps = [(near_axis, 2**k) for k in range(near.bit_length() - 1)]
    steps += [(far_axis, 2**k) for k in reversed(range(far.bit_length() - 1))]
    other = jnp.zeros_like(value)
    for place, (axis, step) in enumerate(steps):
        value = value + other if place else value
        other = lax.ppermute(value, axis, [(at, at ^ step) for at in range(lax.axis_size(axis))])
    return value, other


def gelu_pair(preact):
    coef = 0.7978845608
    square = preact * preact
    tval = jnp.tanh(coef * (preact + 0.044715 * (square * preact)))
    half = 0.5 * (1.0 + tval)
    slope_val = half + 0.5 * preact * (1.0 - tval * tval) * coef * (1.0 + 3.0 * 0.044715 * square)
    return (preact * half, slope_val)


def lane_of(shape):
    return lax.broadcasted_iota(jnp.int32, shape, len(shape) - 1)


def pack_group(rows):
    half = len(rows) // 2
    width = rows[0].shape[-1]
    lane = lane_of(rows[0].shape)
    pair = lane // (2 * DILATION)
    front = lane % (2 * DILATION) < DILATION

    def joined(part):
        total = pltpu.roll(part[0], DILATION, 1)
        for k in range(1, half):
            total = jnp.where(pair == k, pltpu.roll(part[k], DILATION + 2 * DILATION * k, 1), total)
        return total

    low, high = joined(rows[:half]), joined(rows[half:])
    first = jnp.where(front, pltpu.roll(low, width - DILATION, 1), high)
    last = jnp.where(front, low, pltpu.roll(high, DILATION, 1))
    return first, last


def unpack_group(from_left, from_right, count):
    half = count // 2
    width = from_left.shape[-1]
    front = lane_of(from_left.shape) % (2 * DILATION) < DILATION
    low = jnp.where(front, from_right, pltpu.roll(from_left, DILATION, 1))
    high = jnp.where(front, pltpu.roll(from_right, width - DILATION, 1), from_left)
    return [
        pltpu.roll(low if k < half else high, (width - DILATION - 2 * DILATION * (k % half)) % width, 1)
        for k in range(count)
    ]


def pack_rows(block, store, first_group):
    pieces = block.shape[-1] // DILATION
    for group in range(block.shape[0] // pieces):
        first, last = pack_group([block[group * pieces + k] for k in range(pieces)])
        store(first_group + group, first, last)


def own_kernel(image_ref, rows_ref, rims_ref):
    count = image_ref.shape[1] // DILATION
    groups = rims_ref.shape[1] // count

    def store(place, first, last):
        rims_ref[0, place] = first
        rims_ref[1, place] = last

    def body(block, carry):
        start = pl.multiple_of(block * DILATION, DILATION)
        rows = jnp.swapaxes(image_ref[:, pl.ds(start, DILATION), :], 0, 1)
        rows_ref[pl.ds(start, DILATION)] = rows
        pack_rows(rows, store, block * groups)
        return carry

    lax.fori_loop(0, count, body, 0)


def either(axis, body, one, two):
    odd = lax.axis_index(axis) % 2 == 1
    pl.when(odd)(lambda: body(one, two))
    pl.when(jnp.logical_not(odd))(lambda: body(two, one))


def rim_kernel(swap, one_ref, two_ref, rims_ref, send_one_ref, send_two_ref, outer_ref):
    own = rims_ref.shape[1]
    groups = (send_one_ref.shape[0] - own) // 2

    def order(upper_ref, lower_ref):
        for index, ref in enumerate((upper_ref, lower_ref)):
            outer_ref[index] = jnp.swapaxes(ref[...], 0, 1) if swap else ref[...]

    def pack(send_first_ref, send_last_ref):
        def store(place, first, last):
            send_first_ref[place] = first
            send_last_ref[place] = last

        send_first_ref[groups : groups + own] = rims_ref[0]
        send_last_ref[groups : groups + own] = rims_ref[1]
        for index in range(2):
            pack_rows(outer_ref[index], store, index * (groups + own))

    either("row", order, one_ref, two_ref)
    either("col", pack, send_one_ref, send_two_ref)
    clear_if(alone("col", 0), send_one_ref)
    clear_if(alone("col", 1), send_two_ref)


def spread(rows_of, left_ref, right_ref, stack_ref, block, group_start):
    channels, width = left_ref.shape[1:]
    pieces = width // DILATION
    lane = lane_of((channels, width))
    for group in range(DILATION // pieces):
        rims = unpack_group(left_ref[group_start + group], right_ref[group_start + group], pieces)
        for k in range(pieces):
            row = group * pieces + k
            value = rows_of(row)
            columns = slice(row * width, (row + 1) * width)
            before = jnp.where(lane < DILATION, rims[k], pltpu.roll(value, DILATION, 1))
            after = jnp.where(lane >= width - DILATION, rims[k], pltpu.roll(value, width - DILATION, 1))
            stack_ref[block, 0:channels, columns] = before
            stack_ref[block, channels : 2 * channels, columns] = value
            stack_ref[block, 2 * channels : 3 * channels, columns] = after


def spread_all(own_ref, outer_ref, one_ref, two_ref, stack_ref):
    count = own_ref.shape[0] // DILATION
    groups = one_ref.shape[0] // (count + 2)

    def every(left_ref, right_ref):
        spread(lambda row: outer_ref[0, row], left_ref, right_ref, stack_ref, 0, 0)

        def body(block, carry):
            spread(
                lambda row: own_ref[block * DILATION + row],
                left_ref, right_ref, stack_ref, block + 1, (block + 1) * groups,
            )
            return carry

        lax.fori_loop(0, count, body, 0)
        spread(lambda row: outer_ref[1, row], left_ref, right_ref, stack_ref, count + 1, (count + 1) * groups)

    either("col", every, one_ref, two_ref)


def forward_kernel(
    scale, own_ref, outer_ref, one_ref, two_ref, cotangent_ref, weight_ref, bias_ref,
    activation_ref, grad_ref, send_one_ref, send_two_ref, rims_ref, terms_ref, stack_ref, sum_ref,
):
    height, channels, width = own_ref.shape
    count = height // DILATION
    groups = rims_ref.shape[1] // count
    spread_all(own_ref, outer_ref, one_ref, two_ref, stack_ref)
    terms_ref[...] = jnp.zeros_like(terms_ref)
    sum_ref[...] = jnp.zeros_like(sum_ref)
    depth = 9 * channels

    def store(place, first, last):
        rims_ref[0, place] = first
        rims_ref[1, place] = last

    def body(block, carry):
        start = pl.multiple_of(block * DILATION, DILATION)
        stacked = stack_ref[pl.ds(block, 3)].reshape(depth, DILATION * width)
        preact = jnp.dot(weight_ref[...], stacked, preferred_element_type=jnp.float32)
        cotangent = jnp.swapaxes(cotangent_ref[:, pl.ds(start, DILATION), :], 0, 1)
        bias = jnp.broadcast_to(bias_ref[...], (channels, width))
        values, grads = [], []
        total = sum_ref[...]
        for row in range(DILATION):
            value, slope_val = gelu_pair(preact[:, row * width : (row + 1) * width] + bias)
            values.append(value.astype(jnp.bfloat16))
            grad = (cotangent[row].astype(jnp.float32) * slope_val).astype(jnp.bfloat16)
            grads.append(grad)
            total = total + grad.astype(jnp.float32)
            grad_ref[start + row] = grad
        sum_ref[...] = total
        activation_ref[:, pl.ds(start, DILATION), :] = jnp.swapaxes(jnp.stack(values), 0, 1)
        terms_ref[:, :depth] += lax.dot_general(
            jnp.concatenate(grads, axis=1), stacked, (((1,), (1,)), ((), ())),
            preferred_element_type=jnp.float32,
        )
        pack_rows(jnp.stack(grads), store, block * groups)
        return carry

    lax.fori_loop(0, count, body, 0)
    end = height - DILATION
    odd = lax.axis_index("row") % 2
    send_one_ref[...] = grad_ref[pl.ds((1 - odd) * end, DILATION)]
    send_two_ref[...] = grad_ref[pl.ds(odd * end, DILATION)]
    clear_if(alone("row", 0), send_one_ref)
    clear_if(alone("row", 1), send_two_ref)
    terms_ref[:, :depth] = terms_ref[:, :depth] * scale
    sums = jnp.sum(sum_ref[...], axis=1, keepdims=True) * scale
    terms_ref[:, depth:] = jnp.broadcast_to(sums, (channels, terms_ref.shape[1] - depth))


def backward_kernel(
    own_ref, outer_ref, one_ref, two_ref, weight_ref, out_ref, stack_ref
):
    height, channels, width = own_ref.shape
    spread_all(own_ref, outer_ref, one_ref, two_ref, stack_ref)

    def body(block, carry):
        start = pl.multiple_of(block * DILATION, DILATION)
        stacked = stack_ref[pl.ds(block, 3)].reshape(9 * channels, DILATION * width)
        total = jnp.dot(weight_ref[...], stacked, preferred_element_type=jnp.float32).astype(jnp.bfloat16)
        rows = jnp.stack([total[:, row * width : (row + 1) * width] for row in range(DILATION)])
        out_ref[:, pl.ds(start, DILATION), :] = jnp.swapaxes(rows, 0, 1)
        return carry

    lax.fori_loop(0, height // DILATION, body, 0)


def finish_kernel(one_ref, other_ref, weight_ref, bias_ref):
    total = one_ref[...] + other_ref[...]
    channels = total.shape[0]
    for tap in range(9):
        weight_ref[tap // 3, tap % 3] = total[:, tap * channels : (tap + 1) * channels]
    flipped = jnp.transpose(total[:, total.shape[1] - 128 :])
    bias_ref[...] = flipped[127:128, :channels]


def call(kernel, out_shapes, operands, scratch=(), flops=0):
    whole = pl.BlockSpec(memory_space=pltpu.VMEM)
    size = sum(math.prod(x.shape) * jnp.dtype(x.dtype).itemsize for x in (*operands, *out_shapes))
    return pl.pallas_call(
        kernel,
        out_shape=out_shapes,
        in_specs=[whole] * len(operands),
        out_specs=[whole] * len(out_shapes),
        scratch_shapes=list(scratch),
        compiler_params=pltpu.CompilerParams(vmem_limit_bytes=VMEM_BYTES),
        cost_estimate=pl.CostEstimate(flops=flops, bytes_accessed=size, transcendentals=0),
    )(*operands)


def shards(image, weight, bias, cotangent):
    channels, height, width = image.shape
    bf16, f32 = jnp.bfloat16, jnp.float32
    scale = 1.0 / math.sqrt(height * lax.axis_size("row") * width * lax.axis_size("col"))
    shape = jax.ShapeDtypeStruct
    pieces = width // DILATION
    own_groups, all_groups = height // pieces, (height + 2 * DILATION) // pieces
    depth = 9 * channels
    stack = pltpu.VMEM((height // DILATION + 2, 3 * channels, DILATION * width), bf16)
    edge = shape((DILATION, channels, width), bf16)
    packed = shape((all_groups, channels, width), bf16)
    own_rims = shape((2, own_groups, channels, width), bf16)
    rows = shape((height, channels, width), bf16)
    flops = 2 * depth * channels * height * width

    odd = lax.axis_index("row") % 2
    outer = shape((2, DILATION, channels, width), bf16)
    end = height - DILATION


    def image_rim(start, first):
        rim = lax.dynamic_slice_in_dim(image, start, DILATION, 1)
        flag = alone("row", first)
        return rim if flag is None else jnp.where(flag, jnp.zeros_like(rim), rim)

    one = swap_pairs(image_rim((1 - odd) * end, 0), "row", 0)
    two = swap_pairs(image_rim(odd * end, 1), "row", 1)
    image_rows, rims = call(own_kernel, (rows, own_rims), (image,))
    forward_weight = jnp.transpose(weight, (2, 0, 1, 3)).reshape(channels, depth)
    backward_weight = jnp.transpose(weight[::-1, ::-1], (3, 0, 1, 2)).reshape(channels, depth)
    one, two, image_outer = call(
        functools.partial(rim_kernel, True), (packed, packed, outer), (one, two, rims)
    )
    two, one = swap_pairs(two, "col", 1), swap_pairs(one, "col", 0)
    activation, grads, one, two, rims, terms = call(
        functools.partial(forward_kernel, scale),
        (
            shape(image.shape, bf16), rows, edge, edge, own_rims,
            shape((channels, -(-(depth + 1) // 128) * 128), f32),
        ),
        (image_rows, image_outer, one, two, cotangent, forward_weight, bias[:, None]),
        (stack, pltpu.VMEM((channels, width), f32)),
        2 * flops,
    )
    one, two = swap_pairs(one, "row", 0), swap_pairs(two, "row", 1)
    one, two, grad_outer = call(
        functools.partial(rim_kernel, False), (packed, packed, outer), (one, two, rims)
    )
    two, one = swap_pairs(two, "col", 1), swap_pairs(one, "col", 0)
    (grad_image,) = call(
        backward_kernel,
        (shape(image.shape, bf16),),
        (grads, grad_outer, one, two, backward_weight),
        (stack,),
        flops,
    )
    one, other = add_pairs(terms, "col", "row")
    grad_weight, grad_bias = call(
        finish_kernel, (shape(weight.shape, f32), shape((1, channels), f32)), (one, other)
    )
    return (activation, grad_image, grad_weight, grad_bias.reshape(channels))


def solution(mesh):
    return jax.shard_map(
        shards,
        mesh=mesh,
        in_specs=(P(None, "row", "col"), P(), P(), P(None, "row", "col")),
        out_specs=(P(None, "row", "col"), P(None, "row", "col"), P(), P()),
        check_vma=False,
    )
```

```python
import functools
import math

import jax
import jax.numpy as jnp
from jax import lax
from jax.experimental import pallas as pl
from jax.experimental.pallas import tpu as pltpu
from jax.sharding import PartitionSpec as P

DILATION = 16
VMEM_BYTES = 16 * 2**20


def partners(axis, first):
    count = lax.axis_size(axis)
    to = list(range(count))
    for at in range(first, count - 1, 2):
        to[at], to[at + 1] = at + 1, at
    return list(enumerate(to))


def alone(axis, first):
    places = [at for at, other in partners(axis, first) if at == other]
    at = lax.axis_index(axis)
    return functools.reduce(jnp.logical_or, [at == place for place in places]) if places else None


def clear_if(flag, ref):
    if flag is not None:
        @pl.when(flag)
        def _():
            ref[...] = jnp.zeros_like(ref)


def swap_pairs(value, axis, first):
    other_axis = "col" if axis == "row" else "row"
    columns = lax.axis_size("col")

    def place(at, other):
        row, column = (at, other) if axis == "row" else (other, at)
        return row * columns + column

    pairs = []
    for at, to in partners(axis, first):
        for other, other_to in partners(other_axis, 0):
            pairs.append((place(at, other), place(to, other if to != at else other_to)))
    return lax.ppermute(value, ("row", "col"), pairs)


def rounds_of(axis):
    bits = [2**k for k in reversed(range(lax.axis_size(axis).bit_length() - 1))]
    return [(axis, bits[at : at + 2]) for at in range(0, len(bits), 2)]


def add_pairs(value, near_axis, far_axis):
    other = jnp.zeros_like(value)
    for place, (axis, bits) in enumerate(rounds_of(near_axis) + rounds_of(far_axis)):
        value = value + other if place else value
        masks = bits[::-1] + [sum(bits)] if len(bits) == 2 else bits
        came = [
            lax.ppermute(value, axis, [(at, at ^ mask) for at in range(lax.axis_size(axis))]) for mask in masks
        ]
        if len(came) == 3:
            value, other = value + came[0], came[1] + came[2]
        else:
            other = came[0]
    return value, other


def gelu_pair(preact):
    coef = 0.7978845608
    square = preact * preact
    tval = jnp.tanh(coef * (preact + 0.044715 * (square * preact)))
    half = 0.5 * (1.0 + tval)
    slope_val = half + 0.5 * preact * (1.0 - tval * tval) * coef * (1.0 + 3.0 * 0.044715 * square)
    return (preact * half, slope_val)


def lane_of(shape):
    return lax.broadcasted_iota(jnp.int32, shape, len(shape) - 1)


def pack_group(rows):
    half = len(rows) // 2
    width = rows[0].shape[-1]
    lane = lane_of(rows[0].shape)
    pair = lane // (2 * DILATION)
    front = lane % (2 * DILATION) < DILATION

    def joined(part):
        total = pltpu.roll(part[0], DILATION, 1)
        for k in range(1, half):
            total = jnp.where(pair == k, pltpu.roll(part[k], DILATION + 2 * DILATION * k, 1), total)
        return total

    low, high = joined(rows[:half]), joined(rows[half:])
    first = jnp.where(front, pltpu.roll(low, width - DILATION, 1), high)
    last = jnp.where(front, low, pltpu.roll(high, DILATION, 1))
    return first, last


def unpack_group(from_left, from_right, count):
    half = count // 2
    width = from_left.shape[-1]
    front = lane_of(from_left.shape) % (2 * DILATION) < DILATION
    low = jnp.where(front, from_right, pltpu.roll(from_left, DILATION, 1))
    high = jnp.where(front, pltpu.roll(from_right, width - DILATION, 1), from_left)
    return [
        pltpu.roll(low if k < half else high, (width - DILATION - 2 * DILATION * (k % half)) % width, 1)
        for k in range(count)
    ]


def pack_rows(block, store, first_group):
    pieces = block.shape[-1] // DILATION
    for group in range(block.shape[0] // pieces):
        first, last = pack_group([block[group * pieces + k] for k in range(pieces)])
        store(first_group + group, first, last)


def own_kernel(image_ref, rows_ref, rims_ref):
    count = image_ref.shape[1] // DILATION
    groups = rims_ref.shape[1] // count

    def store(place, first, last):
        rims_ref[0, place] = first
        rims_ref[1, place] = last

    def body(block, carry):
        start = pl.multiple_of(block * DILATION, DILATION)
        rows = jnp.swapaxes(image_ref[:, pl.ds(start, DILATION), :], 0, 1)
        rows_ref[pl.ds(start, DILATION)] = rows
        pack_rows(rows, store, block * groups)
        return carry

    lax.fori_loop(0, count, body, 0)


def either(axis, body, one, two):
    odd = lax.axis_index(axis) % 2 == 1
    pl.when(odd)(lambda: body(one, two))
    pl.when(jnp.logical_not(odd))(lambda: body(two, one))


def rim_kernel(swap, one_ref, two_ref, rims_ref, send_one_ref, send_two_ref, outer_ref):
    own = rims_ref.shape[1]
    groups = (send_one_ref.shape[0] - own) // 2

    def order(upper_ref, lower_ref):
        for index, ref in enumerate((upper_ref, lower_ref)):
            outer_ref[index] = jnp.swapaxes(ref[...], 0, 1) if swap else ref[...]

    def pack(send_first_ref, send_last_ref):
        def store(place, first, last):
            send_first_ref[place] = first
            send_last_ref[place] = last

        send_first_ref[groups : groups + own] = rims_ref[0]
        send_last_ref[groups : groups + own] = rims_ref[1]
        for index in range(2):
            pack_rows(outer_ref[index], store, index * (groups + own))

    either("row", order, one_ref, two_ref)
    either("col", pack, send_one_ref, send_two_ref)
    clear_if(alone("col", 0), send_one_ref)
    clear_if(alone("col", 1), send_two_ref)


def spread(rows_of, left_ref, right_ref, stack_ref, block, group_start):
    channels, width = left_ref.shape[1:]
    pieces = width // DILATION
    lane = lane_of((channels, width))
    for group in range(DILATION // pieces):
        rims = unpack_group(left_ref[group_start + group], right_ref[group_start + group], pieces)
        for k in range(pieces):
            row = group * pieces + k
            value = rows_of(row)
            columns = slice(row * width, (row + 1) * width)
            before = jnp.where(lane < DILATION, rims[k], pltpu.roll(value, DILATION, 1))
            after = jnp.where(lane >= width - DILATION, rims[k], pltpu.roll(value, width - DILATION, 1))
            stack_ref[block, 0:channels, columns] = before
            stack_ref[block, channels : 2 * channels, columns] = value
            stack_ref[block, 2 * channels : 3 * channels, columns] = after


def spread_all(own_ref, outer_ref, one_ref, two_ref, stack_ref):
    count = own_ref.shape[0] // DILATION
    groups = one_ref.shape[0] // (count + 2)

    def every(left_ref, right_ref):
        spread(lambda row: outer_ref[0, row], left_ref, right_ref, stack_ref, 0, 0)

        def body(block, carry):
            spread(
                lambda row: own_ref[block * DILATION + row],
                left_ref, right_ref, stack_ref, block + 1, (block + 1) * groups,
            )
            return carry

        lax.fori_loop(0, count, body, 0)
        spread(lambda row: outer_ref[1, row], left_ref, right_ref, stack_ref, count + 1, (count + 1) * groups)

    either("col", every, one_ref, two_ref)


def forward_kernel(
    scale, own_ref, outer_ref, one_ref, two_ref, cotangent_ref, weight_ref, bias_ref,
    activation_ref, grad_ref, send_one_ref, send_two_ref, rims_ref, terms_ref, stack_ref, sum_ref,
):
    height, channels, width = own_ref.shape
    count = height // DILATION
    groups = rims_ref.shape[1] // count
    spread_all(own_ref, outer_ref, one_ref, two_ref, stack_ref)
    terms_ref[...] = jnp.zeros_like(terms_ref)
    sum_ref[...] = jnp.zeros_like(sum_ref)
    depth = 9 * channels

    def store(place, first, last):
        rims_ref[0, place] = first
        rims_ref[1, place] = last

    def body(block, carry):
        start = pl.multiple_of(block * DILATION, DILATION)
        stacked = stack_ref[pl.ds(block, 3)].reshape(depth, DILATION * width)
        preact = jnp.dot(weight_ref[...], stacked, preferred_element_type=jnp.float32)
        cotangent = jnp.swapaxes(cotangent_ref[:, pl.ds(start, DILATION), :], 0, 1)
        bias = jnp.broadcast_to(bias_ref[...], (channels, width))
        values, grads = [], []
        total = sum_ref[...]
        for row in range(DILATION):
            value, slope_val = gelu_pair(preact[:, row * width : (row + 1) * width] + bias)
            values.append(value.astype(jnp.bfloat16))
            grad = (cotangent[row].astype(jnp.float32) * slope_val).astype(jnp.bfloat16)
            grads.append(grad)
            total = total + grad.astype(jnp.float32)
            grad_ref[start + row] = grad
        sum_ref[...] = total
        activation_ref[:, pl.ds(start, DILATION), :] = jnp.swapaxes(jnp.stack(values), 0, 1)
        terms_ref[:, :depth] += lax.dot_general(
            jnp.concatenate(grads, axis=1), stacked, (((1,), (1,)), ((), ())),
            preferred_element_type=jnp.float32,
        )
        pack_rows(jnp.stack(grads), store, block * groups)
        return carry

    lax.fori_loop(0, count, body, 0)
    end = height - DILATION
    odd = lax.axis_index("row") % 2
    send_one_ref[...] = grad_ref[pl.ds((1 - odd) * end, DILATION)]
    send_two_ref[...] = grad_ref[pl.ds(odd * end, DILATION)]
    clear_if(alone("row", 0), send_one_ref)
    clear_if(alone("row", 1), send_two_ref)
    terms_ref[:, :depth] = terms_ref[:, :depth] * scale
    sums = jnp.sum(sum_ref[...], axis=1, keepdims=True) * scale
    terms_ref[:, depth:] = jnp.broadcast_to(sums, (channels, terms_ref.shape[1] - depth))


def backward_kernel(
    own_ref, outer_ref, one_ref, two_ref, weight_ref, out_ref, stack_ref
):
    height, channels, width = own_ref.shape
    spread_all(own_ref, outer_ref, one_ref, two_ref, stack_ref)

    def body(block, carry):
        start = pl.multiple_of(block * DILATION, DILATION)
        stacked = stack_ref[pl.ds(block, 3)].reshape(9 * channels, DILATION * width)
        total = jnp.dot(weight_ref[...], stacked, preferred_element_type=jnp.float32).astype(jnp.bfloat16)
        rows = jnp.stack([total[:, row * width : (row + 1) * width] for row in range(DILATION)])
        out_ref[:, pl.ds(start, DILATION), :] = jnp.swapaxes(rows, 0, 1)
        return carry

    lax.fori_loop(0, height // DILATION, body, 0)


def finish_kernel(one_ref, other_ref, weight_ref, bias_ref):
    total = one_ref[...] + other_ref[...]
    channels = total.shape[0]
    for tap in range(9):
        weight_ref[tap // 3, tap % 3] = total[:, tap * channels : (tap + 1) * channels]
    flipped = jnp.transpose(total[:, total.shape[1] - 128 :])
    bias_ref[...] = flipped[127:128, :channels]


def call(kernel, out_shapes, operands, scratch=(), flops=0):
    whole = pl.BlockSpec(memory_space=pltpu.VMEM)
    size = sum(math.prod(x.shape) * jnp.dtype(x.dtype).itemsize for x in (*operands, *out_shapes))
    return pl.pallas_call(
        kernel,
        out_shape=out_shapes,
        in_specs=[whole] * len(operands),
        out_specs=[whole] * len(out_shapes),
        scratch_shapes=list(scratch),
        compiler_params=pltpu.CompilerParams(vmem_limit_bytes=VMEM_BYTES),
        cost_estimate=pl.CostEstimate(flops=flops, bytes_accessed=size, transcendentals=0),
    )(*operands)


def shards(image, weight, bias, cotangent):
    channels, height, width = image.shape
    bf16, f32 = jnp.bfloat16, jnp.float32
    scale = 1.0 / math.sqrt(height * lax.axis_size("row") * width * lax.axis_size("col"))
    shape = jax.ShapeDtypeStruct
    pieces = width // DILATION
    own_groups, all_groups = height // pieces, (height + 2 * DILATION) // pieces
    depth = 9 * channels
    stack = pltpu.VMEM((height // DILATION + 2, 3 * channels, DILATION * width), bf16)
    edge = shape((DILATION, channels, width), bf16)
    packed = shape((all_groups, channels, width), bf16)
    own_rims = shape((2, own_groups, channels, width), bf16)
    rows = shape((height, channels, width), bf16)
    flops = 2 * depth * channels * height * width

    odd = lax.axis_index("row") % 2
    outer = shape((2, DILATION, channels, width), bf16)
    end = height - DILATION


    def image_rim(start, first):
        rim = lax.dynamic_slice_in_dim(image, start, DILATION, 1)
        flag = alone("row", first)
        return rim if flag is None else jnp.where(flag, jnp.zeros_like(rim), rim)

    one = swap_pairs(image_rim((1 - odd) * end, 0), "row", 0)
    two = swap_pairs(image_rim(odd * end, 1), "row", 1)
    image_rows, rims = call(own_kernel, (rows, own_rims), (image,))
    forward_weight = jnp.transpose(weight, (2, 0, 1, 3)).reshape(channels, depth)
    backward_weight = jnp.transpose(weight[::-1, ::-1], (3, 0, 1, 2)).reshape(channels, depth)
    one, two, image_outer = call(
        functools.partial(rim_kernel, True), (packed, packed, outer), (one, two, rims)
    )
    two, one = swap_pairs(two, "col", 1), swap_pairs(one, "col", 0)
    activation, grads, one, two, rims, terms = call(
        functools.partial(forward_kernel, scale),
        (
            shape(image.shape, bf16), rows, edge, edge, own_rims,
            shape((channels, -(-(depth + 1) // 128) * 128), f32),
        ),
        (image_rows, image_outer, one, two, cotangent, forward_weight, bias[:, None]),
        (stack, pltpu.VMEM((channels, width), f32)),
        2 * flops,
    )
    one, two = swap_pairs(one, "row", 0), swap_pairs(two, "row", 1)
    one, two, grad_outer = call(
        functools.partial(rim_kernel, False), (packed, packed, outer), (one, two, rims)
    )
    two, one = swap_pairs(two, "col", 1), swap_pairs(one, "col", 0)
    (grad_image,) = call(
        backward_kernel,
        (shape(image.shape, bf16),),
        (grads, grad_outer, one, two, backward_weight),
        (stack,),
        flops,
    )
    one, other = add_pairs(terms, "col", "row")
    grad_weight, grad_bias = call(
        finish_kernel, (shape(weight.shape, f32), shape((1, channels), f32)), (one, other)
    )
    return (activation, grad_image, grad_weight, grad_bias.reshape(channels))


def solution(mesh):
    return jax.shard_map(
        shards,
        mesh=mesh,
        in_specs=(P(None, "row", "col"), P(), P(), P(None, "row", "col")),
        out_specs=(P(None, "row", "col"), P(None, "row", "col"), P(), P()),
        check_vma=False,
    )
```

```python
import functools
import math

import jax
import jax.numpy as jnp
from jax import lax
from jax.experimental import pallas as pl
from jax.experimental.pallas import tpu as pltpu
from jax.sharding import PartitionSpec as P

DILATION = 16
VMEM_BYTES = 16 * 2**20


def partners(axis, first):
    count = lax.axis_size(axis)
    to = list(range(count))
    for at in range(first, count - 1, 2):
        to[at], to[at + 1] = at + 1, at
    return list(enumerate(to))


def alone(axis, first):
    places = [at for at, other in partners(axis, first) if at == other]
    at = lax.axis_index(axis)
    return functools.reduce(jnp.logical_or, [at == place for place in places]) if places else None


def clear_if(flag, ref):
    if flag is not None:
        @pl.when(flag)
        def _():
            ref[...] = jnp.zeros_like(ref)


def swap_pairs(value, axis, first):
    other_axis = "col" if axis == "row" else "row"
    columns = lax.axis_size("col")

    def place(at, other):
        row, column = (at, other) if axis == "row" else (other, at)
        return row * columns + column

    pairs = []
    for at, to in partners(axis, first):
        for other, other_to in partners(other_axis, 0):
            pairs.append((place(at, other), place(to, other if to != at else other_to)))
    return lax.ppermute(value, ("row", "col"), pairs)


def rounds_of(axis):
    bits = [2**k for k in reversed(range(lax.axis_size(axis).bit_length() - 1))]
    return [(axis, bits[at : at + 2]) for at in range(0, len(bits), 2)]


def add_pairs(value, near_axis, far_axis):
    other = jnp.zeros_like(value)
    for place, (axis, bits) in enumerate(rounds_of(near_axis) + rounds_of(far_axis)):
        value = value + other if place else value
        masks = bits[::-1] + [sum(bits)] if len(bits) == 2 else bits
        came = [
            lax.ppermute(value, axis, [(at, at ^ mask) for at in range(lax.axis_size(axis))]) for mask in masks
        ]
        if len(came) == 3:
            value, other = value + came[0], came[1] + came[2]
        else:
            other = came[0]
    return value, other


def gelu_pair(preact):
    coef = 0.7978845608
    square = preact * preact
    tval = jnp.tanh(coef * (preact + 0.044715 * (square * preact)))
    half = 0.5 * (1.0 + tval)
    slope_val = half + 0.5 * preact * (1.0 - tval * tval) * coef * (1.0 + 3.0 * 0.044715 * square)
    return (preact * half, slope_val)


def lane_of(shape):
    return lax.broadcasted_iota(jnp.int32, shape, len(shape) - 1)


def pack_group(rows):
    half = len(rows) // 2
    width = rows[0].shape[-1]
    lane = lane_of(rows[0].shape)
    pair = lane // (2 * DILATION)
    front = lane % (2 * DILATION) < DILATION

    def joined(part):
        total = pltpu.roll(part[0], DILATION, 1)
        for k in range(1, half):
            total = jnp.where(pair == k, pltpu.roll(part[k], DILATION + 2 * DILATION * k, 1), total)
        return total

    low, high = joined(rows[:half]), joined(rows[half:])
    first = jnp.where(front, pltpu.roll(low, width - DILATION, 1), high)
    last = jnp.where(front, low, pltpu.roll(high, DILATION, 1))
    return first, last


def unpack_group(from_left, from_right, count):
    half = count // 2
    width = from_left.shape[-1]
    front = lane_of(from_left.shape) % (2 * DILATION) < DILATION
    low = jnp.where(front, from_right, pltpu.roll(from_left, DILATION, 1))
    high = jnp.where(front, pltpu.roll(from_right, width - DILATION, 1), from_left)
    return [
        pltpu.roll(low if k < half else high, (width - DILATION - 2 * DILATION * (k % half)) % width, 1)
        for k in range(count)
    ]


def pack_rows(block, store, first_group):
    pieces = block.shape[-1] // DILATION
    for group in range(block.shape[0] // pieces):
        first, last = pack_group([block[group * pieces + k] for k in range(pieces)])
        store(first_group + group, first, last)


def own_kernel(image_ref, rows_ref, rims_ref):
    count = image_ref.shape[1] // DILATION
    groups = rims_ref.shape[1] // count

    def store(place, first, last):
        rims_ref[0, place] = first
        rims_ref[1, place] = last

    def body(block, carry):
        start = pl.multiple_of(block * DILATION, DILATION)
        rows = jnp.swapaxes(image_ref[:, pl.ds(start, DILATION), :], 0, 1)
        rows_ref[pl.ds(start, DILATION)] = rows
        pack_rows(rows, store, block * groups)
        return carry

    lax.fori_loop(0, count, body, 0)


def either(axis, body, one, two):
    odd = lax.axis_index(axis) % 2 == 1
    pl.when(odd)(lambda: body(one, two))
    pl.when(jnp.logical_not(odd))(lambda: body(two, one))


def rim_kernel(swap, one_ref, two_ref, rims_ref, send_one_ref, send_two_ref, outer_ref):
    own = rims_ref.shape[1]
    groups = (send_one_ref.shape[0] - own) // 2

    def order(upper_ref, lower_ref):
        for index, ref in enumerate((upper_ref, lower_ref)):
            outer_ref[index] = jnp.swapaxes(ref[...], 0, 1) if swap else ref[...]

    def pack(send_first_ref, send_last_ref):
        def store(place, first, last):
            send_first_ref[place] = first
            send_last_ref[place] = last

        send_first_ref[groups : groups + own] = rims_ref[0]
        send_last_ref[groups : groups + own] = rims_ref[1]
        for index in range(2):
            pack_rows(outer_ref[index], store, index * (groups + own))

    either("row", order, one_ref, two_ref)
    either("col", pack, send_one_ref, send_two_ref)
    clear_if(alone("col", 0), send_one_ref)
    clear_if(alone("col", 1), send_two_ref)


def spread(rows_of, left_ref, right_ref, stack_ref, block, group_start):
    channels, width = left_ref.shape[1:]
    pieces = width // DILATION
    lane = lane_of((channels, width))
    for group in range(DILATION // pieces):
        rims = unpack_group(left_ref[group_start + group], right_ref[group_start + group], pieces)
        for k in range(pieces):
            row = group * pieces + k
            value = rows_of(row)
            columns = slice(row * width, (row + 1) * width)
            before = jnp.where(lane < DILATION, rims[k], pltpu.roll(value, DILATION, 1))
            after = jnp.where(lane >= width - DILATION, rims[k], pltpu.roll(value, width - DILATION, 1))
            stack_ref[block, 0:channels, columns] = before
            stack_ref[block, channels : 2 * channels, columns] = value
            stack_ref[block, 2 * channels : 3 * channels, columns] = after


def spread_all(own_ref, outer_ref, one_ref, two_ref, stack_ref):
    count = own_ref.shape[0] // DILATION
    groups = one_ref.shape[0] // (count + 2)

    def every(left_ref, right_ref):
        spread(lambda row: outer_ref[0, row], left_ref, right_ref, stack_ref, 0, 0)

        def body(block, carry):
            spread(
                lambda row: own_ref[block * DILATION + row],
                left_ref, right_ref, stack_ref, block + 1, (block + 1) * groups,
            )
            return carry

        lax.fori_loop(0, count, body, 0)
        spread(lambda row: outer_ref[1, row], left_ref, right_ref, stack_ref, count + 1, (count + 1) * groups)

    either("col", every, one_ref, two_ref)


def forward_kernel(
    scale, own_ref, outer_ref, one_ref, two_ref, cotangent_ref, weight_ref, bias_ref,
    activation_ref, grad_ref, send_one_ref, send_two_ref, rims_ref, terms_ref, stack_ref, sum_ref,
):
    height, channels, width = own_ref.shape
    count = height // DILATION
    groups = rims_ref.shape[1] // count
    spread_all(own_ref, outer_ref, one_ref, two_ref, stack_ref)
    terms_ref[...] = jnp.zeros_like(terms_ref)
    sum_ref[...] = jnp.zeros_like(sum_ref)
    depth = 9 * channels

    def store(place, first, last):
        rims_ref[0, place] = first
        rims_ref[1, place] = last

    def body(block, carry):
        start = pl.multiple_of(block * DILATION, DILATION)
        stacked = stack_ref[pl.ds(block, 3)].reshape(depth, DILATION * width)
        preact = jnp.dot(weight_ref[...], stacked, preferred_element_type=jnp.float32)
        cotangent = jnp.swapaxes(cotangent_ref[:, pl.ds(start, DILATION), :], 0, 1)
        bias = jnp.broadcast_to(bias_ref[...], (channels, width))
        values, grads = [], []
        total = sum_ref[...]
        for row in range(DILATION):
            value, slope_val = gelu_pair(preact[:, row * width : (row + 1) * width] + bias)
            values.append(value.astype(jnp.bfloat16))
            grad = (cotangent[row].astype(jnp.float32) * slope_val).astype(jnp.bfloat16)
            grads.append(grad)
            total = total + grad.astype(jnp.float32)
            grad_ref[start + row] = grad
        sum_ref[...] = total
        activation_ref[:, pl.ds(start, DILATION), :] = jnp.swapaxes(jnp.stack(values), 0, 1)
        terms_ref[:, :depth] += lax.dot_general(
            jnp.concatenate(grads, axis=1), stacked, (((1,), (1,)), ((), ())),
            preferred_element_type=jnp.float32,
        )
        pack_rows(jnp.stack(grads), store, block * groups)
        return carry

    lax.fori_loop(0, count, body, 0)
    end = height - DILATION
    odd = lax.axis_index("row") % 2
    send_one_ref[...] = grad_ref[pl.ds((1 - odd) * end, DILATION)]
    send_two_ref[...] = grad_ref[pl.ds(odd * end, DILATION)]
    clear_if(alone("row", 0), send_one_ref)
    clear_if(alone("row", 1), send_two_ref)
    terms_ref[:, :depth] = terms_ref[:, :depth] * scale
    sums = jnp.sum(sum_ref[...], axis=1, keepdims=True) * scale
    terms_ref[:, depth:] = jnp.broadcast_to(sums, (channels, terms_ref.shape[1] - depth))


def backward_kernel(
    own_ref, outer_ref, one_ref, two_ref, weight_ref, out_ref, stack_ref
):
    height, channels, width = own_ref.shape
    spread_all(own_ref, outer_ref, one_ref, two_ref, stack_ref)

    def body(block, carry):
        start = pl.multiple_of(block * DILATION, DILATION)
        stacked = stack_ref[pl.ds(block, 3)].reshape(9 * channels, DILATION * width)
        total = jnp.dot(weight_ref[...], stacked, preferred_element_type=jnp.float32).astype(jnp.bfloat16)
        rows = jnp.stack([total[:, row * width : (row + 1) * width] for row in range(DILATION)])
        out_ref[:, pl.ds(start, DILATION), :] = jnp.swapaxes(rows, 0, 1)
        return carry

    lax.fori_loop(0, height // DILATION, body, 0)


def finish_kernel(one_ref, other_ref, after_ref, weight_ref, bias_ref):
    total = one_ref[...] + other_ref[...]
    channels = total.shape[0]
    for tap in range(9):
        weight_ref[tap // 3, tap % 3] = total[:, tap * channels : (tap + 1) * channels]
    flipped = jnp.transpose(total[:, total.shape[1] - 128 :])
    bias_ref[...] = flipped[127:128, :channels]


def call(kernel, out_shapes, operands, scratch=(), flops=0, after=()):
    whole = pl.BlockSpec(memory_space=pltpu.VMEM)
    size = sum(math.prod(x.shape) * jnp.dtype(x.dtype).itemsize for x in (*operands, *out_shapes))
    return pl.pallas_call(
        kernel,
        out_shape=out_shapes,
        in_specs=[whole] * len(operands) + [pl.BlockSpec(memory_space=pl.ANY)] * len(after),
        out_specs=[whole] * len(out_shapes),
        scratch_shapes=list(scratch),
        compiler_params=pltpu.CompilerParams(vmem_limit_bytes=VMEM_BYTES),
        cost_estimate=pl.CostEstimate(flops=flops, bytes_accessed=size, transcendentals=0),
    )(*operands, *after)


def shards(image, weight, bias, cotangent):
    channels, height, width = image.shape
    bf16, f32 = jnp.bfloat16, jnp.float32
    scale = 1.0 / math.sqrt(height * lax.axis_size("row") * width * lax.axis_size("col"))
    shape = jax.ShapeDtypeStruct
    pieces = width // DILATION
    own_groups, all_groups = height // pieces, (height + 2 * DILATION) // pieces
    depth = 9 * channels
    stack = pltpu.VMEM((height // DILATION + 2, 3 * channels, DILATION * width), bf16)
    edge = shape((DILATION, channels, width), bf16)
    packed = shape((all_groups, channels, width), bf16)
    own_rims = shape((2, own_groups, channels, width), bf16)
    rows = shape((height, channels, width), bf16)
    flops = 2 * depth * channels * height * width

    odd = lax.axis_index("row") % 2
    outer = shape((2, DILATION, channels, width), bf16)
    end = height - DILATION


    def image_rim(start, first):
        rim = lax.dynamic_slice_in_dim(image, start, DILATION, 1)
        flag = alone("row", first)
        return rim if flag is None else jnp.where(flag, jnp.zeros_like(rim), rim)

    one = swap_pairs(image_rim((1 - odd) * end, 0), "row", 0)
    two = swap_pairs(image_rim(odd * end, 1), "row", 1)
    image_rows, rims = call(own_kernel, (rows, own_rims), (image,))
    forward_weight = jnp.transpose(weight, (2, 0, 1, 3)).reshape(channels, depth)
    backward_weight = jnp.transpose(weight[::-1, ::-1], (3, 0, 1, 2)).reshape(channels, depth)
    one, two, image_outer = call(
        functools.partial(rim_kernel, True), (packed, packed, outer), (one, two, rims)
    )
    two, one = swap_pairs(two, "col", 1), swap_pairs(one, "col", 0)
    activation, grads, one, two, rims, terms = call(
        functools.partial(forward_kernel, scale),
        (
            shape(image.shape, bf16), rows, edge, edge, own_rims,
            shape((channels, -(-(depth + 1) // 128) * 128), f32),
        ),
        (image_rows, image_outer, one, two, cotangent, forward_weight, bias[:, None]),
        (stack, pltpu.VMEM((channels, width), f32)),
        2 * flops,
    )
    one, two = swap_pairs(one, "row", 0), swap_pairs(two, "row", 1)
    one, two, grad_outer = call(
        functools.partial(rim_kernel, False), (packed, packed, outer), (one, two, rims)
    )
    two, one = swap_pairs(two, "col", 1), swap_pairs(one, "col", 0)
    (grad_image,) = call(
        backward_kernel,
        (shape(image.shape, bf16),),
        (grads, grad_outer, one, two, backward_weight),
        (stack,),
        flops,
    )
    one, other = add_pairs(terms, "col", "row")
    grad_weight, grad_bias = call(
        finish_kernel, (shape(weight.shape, f32), shape((1, channels), f32)), (one, other),
        after=(grad_image,),
    )
    return (activation, grad_image, grad_weight, grad_bias.reshape(channels))


def solution(mesh):
    return jax.shard_map(
        shards,
        mesh=mesh,
        in_specs=(P(None, "row", "col"), P(), P(), P(None, "row", "col")),
        out_specs=(P(None, "row", "col"), P(None, "row", "col"), P(), P()),
        check_vma=False,
    )
```

```python
import functools
import math

import jax
import jax.numpy as jnp
from jax import lax
from jax.experimental import pallas as pl
from jax.experimental.pallas import tpu as pltpu
from jax.sharding import PartitionSpec as P

DILATION = 16
VMEM_BYTES = 16 * 2**20


def partners(axis, first):
    count = lax.axis_size(axis)
    to = list(range(count))
    for at in range(first, count - 1, 2):
        to[at], to[at + 1] = at + 1, at
    return list(enumerate(to))


def alone(axis, first):
    places = [at for at, other in partners(axis, first) if at == other]
    at = lax.axis_index(axis)
    return functools.reduce(jnp.logical_or, [at == place for place in places]) if places else None


def clear_if(flag, ref):
    if flag is not None:
        @pl.when(flag)
        def _():
            ref[...] = jnp.zeros_like(ref)


def swap_pairs(value, axis, first):
    other_axis = "col" if axis == "row" else "row"
    columns = lax.axis_size("col")

    def place(at, other):
        row, column = (at, other) if axis == "row" else (other, at)
        return row * columns + column

    pairs = []
    for at, to in partners(axis, first):
        for other, other_to in partners(other_axis, 0):
            pairs.append((place(at, other), place(to, other if to != at else other_to)))
    return lax.ppermute(value, ("row", "col"), pairs)


def rounds_of(axis):
    bits = [2**k for k in reversed(range(lax.axis_size(axis).bit_length() - 1))]
    return [(axis, bits[at : at + 2]) for at in range(0, len(bits), 2)]


def swap_corners(value, first_row, first_column):
    columns = lax.axis_size("col")
    pairs = [
        (row * columns + column, row_to * columns + column_to)
        for row, row_to in partners("row", first_row)
        for column, column_to in partners("col", first_column)
    ]
    return lax.ppermute(value, ("row", "col"), pairs)


def add_pairs(value, near_axis, far_axis):
    other = jnp.zeros_like(value)
    for place, (axis, bits) in enumerate(rounds_of(near_axis) + rounds_of(far_axis)):
        value = value + other if place else value
        masks = bits[::-1] + [sum(bits)] if len(bits) == 2 else bits
        came = [
            lax.ppermute(value, axis, [(at, at ^ mask) for at in range(lax.axis_size(axis))]) for mask in masks
        ]
        if len(came) == 3:
            value, other = value + came[0], came[1] + came[2]
        else:
            other = came[0]
    return value, other


def gelu_pair(preact):
    coef = 0.7978845608
    square = preact * preact
    tval = jnp.tanh(coef * (preact + 0.044715 * (square * preact)))
    half = 0.5 * (1.0 + tval)
    slope_val = half + 0.5 * preact * (1.0 - tval * tval) * coef * (1.0 + 3.0 * 0.044715 * square)
    return (preact * half, slope_val)


def lane_of(shape):
    return lax.broadcasted_iota(jnp.int32, shape, len(shape) - 1)


def pack_group(rows):
    half = len(rows) // 2
    width = rows[0].shape[-1]
    lane = lane_of(rows[0].shape)
    pair = lane // (2 * DILATION)
    front = lane % (2 * DILATION) < DILATION

    def joined(part):
        total = pltpu.roll(part[0], DILATION, 1)
        for k in range(1, half):
            total = jnp.where(pair == k, pltpu.roll(part[k], DILATION + 2 * DILATION * k, 1), total)
        return total

    low, high = joined(rows[:half]), joined(rows[half:])
    first = jnp.where(front, pltpu.roll(low, width - DILATION, 1), high)
    last = jnp.where(front, low, pltpu.roll(high, DILATION, 1))
    return first, last


def unpack_group(from_left, from_right, count):
    half = count // 2
    width = from_left.shape[-1]
    front = lane_of(from_left.shape) % (2 * DILATION) < DILATION
    low = jnp.where(front, from_right, pltpu.roll(from_left, DILATION, 1))
    high = jnp.where(front, pltpu.roll(from_right, width - DILATION, 1), from_left)
    return [
        pltpu.roll(low if k < half else high, (width - DILATION - 2 * DILATION * (k % half)) % width, 1)
        for k in range(count)
    ]


def pack_rows(block, store, first_group):
    pieces = block.shape[-1] // DILATION
    for group in range(block.shape[0] // pieces):
        first, last = pack_group([block[group * pieces + k] for k in range(pieces)])
        store(first_group + group, first, last)


def own_kernel(image_ref, rows_ref, one_ref, two_ref, corner_one_ref, corner_two_ref, rims_ref):
    count = image_ref.shape[1] // DILATION
    groups = rims_ref.shape[1] // count

    def store(place, first, last):
        rims_ref[0, place] = first
        rims_ref[1, place] = last

    def body(block, carry):
        start = pl.multiple_of(block * DILATION, DILATION)
        rows = jnp.swapaxes(image_ref[:, pl.ds(start, DILATION), :], 0, 1)
        rows_ref[pl.ds(start, DILATION)] = rows
        pack_rows(rows, store, block * groups)
        return carry

    lax.fori_loop(0, count, body, 0)
    odd_row, odd_column = lax.axis_index("row") % 2, lax.axis_index("col") % 2
    start = (1 - odd_row) * (rims_ref.shape[1] - groups)
    one_ref[...] = rims_ref[1 - odd_column]
    two_ref[...] = rims_ref[odd_column]
    corner_one_ref[...] = rims_ref[1 - odd_column, pl.ds(start, groups)]
    corner_two_ref[...] = rims_ref[odd_column, pl.ds(start, groups)]
    for first, rim_ref, corner_ref in ((0, one_ref, corner_one_ref), (1, two_ref, corner_two_ref)):
        clear_if(alone("col", first), rim_ref)
        clear_if(alone("col", first), corner_ref)
        clear_if(alone("row", 0), corner_ref)


def join_kernel(rows_ref, edge_ref, one_ref, two_ref, corner_one_ref, corner_two_ref, out_ref, near_ref):
    odd = lax.axis_index("row") % 2
    groups = (out_ref.shape[0] - DILATION) // 2
    start = odd * (one_ref.shape[0] - groups)
    out_ref[:DILATION] = rows_ref[pl.ds(odd * (rows_ref.shape[0] - DILATION), DILATION)]
    out_ref[DILATION : DILATION + groups] = one_ref[pl.ds(start, groups)]
    out_ref[DILATION + groups :] = two_ref[pl.ds(start, groups)]
    clear_if(alone("row", 1), out_ref)
    near_ref[:DILATION] = jnp.swapaxes(edge_ref[...], 0, 1)
    near_ref[DILATION : DILATION + groups] = corner_one_ref[...]
    near_ref[DILATION + groups :] = corner_two_ref[...]


def either(axis, body, one, two):
    odd = lax.axis_index(axis) % 2 == 1
    pl.when(odd)(lambda: body(one, two))
    pl.when(jnp.logical_not(odd))(lambda: body(two, one))


def rim_kernel(one_ref, two_ref, rims_ref, send_one_ref, send_two_ref, outer_ref):
    own = rims_ref.shape[1]
    groups = (send_one_ref.shape[0] - own) // 2

    def order(upper_ref, lower_ref):
        for index, ref in enumerate((upper_ref, lower_ref)):
            outer_ref[index] = ref[...]

    def pack(send_first_ref, send_last_ref):
        def store(place, first, last):
            send_first_ref[place] = first
            send_last_ref[place] = last

        send_first_ref[groups : groups + own] = rims_ref[0]
        send_last_ref[groups : groups + own] = rims_ref[1]
        for index in range(2):
            pack_rows(outer_ref[index], store, index * (groups + own))

    either("row", order, one_ref, two_ref)
    either("col", pack, send_one_ref, send_two_ref)
    clear_if(alone("col", 0), send_one_ref)
    clear_if(alone("col", 1), send_two_ref)


def spread(rows_of, left_of, right_of, stack_ref, block):
    channels, width = stack_ref.shape[1] // 3, stack_ref.shape[2] // DILATION
    pieces = width // DILATION
    lane = lane_of((channels, width))
    for group in range(DILATION // pieces):
        rims = unpack_group(left_of(group), right_of(group), pieces)
        for k in range(pieces):
            row = group * pieces + k
            value = rows_of(row)
            columns = slice(row * width, (row + 1) * width)
            before = jnp.where(lane < DILATION, rims[k], pltpu.roll(value, DILATION, 1))
            after = jnp.where(lane >= width - DILATION, rims[k], pltpu.roll(value, width - DILATION, 1))
            stack_ref[block, 0:channels, columns] = before
            stack_ref[block, channels : 2 * channels, columns] = value
            stack_ref[block, 2 * channels : 3 * channels, columns] = after


def spread_blocks(blocks, left_ref, right_ref, stack_ref):
    for rows_of, left_start, right_start, place in blocks:
        spread(
            rows_of,
            lambda group, start=left_start: left_ref[start + group],
            lambda group, start=right_start: right_ref[start + group],
            stack_ref,
            place,
        )


def spread_own(own_ref, left_ref, right_ref, stack_ref, start):
    count = own_ref.shape[0] // DILATION
    groups = DILATION * DILATION // own_ref.shape[2]

    def body(block, carry):
        at = start + block * groups
        spread_blocks(
            [(lambda row: own_ref[block * DILATION + row], at, at, block + 1)], left_ref, right_ref, stack_ref
        )
        return carry

    lax.fori_loop(0, count, body, 0)


def spread_joined(own_ref, near_ref, far_ref, one_ref, two_ref, stack_ref):
    last = own_ref.shape[0] // DILATION + 1
    groups = (near_ref.shape[0] - DILATION) // 2
    near = jnp.where(lax.axis_index("row") % 2 == 1, 0, last)

    def every(left, right):
        (left_ref, left_start), (right_ref, right_start) = left, right
        spread_own(own_ref, left_ref, right_ref, stack_ref, 0)
        for ref, place in ((near_ref, near), (far_ref, last - near)):
            block = (lambda row, ref=ref: ref[row], left_start, right_start, place)
            spread_blocks([block], ref, ref, stack_ref)

    either("col", every, (one_ref, DILATION), (two_ref, DILATION + groups))


def spread_outer(own_ref, outer_ref, one_ref, two_ref, stack_ref):
    count = own_ref.shape[0] // DILATION
    groups = one_ref.shape[0] // (count + 2)
    end = (count + 1) * groups

    def every(left_ref, right_ref):
        blocks = [
            (lambda row: outer_ref[0, row], 0, 0, 0), (lambda row: outer_ref[1, row], end, end, count + 1)
        ]
        spread_blocks(blocks, left_ref, right_ref, stack_ref)
        spread_own(own_ref, left_ref, right_ref, stack_ref, groups)

    either("col", every, one_ref, two_ref)


def forward_kernel(
    scale, own_ref, near_ref, far_ref, one_ref, two_ref, cotangent_ref, weight_ref, bias_ref,
    activation_ref, grad_ref, send_one_ref, send_two_ref, rims_ref, terms_ref, stack_ref, sum_ref,
):
    height, channels, width = own_ref.shape
    count = height // DILATION
    groups = rims_ref.shape[1] // count
    spread_joined(own_ref, near_ref, far_ref, one_ref, two_ref, stack_ref)
    terms_ref[...] = jnp.zeros_like(terms_ref)
    sum_ref[...] = jnp.zeros_like(sum_ref)
    depth = 9 * channels

    def store(place, first, last):
        rims_ref[0, place] = first
        rims_ref[1, place] = last

    def body(block, carry):
        start = pl.multiple_of(block * DILATION, DILATION)
        stacked = stack_ref[pl.ds(block, 3)].reshape(depth, DILATION * width)
        preact = jnp.dot(weight_ref[...], stacked, preferred_element_type=jnp.float32)
        cotangent = jnp.swapaxes(cotangent_ref[:, pl.ds(start, DILATION), :], 0, 1)
        bias = jnp.broadcast_to(bias_ref[...], (channels, width))
        values, grads = [], []
        total = sum_ref[...]
        for row in range(DILATION):
            value, slope_val = gelu_pair(preact[:, row * width : (row + 1) * width] + bias)
            values.append(value.astype(jnp.bfloat16))
            grad = (cotangent[row].astype(jnp.float32) * slope_val).astype(jnp.bfloat16)
            grads.append(grad)
            total = total + grad.astype(jnp.float32)
            grad_ref[start + row] = grad
        sum_ref[...] = total
        activation_ref[:, pl.ds(start, DILATION), :] = jnp.swapaxes(jnp.stack(values), 0, 1)
        terms_ref[:, :depth] += lax.dot_general(
            jnp.concatenate(grads, axis=1), stacked, (((1,), (1,)), ((), ())),
            preferred_element_type=jnp.float32,
        )
        pack_rows(jnp.stack(grads), store, block * groups)
        return carry

    lax.fori_loop(0, count, body, 0)
    end = height - DILATION
    odd = lax.axis_index("row") % 2
    send_one_ref[...] = grad_ref[pl.ds((1 - odd) * end, DILATION)]
    send_two_ref[...] = grad_ref[pl.ds(odd * end, DILATION)]
    clear_if(alone("row", 0), send_one_ref)
    clear_if(alone("row", 1), send_two_ref)
    terms_ref[:, :depth] = terms_ref[:, :depth] * scale
    sums = jnp.sum(sum_ref[...], axis=1, keepdims=True) * scale
    terms_ref[:, depth:] = jnp.broadcast_to(sums, (channels, terms_ref.shape[1] - depth))


def backward_kernel(
    own_ref, outer_ref, one_ref, two_ref, weight_ref, out_ref, token_ref, stack_ref
):
    height, channels, width = own_ref.shape
    token_ref[...] = jnp.zeros_like(token_ref)
    spread_outer(own_ref, outer_ref, one_ref, two_ref, stack_ref)

    def body(block, carry):
        start = pl.multiple_of(block * DILATION, DILATION)
        stacked = stack_ref[pl.ds(block, 3)].reshape(9 * channels, DILATION * width)
        total = jnp.dot(weight_ref[...], stacked, preferred_element_type=jnp.float32).astype(jnp.bfloat16)
        rows = jnp.stack([total[:, row * width : (row + 1) * width] for row in range(DILATION)])
        out_ref[:, pl.ds(start, DILATION), :] = jnp.swapaxes(rows, 0, 1)
        return carry

    lax.fori_loop(0, height // DILATION, body, 0)


def finish_kernel(one_ref, other_ref, after_ref, weight_ref, bias_ref):
    total = one_ref[...] + other_ref[...]
    channels = total.shape[0]
    for tap in range(9):
        weight_ref[tap // 3, tap % 3] = total[:, tap * channels : (tap + 1) * channels]
    flipped = jnp.transpose(total[:, total.shape[1] - 128 :])
    bias_ref[...] = flipped[127:128, :channels]


def call(kernel, out_shapes, operands, scratch=(), flops=0):
    whole = pl.BlockSpec(memory_space=pltpu.VMEM)
    size = sum(math.prod(x.shape) * jnp.dtype(x.dtype).itemsize for x in (*operands, *out_shapes))
    return pl.pallas_call(
        kernel,
        out_shape=out_shapes,
        in_specs=[whole] * len(operands),
        out_specs=[whole] * len(out_shapes),
        scratch_shapes=list(scratch),
        compiler_params=pltpu.CompilerParams(vmem_limit_bytes=VMEM_BYTES),
        cost_estimate=pl.CostEstimate(flops=flops, bytes_accessed=size, transcendentals=0),
    )(*operands)


def shards(image, weight, bias, cotangent):
    channels, height, width = image.shape
    bf16, f32 = jnp.bfloat16, jnp.float32
    scale = 1.0 / math.sqrt(height * lax.axis_size("row") * width * lax.axis_size("col"))
    shape = jax.ShapeDtypeStruct
    pieces = width // DILATION
    groups, own_groups = DILATION // pieces, height // pieces
    depth = 9 * channels
    stack = pltpu.VMEM((height // DILATION + 2, 3 * channels, DILATION * width), bf16)
    edge = shape((DILATION, channels, width), bf16)
    corner = shape((groups, channels, width), bf16)
    own_packed = shape((own_groups, channels, width), bf16)
    packed = shape((own_groups + 2 * groups, channels, width), bf16)
    joint = shape((DILATION + 2 * groups, channels, width), bf16)
    own_rims = shape((2, own_groups, channels, width), bf16)
    outer = shape((2, DILATION, channels, width), bf16)
    rows = shape((height, channels, width), bf16)
    flops = 2 * depth * channels * height * width

    even = 1 - lax.axis_index("row") % 2
    rim = lax.dynamic_slice_in_dim(image, even * (height - DILATION), DILATION, 1)
    flag = alone("row", 0)
    rim = swap_pairs(rim if flag is None else jnp.where(flag, jnp.zeros_like(rim), rim), "row", 0)
    image_rows, one, two, corner_one, corner_two = call(
        own_kernel, (rows, own_packed, own_packed, corner, corner), (image,), (pltpu.VMEM(own_rims.shape, bf16),)
    )
    forward_weight = jnp.transpose(weight, (2, 0, 1, 3)).reshape(channels, depth)
    backward_weight = jnp.transpose(weight[::-1, ::-1], (3, 0, 1, 2)).reshape(channels, depth)
    one, two = swap_pairs(one, "col", 0), swap_pairs(two, "col", 1)
    corner_one, corner_two = swap_corners(corner_one, 0, 0), swap_corners(corner_two, 0, 1)
    far, near = call(join_kernel, (joint, joint), (image_rows, rim, one, two, corner_one, corner_two))
    far = swap_pairs(far, "row", 1)
    activation, grads, one, two, rims, terms = call(
        functools.partial(forward_kernel, scale),
        (
            shape(image.shape, bf16), rows, edge, edge, own_rims,
            shape((channels, -(-(depth + 1) // 128) * 128), f32),
        ),
        (image_rows, near, far, one, two, cotangent, forward_weight, bias[:, None]),
        (stack, pltpu.VMEM((channels, width), f32)),
        2 * flops,
    )
    one, two = swap_pairs(one, "row", 0), swap_pairs(two, "row", 1)
    one, two, grad_outer = call(rim_kernel, (packed, packed, outer), (one, two, rims))
    two, one = swap_pairs(two, "col", 1), swap_pairs(one, "col", 0)
    grad_image, token = call(
        backward_kernel,
        (shape(image.shape, bf16), shape((8, 128), f32)),
        (grads, grad_outer, one, two, backward_weight),
        (stack,),
        flops,
    )
    one, other = add_pairs(terms, "col", "row")
    grad_weight, grad_bias = call(
        finish_kernel, (shape(weight.shape, f32), shape((1, channels), f32)), (one, other, token)
    )
    return (activation, grad_image, grad_weight, grad_bias.reshape(channels))


def solution(mesh):
    return jax.shard_map(
        shards,
        mesh=mesh,
        in_specs=(P(None, "row", "col"), P(), P(), P(None, "row", "col")),
        out_specs=(P(None, "row", "col"), P(None, "row", "col"), P(), P()),
        check_vma=False,
    )
```

```python
import functools
import math

import jax
import jax.numpy as jnp
from jax import lax
from jax.experimental import pallas as pl
from jax.experimental.pallas import tpu as pltpu
from jax.sharding import PartitionSpec as P

DILATION = 16
VMEM_BYTES = 16 * 2**20


def partners(axis, first):
    count = lax.axis_size(axis)
    to = list(range(count))
    for at in range(first, count - 1, 2):
        to[at], to[at + 1] = at + 1, at
    return list(enumerate(to))


def alone(axis, first):
    places = [at for at, other in partners(axis, first) if at == other]
    at = lax.axis_index(axis)
    return functools.reduce(jnp.logical_or, [at == place for place in places]) if places else None


def clear_if(flag, ref):
    if flag is not None:
        @pl.when(flag)
        def _():
            ref[...] = jnp.zeros_like(ref)


def swap_pairs(value, axis, first):
    other_axis = "col" if axis == "row" else "row"
    columns = lax.axis_size("col")

    def place(at, other):
        row, column = (at, other) if axis == "row" else (other, at)
        return row * columns + column

    pairs = []
    for at, to in partners(axis, first):
        for other, other_to in partners(other_axis, 0):
            pairs.append((place(at, other), place(to, other if to != at else other_to)))
    return lax.ppermute(value, ("row", "col"), pairs)


def rounds_of(axis):
    bits = [2**k for k in reversed(range(lax.axis_size(axis).bit_length() - 1))]
    return [(axis, bits[at : at + 2]) for at in range(0, len(bits), 2)]


def add_pairs(value, near_axis, far_axis):
    other = jnp.zeros_like(value)
    for place, (axis, bits) in enumerate(rounds_of(near_axis) + rounds_of(far_axis)):
        value = value + other if place else value
        masks = bits[::-1] + [sum(bits)] if len(bits) == 2 else bits
        came = [
            lax.ppermute(value, axis, [(at, at ^ mask) for at in range(lax.axis_size(axis))]) for mask in masks
        ]
        if len(came) == 3:
            value, other = value + came[0], came[1] + came[2]
        else:
            other = came[0]
    return value, other


def gelu_pair(preact):
    coef = 0.7978845608
    square = preact * preact
    tval = jnp.tanh(coef * (preact + 0.044715 * (square * preact)))
    half = 0.5 * (1.0 + tval)
    slope_val = half + 0.5 * preact * (1.0 - tval * tval) * coef * (1.0 + 3.0 * 0.044715 * square)
    return (preact * half, slope_val)


def lane_of(shape):
    return lax.broadcasted_iota(jnp.int32, shape, len(shape) - 1)


def pack_group(rows):
    half = len(rows) // 2
    width = rows[0].shape[-1]
    lane = lane_of(rows[0].shape)
    pair = lane // (2 * DILATION)
    front = lane % (2 * DILATION) < DILATION

    def joined(part):
        total = pltpu.roll(part[0], DILATION, 1)
        for k in range(1, half):
            total = jnp.where(pair == k, pltpu.roll(part[k], DILATION + 2 * DILATION * k, 1), total)
        return total

    low, high = joined(rows[:half]), joined(rows[half:])
    first = jnp.where(front, pltpu.roll(low, width - DILATION, 1), high)
    last = jnp.where(front, low, pltpu.roll(high, DILATION, 1))
    return first, last


def unpack_group(from_left, from_right, count):
    half = count // 2
    width = from_left.shape[-1]
    front = lane_of(from_left.shape) % (2 * DILATION) < DILATION
    low = jnp.where(front, from_right, pltpu.roll(from_left, DILATION, 1))
    high = jnp.where(front, pltpu.roll(from_right, width - DILATION, 1), from_left)
    return [
        pltpu.roll(low if k < half else high, (width - DILATION - 2 * DILATION * (k % half)) % width, 1)
        for k in range(count)
    ]


def pack_rows(block, store, first_group):
    pieces = block.shape[-1] // DILATION
    for group in range(block.shape[0] // pieces):
        first, last = pack_group([block[group * pieces + k] for k in range(pieces)])
        store(first_group + group, first, last)


def own_kernel(image_ref, rows_ref, rims_ref):
    count = image_ref.shape[1] // DILATION
    groups = rims_ref.shape[1] // count

    def store(place, first, last):
        rims_ref[0, place] = first
        rims_ref[1, place] = last

    def body(block, carry):
        start = pl.multiple_of(block * DILATION, DILATION)
        rows = jnp.swapaxes(image_ref[:, pl.ds(start, DILATION), :], 0, 1)
        rows_ref[pl.ds(start, DILATION)] = rows
        pack_rows(rows, store, block * groups)
        return carry

    lax.fori_loop(0, count, body, 0)


def either(axis, body, one, two):
    odd = lax.axis_index(axis) % 2 == 1
    pl.when(odd)(lambda: body(one, two))
    pl.when(jnp.logical_not(odd))(lambda: body(two, one))


def rim_kernel(swap, one_ref, two_ref, rims_ref, send_one_ref, send_two_ref, outer_ref):
    own = rims_ref.shape[1]
    groups = (send_one_ref.shape[0] - own) // 2

    def order(upper_ref, lower_ref):
        for index, ref in enumerate((upper_ref, lower_ref)):
            outer_ref[index] = jnp.swapaxes(ref[...], 0, 1) if swap else ref[...]

    def pack(send_first_ref, send_last_ref):
        def store(place, first, last):
            send_first_ref[place] = first
            send_last_ref[place] = last

        send_first_ref[groups : groups + own] = rims_ref[0]
        send_last_ref[groups : groups + own] = rims_ref[1]
        for index in range(2):
            pack_rows(outer_ref[index], store, index * (groups + own))

    either("row", order, one_ref, two_ref)
    either("col", pack, send_one_ref, send_two_ref)
    clear_if(alone("col", 0), send_one_ref)
    clear_if(alone("col", 1), send_two_ref)


def spread(rows_of, left_ref, right_ref, stack_ref, block, group_start):
    channels, width = left_ref.shape[1:]
    pieces = width // DILATION
    lane = lane_of((channels, width))
    for group in range(DILATION // pieces):
        rims = unpack_group(left_ref[group_start + group], right_ref[group_start + group], pieces)
        for k in range(pieces):
            row = group * pieces + k
            value = rows_of(row)
            columns = slice(row * width, (row + 1) * width)
            before = jnp.where(lane < DILATION, rims[k], pltpu.roll(value, DILATION, 1))
            after = jnp.where(lane >= width - DILATION, rims[k], pltpu.roll(value, width - DILATION, 1))
            stack_ref[block, 0:channels, columns] = before
            stack_ref[block, channels : 2 * channels, columns] = value
            stack_ref[block, 2 * channels : 3 * channels, columns] = after


def spread_all(own_ref, outer_ref, one_ref, two_ref, stack_ref):
    count = own_ref.shape[0] // DILATION
    groups = one_ref.shape[0] // (count + 2)

    def every(left_ref, right_ref):
        spread(lambda row: outer_ref[0, row], left_ref, right_ref, stack_ref, 0, 0)

        def body(block, carry):
            spread(
                lambda row: own_ref[block * DILATION + row],
                left_ref, right_ref, stack_ref, block + 1, (block + 1) * groups,
            )
            return carry

        lax.fori_loop(0, count, body, 0)
        spread(lambda row: outer_ref[1, row], left_ref, right_ref, stack_ref, count + 1, (count + 1) * groups)

    either("col", every, one_ref, two_ref)


def forward_kernel(
    scale, own_ref, outer_ref, one_ref, two_ref, cotangent_ref, weight_ref, bias_ref,
    activation_ref, grad_ref, send_one_ref, send_two_ref, rims_ref, terms_ref, stack_ref, sum_ref, taps_ref,
):
    height, channels, width = own_ref.shape
    count = height // DILATION
    groups = rims_ref.shape[1] // count
    spread_all(own_ref, outer_ref, one_ref, two_ref, stack_ref)
    taps_ref[...] = jnp.zeros_like(taps_ref)
    sum_ref[...] = jnp.zeros_like(sum_ref)
    depth = 9 * channels

    def store(place, first, last):
        rims_ref[0, place] = first
        rims_ref[1, place] = last

    def body(block, carry):
        start = pl.multiple_of(block * DILATION, DILATION)
        stacked = stack_ref[pl.ds(block, 3)].reshape(depth, DILATION * width)
        preact = jnp.dot(weight_ref[...], stacked, preferred_element_type=jnp.float32)
        cotangent = jnp.swapaxes(cotangent_ref[:, pl.ds(start, DILATION), :], 0, 1)
        bias = jnp.broadcast_to(bias_ref[...], (channels, width))
        values, grads = [], []
        total = sum_ref[...]
        for row in range(DILATION):
            value, slope_val = gelu_pair(preact[:, row * width : (row + 1) * width] + bias)
            values.append(value.astype(jnp.bfloat16))
            grad = (cotangent[row].astype(jnp.float32) * slope_val).astype(jnp.bfloat16)
            grads.append(grad)
            total = total + grad.astype(jnp.float32)
            grad_ref[start + row] = grad
        sum_ref[...] = total
        activation_ref[:, pl.ds(start, DILATION), :] = jnp.swapaxes(jnp.stack(values), 0, 1)
        taps_ref[...] += lax.dot_general(
            stacked, jnp.concatenate(grads, axis=1), (((1,), (1,)), ((), ())),
            preferred_element_type=jnp.float32,
        )
        pack_rows(jnp.stack(grads), store, block * groups)
        return carry

    lax.fori_loop(0, count, body, 0)
    end = height - DILATION
    odd = lax.axis_index("row") % 2
    send_one_ref[...] = grad_ref[pl.ds((1 - odd) * end, DILATION)]
    send_two_ref[...] = grad_ref[pl.ds(odd * end, DILATION)]
    clear_if(alone("row", 0), send_one_ref)
    clear_if(alone("row", 1), send_two_ref)
    terms_ref[:, :depth] = jnp.transpose(taps_ref[...]) * scale
    sums = jnp.sum(sum_ref[...], axis=1, keepdims=True) * scale
    terms_ref[:, depth:] = jnp.broadcast_to(sums, (channels, terms_ref.shape[1] - depth))


def backward_kernel(
    own_ref, outer_ref, one_ref, two_ref, weight_ref, out_ref, token_ref, stack_ref
):
    height, channels, width = own_ref.shape
    token_ref[...] = jnp.zeros_like(token_ref)
    spread_all(own_ref, outer_ref, one_ref, two_ref, stack_ref)

    def body(block, carry):
        start = pl.multiple_of(block * DILATION, DILATION)
        stacked = stack_ref[pl.ds(block, 3)].reshape(9 * channels, DILATION * width)
        total = jnp.dot(weight_ref[...], stacked, preferred_element_type=jnp.float32).astype(jnp.bfloat16)
        rows = jnp.stack([total[:, row * width : (row + 1) * width] for row in range(DILATION)])
        out_ref[:, pl.ds(start, DILATION), :] = jnp.swapaxes(rows, 0, 1)
        return carry

    lax.fori_loop(0, height // DILATION, body, 0)


def finish_kernel(one_ref, other_ref, after_ref, weight_ref, bias_ref):
    total = one_ref[...] + other_ref[...]
    channels = total.shape[0]
    for tap in range(9):
        weight_ref[tap // 3, tap % 3] = total[:, tap * channels : (tap + 1) * channels]
    flipped = jnp.transpose(total[:, total.shape[1] - 128 :])
    bias_ref[...] = flipped[127:128, :channels]


def call(kernel, out_shapes, operands, scratch=(), flops=0):
    whole = pl.BlockSpec(memory_space=pltpu.VMEM)
    size = sum(math.prod(x.shape) * jnp.dtype(x.dtype).itemsize for x in (*operands, *out_shapes))
    return pl.pallas_call(
        kernel,
        out_shape=out_shapes,
        in_specs=[whole] * len(operands),
        out_specs=[whole] * len(out_shapes),
        scratch_shapes=list(scratch),
        compiler_params=pltpu.CompilerParams(vmem_limit_bytes=VMEM_BYTES),
        cost_estimate=pl.CostEstimate(flops=flops, bytes_accessed=size, transcendentals=0),
    )(*operands)


def shards(image, weight, bias, cotangent):
    channels, height, width = image.shape
    bf16, f32 = jnp.bfloat16, jnp.float32
    scale = 1.0 / math.sqrt(height * lax.axis_size("row") * width * lax.axis_size("col"))
    shape = jax.ShapeDtypeStruct
    pieces = width // DILATION
    own_groups, all_groups = height // pieces, (height + 2 * DILATION) // pieces
    depth = 9 * channels
    stack = pltpu.VMEM((height // DILATION + 2, 3 * channels, DILATION * width), bf16)
    edge = shape((DILATION, channels, width), bf16)
    packed = shape((all_groups, channels, width), bf16)
    own_rims = shape((2, own_groups, channels, width), bf16)
    rows = shape((height, channels, width), bf16)
    flops = 2 * depth * channels * height * width

    odd = lax.axis_index("row") % 2
    outer = shape((2, DILATION, channels, width), bf16)
    end = height - DILATION


    def image_rim(start, first):
        rim = lax.dynamic_slice_in_dim(image, start, DILATION, 1)
        flag = alone("row", first)
        return rim if flag is None else jnp.where(flag, jnp.zeros_like(rim), rim)

    one = swap_pairs(image_rim((1 - odd) * end, 0), "row", 0)
    two = swap_pairs(image_rim(odd * end, 1), "row", 1)
    image_rows, rims = call(own_kernel, (rows, own_rims), (image,))
    forward_weight = jnp.transpose(weight, (2, 0, 1, 3)).reshape(channels, depth)
    backward_weight = jnp.transpose(weight[::-1, ::-1], (3, 0, 1, 2)).reshape(channels, depth)
    one, two, image_outer = call(
        functools.partial(rim_kernel, True), (packed, packed, outer), (one, two, rims)
    )
    two, one = swap_pairs(two, "col", 1), swap_pairs(one, "col", 0)
    activation, grads, one, two, rims, terms = call(
        functools.partial(forward_kernel, scale),
        (
            shape(image.shape, bf16), rows, edge, edge, own_rims,
            shape((channels, -(-(depth + 1) // 128) * 128), f32),
        ),
        (image_rows, image_outer, one, two, cotangent, forward_weight, bias[:, None]),
        (stack, pltpu.VMEM((channels, width), f32), pltpu.VMEM((depth, channels), f32)),
        2 * flops,
    )
    one, two = swap_pairs(one, "row", 0), swap_pairs(two, "row", 1)
    one, two, grad_outer = call(
        functools.partial(rim_kernel, False), (packed, packed, outer), (one, two, rims)
    )
    two, one = swap_pairs(two, "col", 1), swap_pairs(one, "col", 0)
    grad_image, token = call(
        backward_kernel,
        (shape(image.shape, bf16), shape((8, 128), f32)),
        (grads, grad_outer, one, two, backward_weight),
        (stack,),
        flops,
    )
    one, other = add_pairs(terms, "col", "row")
    grad_weight, grad_bias = call(
        finish_kernel, (shape(weight.shape, f32), shape((1, channels), f32)), (one, other, token)
    )
    return (activation, grad_image, grad_weight, grad_bias.reshape(channels))


def solution(mesh):
    return jax.shard_map(
        shards,
        mesh=mesh,
        in_specs=(P(None, "row", "col"), P(), P(), P(None, "row", "col")),
        out_specs=(P(None, "row", "col"), P(None, "row", "col"), P(), P()),
        check_vma=False,
    )
```

```python
import functools
import math

import jax
import jax.numpy as jnp
from jax import lax
from jax.experimental import pallas as pl
from jax.experimental.pallas import tpu as pltpu
from jax.sharding import PartitionSpec as P

DILATION = 16
VMEM_BYTES = 16 * 2**20


def partners(axis, first):
    count = lax.axis_size(axis)
    to = list(range(count))
    for at in range(first, count - 1, 2):
        to[at], to[at + 1] = at + 1, at
    return list(enumerate(to))


def alone(axis, first):
    places = [at for at, other in partners(axis, first) if at == other]
    at = lax.axis_index(axis)
    return functools.reduce(jnp.logical_or, [at == place for place in places]) if places else None


def clear_if(flag, ref):
    if flag is not None:
        @pl.when(flag)
        def _():
            ref[...] = jnp.zeros_like(ref)


def swap_pairs(value, axis, first):
    other_axis = "col" if axis == "row" else "row"
    columns = lax.axis_size("col")

    def place(at, other):
        row, column = (at, other) if axis == "row" else (other, at)
        return row * columns + column

    pairs = []
    for at, to in partners(axis, first):
        for other, other_to in partners(other_axis, 0):
            pairs.append((place(at, other), place(to, other if to != at else other_to)))
    return lax.ppermute(value, ("row", "col"), pairs)


def rounds_of(axis):
    bits = [2**k for k in reversed(range(lax.axis_size(axis).bit_length() - 1))]
    return [(axis, bits[at : at + 2]) for at in range(0, len(bits), 2)]


def add_over(value, axis):
    other = jnp.zeros_like(value)
    for place, (axis, bits) in enumerate(rounds_of(axis)):
        value = value + other if place else value
        masks = bits[::-1] + [sum(bits)] if len(bits) == 2 else bits
        came = [
            lax.ppermute(value, axis, [(at, at ^ mask) for at in range(lax.axis_size(axis))]) for mask in masks
        ]
        if len(came) == 3:
            value, other = value + came[0], came[1] + came[2]
        else:
            other = came[0]
    return value, other


def gelu_pair(preact):
    coef = 0.7978845608
    square = preact * preact
    tval = jnp.tanh(coef * (preact + 0.044715 * (square * preact)))
    half = 0.5 * (1.0 + tval)
    slope_val = half + 0.5 * preact * (1.0 - tval * tval) * coef * (1.0 + 3.0 * 0.044715 * square)
    return (preact * half, slope_val)


def lane_of(shape):
    return lax.broadcasted_iota(jnp.int32, shape, len(shape) - 1)


def pack_group(rows):
    half = len(rows) // 2
    width = rows[0].shape[-1]
    lane = lane_of(rows[0].shape)
    pair = lane // (2 * DILATION)
    front = lane % (2 * DILATION) < DILATION

    def joined(part):
        total = pltpu.roll(part[0], DILATION, 1)
        for k in range(1, half):
            total = jnp.where(pair == k, pltpu.roll(part[k], DILATION + 2 * DILATION * k, 1), total)
        return total

    low, high = joined(rows[:half]), joined(rows[half:])
    first = jnp.where(front, pltpu.roll(low, width - DILATION, 1), high)
    last = jnp.where(front, low, pltpu.roll(high, DILATION, 1))
    return first, last


def unpack_group(from_left, from_right, count):
    half = count // 2
    width = from_left.shape[-1]
    front = lane_of(from_left.shape) % (2 * DILATION) < DILATION
    low = jnp.where(front, from_right, pltpu.roll(from_left, DILATION, 1))
    high = jnp.where(front, pltpu.roll(from_right, width - DILATION, 1), from_left)
    return [
        pltpu.roll(low if k < half else high, (width - DILATION - 2 * DILATION * (k % half)) % width, 1)
        for k in range(count)
    ]


def pack_rows(block, store, first_group):
    pieces = block.shape[-1] // DILATION
    for group in range(block.shape[0] // pieces):
        first, last = pack_group([block[group * pieces + k] for k in range(pieces)])
        store(first_group + group, first, last)


def own_kernel(image_ref, rows_ref, rims_ref):
    count = image_ref.shape[1] // DILATION
    groups = rims_ref.shape[1] // count

    def store(place, first, last):
        rims_ref[0, place] = first
        rims_ref[1, place] = last

    def body(block, carry):
        start = pl.multiple_of(block * DILATION, DILATION)
        rows = jnp.swapaxes(image_ref[:, pl.ds(start, DILATION), :], 0, 1)
        rows_ref[pl.ds(start, DILATION)] = rows
        pack_rows(rows, store, block * groups)
        return carry

    lax.fori_loop(0, count, body, 0)


def either(axis, body, one, two):
    odd = lax.axis_index(axis) % 2 == 1
    pl.when(odd)(lambda: body(one, two))
    pl.when(jnp.logical_not(odd))(lambda: body(two, one))


def rim_kernel(swap, one_ref, two_ref, rims_ref, send_one_ref, send_two_ref, outer_ref):
    own = rims_ref.shape[1]
    groups = (send_one_ref.shape[0] - own) // 2

    def order(upper_ref, lower_ref):
        for index, ref in enumerate((upper_ref, lower_ref)):
            outer_ref[index] = jnp.swapaxes(ref[...], 0, 1) if swap else ref[...]

    def pack(send_first_ref, send_last_ref):
        def store(place, first, last):
            send_first_ref[place] = first
            send_last_ref[place] = last

        send_first_ref[groups : groups + own] = rims_ref[0]
        send_last_ref[groups : groups + own] = rims_ref[1]
        for index in range(2):
            pack_rows(outer_ref[index], store, index * (groups + own))

    either("row", order, one_ref, two_ref)
    either("col", pack, send_one_ref, send_two_ref)
    clear_if(alone("col", 0), send_one_ref)
    clear_if(alone("col", 1), send_two_ref)


def rim_sum_kernel(one_ref, two_ref, rims_ref, value_ref, other_ref, send_one_ref, send_two_ref, outer_ref, sum_ref):
    sum_ref[...] = value_ref[...] + other_ref[...]
    rim_kernel(False, one_ref, two_ref, rims_ref, send_one_ref, send_two_ref, outer_ref)


def spread(rows_of, left_ref, right_ref, stack_ref, block, group_start):
    channels, width = left_ref.shape[1:]
    pieces = width // DILATION
    lane = lane_of((channels, width))
    for group in range(DILATION // pieces):
        rims = unpack_group(left_ref[group_start + group], right_ref[group_start + group], pieces)
        for k in range(pieces):
            row = group * pieces + k
            value = rows_of(row)
            columns = slice(row * width, (row + 1) * width)
            before = jnp.where(lane < DILATION, rims[k], pltpu.roll(value, DILATION, 1))
            after = jnp.where(lane >= width - DILATION, rims[k], pltpu.roll(value, width - DILATION, 1))
            stack_ref[block, 0:channels, columns] = before
            stack_ref[block, channels : 2 * channels, columns] = value
            stack_ref[block, 2 * channels : 3 * channels, columns] = after


def spread_all(own_ref, outer_ref, one_ref, two_ref, stack_ref):
    count = own_ref.shape[0] // DILATION
    groups = one_ref.shape[0] // (count + 2)

    def every(left_ref, right_ref):
        spread(lambda row: outer_ref[0, row], left_ref, right_ref, stack_ref, 0, 0)

        def body(block, carry):
            spread(
                lambda row: own_ref[block * DILATION + row],
                left_ref, right_ref, stack_ref, block + 1, (block + 1) * groups,
            )
            return carry

        lax.fori_loop(0, count, body, 0)
        spread(lambda row: outer_ref[1, row], left_ref, right_ref, stack_ref, count + 1, (count + 1) * groups)

    either("col", every, one_ref, two_ref)


def forward_kernel(
    scale, own_ref, outer_ref, one_ref, two_ref, cotangent_ref, weight_ref, bias_ref,
    activation_ref, grad_ref, send_one_ref, send_two_ref, rims_ref, terms_ref, stack_ref, sum_ref, taps_ref,
):
    height, channels, width = own_ref.shape
    count = height // DILATION
    groups = rims_ref.shape[1] // count
    spread_all(own_ref, outer_ref, one_ref, two_ref, stack_ref)
    taps_ref[...] = jnp.zeros_like(taps_ref)
    sum_ref[...] = jnp.zeros_like(sum_ref)
    depth = 9 * channels

    def store(place, first, last):
        rims_ref[0, place] = first
        rims_ref[1, place] = last

    def body(block, carry):
        start = pl.multiple_of(block * DILATION, DILATION)
        stacked = stack_ref[pl.ds(block, 3)].reshape(depth, DILATION * width)
        preact = jnp.dot(weight_ref[...], stacked, preferred_element_type=jnp.float32)
        cotangent = jnp.swapaxes(cotangent_ref[:, pl.ds(start, DILATION), :], 0, 1)
        bias = jnp.broadcast_to(bias_ref[...], (channels, width))
        values, grads = [], []
        total = sum_ref[...]
        for row in range(DILATION):
            value, slope_val = gelu_pair(preact[:, row * width : (row + 1) * width] + bias)
            values.append(value.astype(jnp.bfloat16))
            grad = (cotangent[row].astype(jnp.float32) * slope_val).astype(jnp.bfloat16)
            grads.append(grad)
            total = total + grad.astype(jnp.float32)
            grad_ref[start + row] = grad
        sum_ref[...] = total
        activation_ref[:, pl.ds(start, DILATION), :] = jnp.swapaxes(jnp.stack(values), 0, 1)
        taps_ref[...] += lax.dot_general(
            stacked, jnp.concatenate(grads, axis=1), (((1,), (1,)), ((), ())),
            preferred_element_type=jnp.float32,
        )
        pack_rows(jnp.stack(grads), store, block * groups)
        return carry

    lax.fori_loop(0, count, body, 0)
    end = height - DILATION
    odd = lax.axis_index("row") % 2
    send_one_ref[...] = grad_ref[pl.ds((1 - odd) * end, DILATION)]
    send_two_ref[...] = grad_ref[pl.ds(odd * end, DILATION)]
    clear_if(alone("row", 0), send_one_ref)
    clear_if(alone("row", 1), send_two_ref)
    terms_ref[:, :depth] = jnp.transpose(taps_ref[...]) * scale
    sums = jnp.sum(sum_ref[...], axis=1, keepdims=True) * scale
    terms_ref[:, depth:] = jnp.broadcast_to(sums, (channels, terms_ref.shape[1] - depth))


def backward_kernel(
    own_ref, outer_ref, one_ref, two_ref, weight_ref, out_ref, token_ref, stack_ref
):
    height, channels, width = own_ref.shape
    token_ref[...] = jnp.zeros_like(token_ref)
    spread_all(own_ref, outer_ref, one_ref, two_ref, stack_ref)

    def body(block, carry):
        start = pl.multiple_of(block * DILATION, DILATION)
        stacked = stack_ref[pl.ds(block, 3)].reshape(9 * channels, DILATION * width)
        total = jnp.dot(weight_ref[...], stacked, preferred_element_type=jnp.float32).astype(jnp.bfloat16)
        rows = jnp.stack([total[:, row * width : (row + 1) * width] for row in range(DILATION)])
        out_ref[:, pl.ds(start, DILATION), :] = jnp.swapaxes(rows, 0, 1)
        return carry

    lax.fori_loop(0, height // DILATION, body, 0)


def finish_kernel(one_ref, other_ref, after_ref, weight_ref, bias_ref):
    total = one_ref[...] + other_ref[...]
    channels = total.shape[0]
    for tap in range(9):
        weight_ref[tap // 3, tap % 3] = total[:, tap * channels : (tap + 1) * channels]
    flipped = jnp.transpose(total[:, total.shape[1] - 128 :])
    bias_ref[...] = flipped[127:128, :channels]


def call(kernel, out_shapes, operands, scratch=(), flops=0):
    whole = pl.BlockSpec(memory_space=pltpu.VMEM)
    size = sum(math.prod(x.shape) * jnp.dtype(x.dtype).itemsize for x in (*operands, *out_shapes))
    return pl.pallas_call(
        kernel,
        out_shape=out_shapes,
        in_specs=[whole] * len(operands),
        out_specs=[whole] * len(out_shapes),
        scratch_shapes=list(scratch),
        compiler_params=pltpu.CompilerParams(vmem_limit_bytes=VMEM_BYTES),
        cost_estimate=pl.CostEstimate(flops=flops, bytes_accessed=size, transcendentals=0),
    )(*operands)


def shards(image, weight, bias, cotangent):
    channels, height, width = image.shape
    bf16, f32 = jnp.bfloat16, jnp.float32
    scale = 1.0 / math.sqrt(height * lax.axis_size("row") * width * lax.axis_size("col"))
    shape = jax.ShapeDtypeStruct
    pieces = width // DILATION
    own_groups, all_groups = height // pieces, (height + 2 * DILATION) // pieces
    depth = 9 * channels
    stack = pltpu.VMEM((height // DILATION + 2, 3 * channels, DILATION * width), bf16)
    edge = shape((DILATION, channels, width), bf16)
    packed = shape((all_groups, channels, width), bf16)
    own_rims = shape((2, own_groups, channels, width), bf16)
    rows = shape((height, channels, width), bf16)
    flops = 2 * depth * channels * height * width

    odd = lax.axis_index("row") % 2
    outer = shape((2, DILATION, channels, width), bf16)
    end = height - DILATION


    def image_rim(start, first):
        rim = lax.dynamic_slice_in_dim(image, start, DILATION, 1)
        flag = alone("row", first)
        return rim if flag is None else jnp.where(flag, jnp.zeros_like(rim), rim)

    one = swap_pairs(image_rim((1 - odd) * end, 0), "row", 0)
    two = swap_pairs(image_rim(odd * end, 1), "row", 1)
    image_rows, rims = call(own_kernel, (rows, own_rims), (image,))
    forward_weight = jnp.transpose(weight, (2, 0, 1, 3)).reshape(channels, depth)
    backward_weight = jnp.transpose(weight[::-1, ::-1], (3, 0, 1, 2)).reshape(channels, depth)
    one, two, image_outer = call(
        functools.partial(rim_kernel, True), (packed, packed, outer), (one, two, rims)
    )
    two, one = swap_pairs(two, "col", 1), swap_pairs(one, "col", 0)
    activation, grads, one, two, rims, terms = call(
        functools.partial(forward_kernel, scale),
        (
            shape(image.shape, bf16), rows, edge, edge, own_rims,
            shape((channels, -(-(depth + 1) // 128) * 128), f32),
        ),
        (image_rows, image_outer, one, two, cotangent, forward_weight, bias[:, None]),
        (stack, pltpu.VMEM((channels, width), f32), pltpu.VMEM((depth, channels), f32)),
        2 * flops,
    )
    one, two = swap_pairs(one, "row", 0), swap_pairs(two, "row", 1)
    one, two, grad_outer, terms = call(
        rim_sum_kernel,
        (packed, packed, outer, shape(terms.shape, f32)),
        (one, two, rims, *add_over(terms, "col")),
    )
    two, one = swap_pairs(two, "col", 1), swap_pairs(one, "col", 0)
    grad_image, token = call(
        backward_kernel,
        (shape(image.shape, bf16), shape((8, 128), f32)),
        (grads, grad_outer, one, two, backward_weight),
        (stack,),
        flops,
    )
    one, other = add_over(terms, "row")
    grad_weight, grad_bias = call(
        finish_kernel, (shape(weight.shape, f32), shape((1, channels), f32)), (one, other, token)
    )
    return (activation, grad_image, grad_weight, grad_bias.reshape(channels))


def solution(mesh):
    return jax.shard_map(
        shards,
        mesh=mesh,
        in_specs=(P(None, "row", "col"), P(), P(), P(None, "row", "col")),
        out_specs=(P(None, "row", "col"), P(None, "row", "col"), P(), P()),
        check_vma=False,
    )
```

```python
import functools
import math

import jax
import jax.numpy as jnp
from jax import lax
from jax.experimental import pallas as pl
from jax.experimental.pallas import tpu as pltpu
from jax.sharding import PartitionSpec as P

DILATION = 16
VMEM_BYTES = 16 * 2**20


def partners(axis, first):
    count = lax.axis_size(axis)
    to = list(range(count))
    for at in range(first, count - 1, 2):
        to[at], to[at + 1] = at + 1, at
    return list(enumerate(to))


def alone(axis, first):
    places = [at for at, other in partners(axis, first) if at == other]
    at = lax.axis_index(axis)
    return functools.reduce(jnp.logical_or, [at == place for place in places]) if places else None


def clear_if(flag, ref):
    if flag is not None:
        @pl.when(flag)
        def _():
            ref[...] = jnp.zeros_like(ref)


def swap_pairs(value, axis, first):
    other_axis = "col" if axis == "row" else "row"
    columns = lax.axis_size("col")

    def place(at, other):
        row, column = (at, other) if axis == "row" else (other, at)
        return row * columns + column

    pairs = []
    for at, to in partners(axis, first):
        for other, other_to in partners(other_axis, 0):
            pairs.append((place(at, other), place(to, other if to != at else other_to)))
    return lax.ppermute(value, ("row", "col"), pairs)


def rounds_of(near_axis, far_axis):
    near = [2**k for k in range(lax.axis_size(near_axis).bit_length() - 1)]
    far = [2**k for k in reversed(range(lax.axis_size(far_axis).bit_length() - 1))]
    rounds = [(near_axis, [bit]) for bit in near]
    return rounds + [(far_axis, far[at : at + 2]) for at in range(0, len(far), 2)]


def add_pairs(value, near_axis, far_axis):
    other = jnp.zeros_like(value)
    for place, (axis, bits) in enumerate(rounds_of(near_axis, far_axis)):
        value = value + other if place else value
        masks = bits[::-1] + [sum(bits)] if len(bits) == 2 else bits
        came = [
            lax.ppermute(value, axis, [(at, at ^ mask) for at in range(lax.axis_size(axis))]) for mask in masks
        ]
        if len(came) == 3:
            value, other = value + came[0], came[1] + came[2]
        else:
            other = came[0]
    return value, other


def gelu_pair(preact):
    coef = 0.7978845608
    square = preact * preact
    tval = jnp.tanh(coef * (preact + 0.044715 * (square * preact)))
    half = 0.5 * (1.0 + tval)
    slope_val = half + 0.5 * preact * (1.0 - tval * tval) * coef * (1.0 + 3.0 * 0.044715 * square)
    return (preact * half, slope_val)


def lane_of(shape):
    return lax.broadcasted_iota(jnp.int32, shape, len(shape) - 1)


def pack_group(rows):
    half = len(rows) // 2
    width = rows[0].shape[-1]
    lane = lane_of(rows[0].shape)
    pair = lane // (2 * DILATION)
    front = lane % (2 * DILATION) < DILATION

    def joined(part):
        total = pltpu.roll(part[0], DILATION, 1)
        for k in range(1, half):
            total = jnp.where(pair == k, pltpu.roll(part[k], DILATION + 2 * DILATION * k, 1), total)
        return total

    low, high = joined(rows[:half]), joined(rows[half:])
    first = jnp.where(front, pltpu.roll(low, width - DILATION, 1), high)
    last = jnp.where(front, low, pltpu.roll(high, DILATION, 1))
    return first, last


def unpack_group(from_left, from_right, count):
    half = count // 2
    width = from_left.shape[-1]
    front = lane_of(from_left.shape) % (2 * DILATION) < DILATION
    low = jnp.where(front, from_right, pltpu.roll(from_left, DILATION, 1))
    high = jnp.where(front, pltpu.roll(from_right, width - DILATION, 1), from_left)
    return [
        pltpu.roll(low if k < half else high, (width - DILATION - 2 * DILATION * (k % half)) % width, 1)
        for k in range(count)
    ]


def pack_rows(block, store, first_group):
    pieces = block.shape[-1] // DILATION
    for group in range(block.shape[0] // pieces):
        first, last = pack_group([block[group * pieces + k] for k in range(pieces)])
        store(first_group + group, first, last)


def own_kernel(image_ref, rows_ref, rims_ref):
    count = image_ref.shape[1] // DILATION
    groups = rims_ref.shape[1] // count

    def store(place, first, last):
        rims_ref[0, place] = first
        rims_ref[1, place] = last

    def body(block, carry):
        start = pl.multiple_of(block * DILATION, DILATION)
        rows = jnp.swapaxes(image_ref[:, pl.ds(start, DILATION), :], 0, 1)
        rows_ref[pl.ds(start, DILATION)] = rows
        pack_rows(rows, store, block * groups)
        return carry

    lax.fori_loop(0, count, body, 0)


def either(axis, body, one, two):
    odd = lax.axis_index(axis) % 2 == 1
    pl.when(odd)(lambda: body(one, two))
    pl.when(jnp.logical_not(odd))(lambda: body(two, one))


def rim_kernel(swap, one_ref, two_ref, rims_ref, send_one_ref, send_two_ref, outer_ref):
    own = rims_ref.shape[1]
    groups = (send_one_ref.shape[0] - own) // 2

    def order(upper_ref, lower_ref):
        for index, ref in enumerate((upper_ref, lower_ref)):
            outer_ref[index] = jnp.swapaxes(ref[...], 0, 1) if swap else ref[...]

    def pack(send_first_ref, send_last_ref):
        def store(place, first, last):
            send_first_ref[place] = first
            send_last_ref[place] = last

        send_first_ref[groups : groups + own] = rims_ref[0]
        send_last_ref[groups : groups + own] = rims_ref[1]
        for index in range(2):
            pack_rows(outer_ref[index], store, index * (groups + own))

    either("row", order, one_ref, two_ref)
    either("col", pack, send_one_ref, send_two_ref)
    clear_if(alone("col", 0), send_one_ref)
    clear_if(alone("col", 1), send_two_ref)


def spread(rows_of, left_ref, right_ref, stack_ref, block, group_start):
    channels, width = left_ref.shape[1:]
    pieces = width // DILATION
    lane = lane_of((channels, width))
    for group in range(DILATION // pieces):
        rims = unpack_group(left_ref[group_start + group], right_ref[group_start + group], pieces)
        for k in range(pieces):
            row = group * pieces + k
            value = rows_of(row)
            columns = slice(row * width, (row + 1) * width)
            before = jnp.where(lane < DILATION, rims[k], pltpu.roll(value, DILATION, 1))
            after = jnp.where(lane >= width - DILATION, rims[k], pltpu.roll(value, width - DILATION, 1))
            stack_ref[block, 0:channels, columns] = before
            stack_ref[block, channels : 2 * channels, columns] = value
            stack_ref[block, 2 * channels : 3 * channels, columns] = after


def spread_all(own_ref, outer_ref, one_ref, two_ref, stack_ref):
    count = own_ref.shape[0] // DILATION
    groups = one_ref.shape[0] // (count + 2)

    def every(left_ref, right_ref):
        spread(lambda row: outer_ref[0, row], left_ref, right_ref, stack_ref, 0, 0)

        def body(block, carry):
            spread(
                lambda row: own_ref[block * DILATION + row],
                left_ref, right_ref, stack_ref, block + 1, (block + 1) * groups,
            )
            return carry

        lax.fori_loop(0, count, body, 0)
        spread(lambda row: outer_ref[1, row], left_ref, right_ref, stack_ref, count + 1, (count + 1) * groups)

    either("col", every, one_ref, two_ref)


def forward_kernel(
    scale, own_ref, outer_ref, one_ref, two_ref, cotangent_ref, weight_ref, bias_ref,
    activation_ref, grad_ref, send_one_ref, send_two_ref, rims_ref, terms_ref, stack_ref, sum_ref, taps_ref,
):
    height, channels, width = own_ref.shape
    count = height // DILATION
    groups = rims_ref.shape[1] // count
    spread_all(own_ref, outer_ref, one_ref, two_ref, stack_ref)
    taps_ref[...] = jnp.zeros_like(taps_ref)
    sum_ref[...] = jnp.zeros_like(sum_ref)
    depth = 9 * channels

    def store(place, first, last):
        rims_ref[0, place] = first
        rims_ref[1, place] = last

    def body(block, carry):
        start = pl.multiple_of(block * DILATION, DILATION)
        stacked = stack_ref[pl.ds(block, 3)].reshape(depth, DILATION * width)
        preact = jnp.dot(weight_ref[...], stacked, preferred_element_type=jnp.float32)
        cotangent = jnp.swapaxes(cotangent_ref[:, pl.ds(start, DILATION), :], 0, 1)
        bias = jnp.broadcast_to(bias_ref[...], (channels, width))
        values, grads = [], []
        total = sum_ref[...]
        for row in range(DILATION):
            value, slope_val = gelu_pair(preact[:, row * width : (row + 1) * width] + bias)
            values.append(value.astype(jnp.bfloat16))
            grad = (cotangent[row].astype(jnp.float32) * slope_val).astype(jnp.bfloat16)
            grads.append(grad)
            total = total + grad.astype(jnp.float32)
            grad_ref[start + row] = grad
        sum_ref[...] = total
        activation_ref[:, pl.ds(start, DILATION), :] = jnp.swapaxes(jnp.stack(values), 0, 1)
        taps_ref[...] += lax.dot_general(
            stacked, jnp.concatenate(grads, axis=1), (((1,), (1,)), ((), ())),
            preferred_element_type=jnp.float32,
        )
        pack_rows(jnp.stack(grads), store, block * groups)
        return carry

    lax.fori_loop(0, count, body, 0)
    end = height - DILATION
    odd = lax.axis_index("row") % 2
    send_one_ref[...] = grad_ref[pl.ds((1 - odd) * end, DILATION)]
    send_two_ref[...] = grad_ref[pl.ds(odd * end, DILATION)]
    clear_if(alone("row", 0), send_one_ref)
    clear_if(alone("row", 1), send_two_ref)
    terms_ref[:, :depth] = jnp.transpose(taps_ref[...]) * scale
    sums = jnp.sum(sum_ref[...], axis=1, keepdims=True) * scale
    terms_ref[:, depth:] = jnp.broadcast_to(sums, (channels, terms_ref.shape[1] - depth))


def backward_kernel(
    own_ref, outer_ref, one_ref, two_ref, weight_ref, out_ref, token_ref, stack_ref
):
    height, channels, width = own_ref.shape
    token_ref[...] = jnp.zeros_like(token_ref)
    spread_all(own_ref, outer_ref, one_ref, two_ref, stack_ref)

    def body(block, carry):
        start = pl.multiple_of(block * DILATION, DILATION)
        stacked = stack_ref[pl.ds(block, 3)].reshape(9 * channels, DILATION * width)
        total = jnp.dot(weight_ref[...], stacked, preferred_element_type=jnp.float32).astype(jnp.bfloat16)
        rows = jnp.stack([total[:, row * width : (row + 1) * width] for row in range(DILATION)])
        out_ref[:, pl.ds(start, DILATION), :] = jnp.swapaxes(rows, 0, 1)
        return carry

    lax.fori_loop(0, height // DILATION, body, 0)


def finish_kernel(one_ref, other_ref, after_ref, weight_ref, bias_ref):
    total = one_ref[...] + other_ref[...]
    channels = total.shape[0]
    for tap in range(9):
        weight_ref[tap // 3, tap % 3] = total[:, tap * channels : (tap + 1) * channels]
    flipped = jnp.transpose(total[:, total.shape[1] - 128 :])
    bias_ref[...] = flipped[127:128, :channels]


def call(kernel, out_shapes, operands, scratch=(), flops=0):
    whole = pl.BlockSpec(memory_space=pltpu.VMEM)
    size = sum(math.prod(x.shape) * jnp.dtype(x.dtype).itemsize for x in (*operands, *out_shapes))
    return pl.pallas_call(
        kernel,
        out_shape=out_shapes,
        in_specs=[whole] * len(operands),
        out_specs=[whole] * len(out_shapes),
        scratch_shapes=list(scratch),
        compiler_params=pltpu.CompilerParams(vmem_limit_bytes=VMEM_BYTES),
        cost_estimate=pl.CostEstimate(flops=flops, bytes_accessed=size, transcendentals=0),
    )(*operands)


def shards(image, weight, bias, cotangent):
    channels, height, width = image.shape
    bf16, f32 = jnp.bfloat16, jnp.float32
    scale = 1.0 / math.sqrt(height * lax.axis_size("row") * width * lax.axis_size("col"))
    shape = jax.ShapeDtypeStruct
    pieces = width // DILATION
    own_groups, all_groups = height // pieces, (height + 2 * DILATION) // pieces
    depth = 9 * channels
    stack = pltpu.VMEM((height // DILATION + 2, 3 * channels, DILATION * width), bf16)
    edge = shape((DILATION, channels, width), bf16)
    packed = shape((all_groups, channels, width), bf16)
    own_rims = shape((2, own_groups, channels, width), bf16)
    rows = shape((height, channels, width), bf16)
    flops = 2 * depth * channels * height * width

    odd = lax.axis_index("row") % 2
    outer = shape((2, DILATION, channels, width), bf16)
    end = height - DILATION


    def image_rim(start, first):
        rim = lax.dynamic_slice_in_dim(image, start, DILATION, 1)
        flag = alone("row", first)
        return rim if flag is None else jnp.where(flag, jnp.zeros_like(rim), rim)

    one = swap_pairs(image_rim((1 - odd) * end, 0), "row", 0)
    two = swap_pairs(image_rim(odd * end, 1), "row", 1)
    image_rows, rims = call(own_kernel, (rows, own_rims), (image,))
    forward_weight = jnp.transpose(weight, (2, 0, 1, 3)).reshape(channels, depth)
    backward_weight = jnp.transpose(weight[::-1, ::-1], (3, 0, 1, 2)).reshape(channels, depth)
    one, two, image_outer = call(
        functools.partial(rim_kernel, True), (packed, packed, outer), (one, two, rims)
    )
    two, one = swap_pairs(two, "col", 1), swap_pairs(one, "col", 0)
    activation, grads, one, two, rims, terms = call(
        functools.partial(forward_kernel, scale),
        (
            shape(image.shape, bf16), rows, edge, edge, own_rims,
            shape((channels, -(-(depth + 1) // 128) * 128), f32),
        ),
        (image_rows, image_outer, one, two, cotangent, forward_weight, bias[:, None]),
        (stack, pltpu.VMEM((channels, width), f32), pltpu.VMEM((depth, channels), f32)),
        2 * flops,
    )
    one, two = swap_pairs(one, "row", 0), swap_pairs(two, "row", 1)
    one, two, grad_outer = call(
        functools.partial(rim_kernel, False), (packed, packed, outer), (one, two, rims)
    )
    two, one = swap_pairs(two, "col", 1), swap_pairs(one, "col", 0)
    grad_image, token = call(
        backward_kernel,
        (shape(image.shape, bf16), shape((8, 128), f32)),
        (grads, grad_outer, one, two, backward_weight),
        (stack,),
        flops,
    )
    one, other = add_pairs(terms, "col", "row")
    grad_weight, grad_bias = call(
        finish_kernel, (shape(weight.shape, f32), shape((1, channels), f32)), (one, other, token)
    )
    return (activation, grad_image, grad_weight, grad_bias.reshape(channels))


def solution(mesh):
    return jax.shard_map(
        shards,
        mesh=mesh,
        in_specs=(P(None, "row", "col"), P(), P(), P(None, "row", "col")),
        out_specs=(P(None, "row", "col"), P(None, "row", "col"), P(), P()),
        check_vma=False,
    )
```

```python
import functools
import math

import jax
import jax.numpy as jnp
from jax import lax
from jax.experimental import pallas as pl
from jax.experimental.pallas import tpu as pltpu
from jax.sharding import PartitionSpec as P

DILATION = 16
VMEM_BYTES = 16 * 2**20


def partners(axis, first):
    count = lax.axis_size(axis)
    to = list(range(count))
    for at in range(first, count - 1, 2):
        to[at], to[at + 1] = at + 1, at
    return list(enumerate(to))


def alone(axis, first):
    places = [at for at, other in partners(axis, first) if at == other]
    at = lax.axis_index(axis)
    return functools.reduce(jnp.logical_or, [at == place for place in places]) if places else None


def clear_if(flag, ref):
    if flag is not None:
        @pl.when(flag)
        def _():
            ref[...] = jnp.zeros_like(ref)


def swap_pairs(value, axis, first):
    other_axis = "col" if axis == "row" else "row"
    columns = lax.axis_size("col")

    def place(at, other):
        row, column = (at, other) if axis == "row" else (other, at)
        return row * columns + column

    pairs = []
    for at, to in partners(axis, first):
        for other, other_to in partners(other_axis, 0):
            pairs.append((place(at, other), place(to, other if to != at else other_to)))
    return lax.ppermute(value, ("row", "col"), pairs)


def rounds_of(axis):
    bits = [2**k for k in reversed(range(lax.axis_size(axis).bit_length() - 1))]
    return [(axis, bits[at : at + 2]) for at in range(0, len(bits), 2)]


def add_pairs(value, near_axis, far_axis):
    other = jnp.zeros_like(value)
    for place, (axis, bits) in enumerate(rounds_of(near_axis) + rounds_of(far_axis)):
        value = value + other if place else value
        masks = bits[::-1] + [sum(bits)] if len(bits) == 2 else bits
        came = [
            lax.ppermute(value, axis, [(at, at ^ mask) for at in range(lax.axis_size(axis))]) for mask in masks
        ]
        if len(came) == 3:
            value, other = value + came[0], came[1] + came[2]
        else:
            other = came[0]
    return value, other


def gelu_pair(preact):
    coef, cubic = 0.7978845608, 0.7978845608 * 0.044715
    square = preact * preact
    half = 0.5 + 0.5 * jnp.tanh(preact * (coef + cubic * square))
    slope_val = half * (1.0 + (1.0 - half) * (preact * (2.0 * coef + 6.0 * cubic * square)))
    return (preact * half, slope_val)


def lane_of(shape):
    return lax.broadcasted_iota(jnp.int32, shape, len(shape) - 1)


def pack_group(rows):
    half = len(rows) // 2
    width = rows[0].shape[-1]
    lane = lane_of(rows[0].shape)
    pair = lane // (2 * DILATION)
    front = lane % (2 * DILATION) < DILATION

    def joined(part):
        total = pltpu.roll(part[0], DILATION, 1)
        for k in range(1, half):
            total = jnp.where(pair == k, pltpu.roll(part[k], DILATION + 2 * DILATION * k, 1), total)
        return total

    low, high = joined(rows[:half]), joined(rows[half:])
    first = jnp.where(front, pltpu.roll(low, width - DILATION, 1), high)
    last = jnp.where(front, low, pltpu.roll(high, DILATION, 1))
    return first, last


def unpack_group(from_left, from_right, count):
    half = count // 2
    width = from_left.shape[-1]
    front = lane_of(from_left.shape) % (2 * DILATION) < DILATION
    low = jnp.where(front, from_right, pltpu.roll(from_left, DILATION, 1))
    high = jnp.where(front, pltpu.roll(from_right, width - DILATION, 1), from_left)
    return [
        pltpu.roll(low if k < half else high, (width - DILATION - 2 * DILATION * (k % half)) % width, 1)
        for k in range(count)
    ]


def pack_rows(block, store, first_group):
    pieces = block.shape[-1] // DILATION
    for group in range(block.shape[0] // pieces):
        first, last = pack_group([block[group * pieces + k] for k in range(pieces)])
        store(first_group + group, first, last)


def rolled(rows):
    axis, width = rows.ndim - 1, rows.shape[-1]
    return pltpu.roll(rows, DILATION, axis), rows, pltpu.roll(rows, width - DILATION, axis)


def own_kernel(image_ref, cotangent_ref, rows_ref, cotangent_rows_ref, rims_ref):
    count = image_ref.shape[1] // DILATION
    groups = rims_ref.shape[1] // count

    def store(place, first, last):
        rims_ref[0, place] = first
        rims_ref[1, place] = last

    def body(block, carry):
        start = pl.multiple_of(block * DILATION, DILATION)
        rows = jnp.swapaxes(image_ref[:, pl.ds(start, DILATION), :], 0, 1)
        for index, moved in enumerate(rolled(rows)):
            rows_ref[index, pl.ds(start, DILATION)] = moved
        cotangent_rows_ref[pl.ds(start, DILATION)] = jnp.swapaxes(
            cotangent_ref[:, pl.ds(start, DILATION), :], 0, 1
        )
        pack_rows(rows, store, block * groups)
        return carry

    lax.fori_loop(0, count, body, 0)


def either(axis, body, one, two):
    odd = lax.axis_index(axis) % 2 == 1
    pl.when(odd)(lambda: body(one, two))
    pl.when(jnp.logical_not(odd))(lambda: body(two, one))


def rim_kernel(swap, one_ref, two_ref, rims_ref, send_one_ref, send_two_ref, outer_ref):
    own = rims_ref.shape[1]
    groups = (send_one_ref.shape[0] - own) // 2

    def order(upper_ref, lower_ref):
        for index, ref in enumerate((upper_ref, lower_ref)):
            outer_ref[index] = jnp.swapaxes(ref[...], 0, 1) if swap else ref[...]

    def pack(send_first_ref, send_last_ref):
        def store(place, first, last):
            send_first_ref[place] = first
            send_last_ref[place] = last

        send_first_ref[groups : groups + own] = rims_ref[0]
        send_last_ref[groups : groups + own] = rims_ref[1]
        for index in range(2):
            pack_rows(outer_ref[index], store, index * (groups + own))

    either("row", order, one_ref, two_ref)
    either("col", pack, send_one_ref, send_two_ref)
    clear_if(alone("col", 0), send_one_ref)
    clear_if(alone("col", 1), send_two_ref)


def spread(rows_of, left_ref, right_ref, stack_ref, block, group_start):
    channels, width = left_ref.shape[1:]
    pieces = width // DILATION
    lane = lane_of((channels, width))
    for group in range(DILATION // pieces):
        rims = unpack_group(left_ref[group_start + group], right_ref[group_start + group], pieces)
        for k in range(pieces):
            row = group * pieces + k
            before, value, after = rows_of(row)
            columns = slice(row * width, (row + 1) * width)
            before = jnp.where(lane < DILATION, rims[k], before)
            after = jnp.where(lane >= width - DILATION, rims[k], after)
            stack_ref[block, 0:channels, columns] = before
            stack_ref[block, channels : 2 * channels, columns] = value
            stack_ref[block, 2 * channels : 3 * channels, columns] = after


def spread_all(own_of, outer_ref, one_ref, two_ref, stack_ref):
    count = stack_ref.shape[0] - 2
    groups = one_ref.shape[0] // (count + 2)

    def every(left_ref, right_ref):
        spread(lambda row: rolled(outer_ref[0, row]), left_ref, right_ref, stack_ref, 0, 0)

        def body(block, carry):
            spread(
                lambda row: own_of(block * DILATION + row),
                left_ref, right_ref, stack_ref, block + 1, (block + 1) * groups,
            )
            return carry

        lax.fori_loop(0, count, body, 0)
        spread(lambda row: rolled(outer_ref[1, row]), left_ref, right_ref, stack_ref, count + 1, (count + 1) * groups)

    either("col", every, one_ref, two_ref)


def forward_kernel(
    scale, own_ref, outer_ref, one_ref, two_ref, cotangent_ref, weight_ref, bias_ref,
    activation_ref, grad_ref, send_one_ref, send_two_ref, rims_ref, terms_ref, stack_ref, sum_ref, taps_ref,
):
    height, channels, width = own_ref.shape[1:]
    count = height // DILATION
    groups = rims_ref.shape[1] // count
    spread_all(lambda at: [own_ref[k, at] for k in range(3)], outer_ref, one_ref, two_ref, stack_ref)
    taps_ref[...] = jnp.zeros_like(taps_ref)
    sum_ref[...] = jnp.zeros_like(sum_ref)
    depth = 9 * channels

    def store(place, first, last):
        rims_ref[0, place] = first
        rims_ref[1, place] = last

    def body(block, carry):
        start = pl.multiple_of(block * DILATION, DILATION)
        stacked = stack_ref[pl.ds(block, 3)].reshape(depth, DILATION * width)
        preact = jnp.dot(weight_ref[...], stacked, preferred_element_type=jnp.float32)
        bias = jnp.broadcast_to(bias_ref[...], (channels, width))
        values, grads = [], []
        total = sum_ref[...]
        for row in range(DILATION):
            value, slope_val = gelu_pair(preact[:, row * width : (row + 1) * width] + bias)
            values.append(value.astype(jnp.bfloat16))
            grad = (cotangent_ref[start + row].astype(jnp.float32) * slope_val).astype(jnp.bfloat16)
            grads.append(grad)
            total = total + grad.astype(jnp.float32)
            grad_ref[start + row] = grad
        sum_ref[...] = total
        activation_ref[:, pl.ds(start, DILATION), :] = jnp.swapaxes(jnp.stack(values), 0, 1)
        taps_ref[...] += lax.dot_general(
            stacked, jnp.concatenate(grads, axis=1), (((1,), (1,)), ((), ())),
            preferred_element_type=jnp.float32,
        )
        pack_rows(jnp.stack(grads), store, block * groups)
        return carry

    lax.fori_loop(0, count, body, 0)
    end = height - DILATION
    odd = lax.axis_index("row") % 2
    send_one_ref[...] = grad_ref[pl.ds((1 - odd) * end, DILATION)]
    send_two_ref[...] = grad_ref[pl.ds(odd * end, DILATION)]
    clear_if(alone("row", 0), send_one_ref)
    clear_if(alone("row", 1), send_two_ref)
    terms_ref[:, :depth] = jnp.transpose(taps_ref[...]) * scale
    sums = jnp.sum(sum_ref[...], axis=1, keepdims=True) * scale
    terms_ref[:, depth:] = jnp.broadcast_to(sums, (channels, terms_ref.shape[1] - depth))


def backward_kernel(
    own_ref, outer_ref, one_ref, two_ref, weight_ref, out_ref, token_ref, stack_ref
):
    height, channels, width = own_ref.shape
    token_ref[...] = jnp.zeros_like(token_ref)
    spread_all(lambda at: rolled(own_ref[at]), outer_ref, one_ref, two_ref, stack_ref)

    def body(block, carry):
        start = pl.multiple_of(block * DILATION, DILATION)
        stacked = stack_ref[pl.ds(block, 3)].reshape(9 * channels, DILATION * width)
        total = jnp.dot(weight_ref[...], stacked, preferred_element_type=jnp.float32).astype(jnp.bfloat16)
        rows = jnp.stack([total[:, row * width : (row + 1) * width] for row in range(DILATION)])
        out_ref[:, pl.ds(start, DILATION), :] = jnp.swapaxes(rows, 0, 1)
        return carry

    lax.fori_loop(0, height // DILATION, body, 0)


def finish_kernel(one_ref, other_ref, after_ref, weight_ref, bias_ref):
    total = one_ref[...] + other_ref[...]
    channels = total.shape[0]
    for tap in range(9):
        weight_ref[tap // 3, tap % 3] = total[:, tap * channels : (tap + 1) * channels]
    flipped = jnp.transpose(total[:, total.shape[1] - 128 :])
    bias_ref[...] = flipped[127:128, :channels]


def call(kernel, out_shapes, operands, scratch=(), flops=0):
    whole = pl.BlockSpec(memory_space=pltpu.VMEM)
    size = sum(math.prod(x.shape) * jnp.dtype(x.dtype).itemsize for x in (*operands, *out_shapes))
    return pl.pallas_call(
        kernel,
        out_shape=out_shapes,
        in_specs=[whole] * len(operands),
        out_specs=[whole] * len(out_shapes),
        scratch_shapes=list(scratch),
        compiler_params=pltpu.CompilerParams(vmem_limit_bytes=VMEM_BYTES),
        cost_estimate=pl.CostEstimate(flops=flops, bytes_accessed=size, transcendentals=0),
    )(*operands)


def shards(image, weight, bias, cotangent):
    channels, height, width = image.shape
    bf16, f32 = jnp.bfloat16, jnp.float32
    scale = 1.0 / math.sqrt(height * lax.axis_size("row") * width * lax.axis_size("col"))
    shape = jax.ShapeDtypeStruct
    pieces = width // DILATION
    own_groups, all_groups = height // pieces, (height + 2 * DILATION) // pieces
    depth = 9 * channels
    stack = pltpu.VMEM((height // DILATION + 2, 3 * channels, DILATION * width), bf16)
    edge = shape((DILATION, channels, width), bf16)
    packed = shape((all_groups, channels, width), bf16)
    own_rims = shape((2, own_groups, channels, width), bf16)
    rows = shape((height, channels, width), bf16)
    flops = 2 * depth * channels * height * width

    odd = lax.axis_index("row") % 2
    outer = shape((2, DILATION, channels, width), bf16)
    end = height - DILATION


    def image_rim(start, first):
        rim = lax.dynamic_slice_in_dim(image, start, DILATION, 1)
        flag = alone("row", first)
        return rim if flag is None else jnp.where(flag, jnp.zeros_like(rim), rim)

    one = swap_pairs(image_rim((1 - odd) * end, 0), "row", 0)
    two = swap_pairs(image_rim(odd * end, 1), "row", 1)
    image_rows, cotangent_rows, rims = call(
        own_kernel, (shape((3, *rows.shape), bf16), rows, own_rims), (image, cotangent)
    )
    forward_weight = jnp.transpose(weight, (2, 0, 1, 3)).reshape(channels, depth)
    backward_weight = jnp.transpose(weight[::-1, ::-1], (3, 0, 1, 2)).reshape(channels, depth)
    one, two, image_outer = call(
        functools.partial(rim_kernel, True), (packed, packed, outer), (one, two, rims)
    )
    two, one = swap_pairs(two, "col", 1), swap_pairs(one, "col", 0)
    activation, grads, one, two, rims, terms = call(
        functools.partial(forward_kernel, scale),
        (
            shape(image.shape, bf16), rows, edge, edge, own_rims,
            shape((channels, -(-(depth + 1) // 128) * 128), f32),
        ),
        (image_rows, image_outer, one, two, cotangent_rows, forward_weight, bias[:, None]),
        (stack, pltpu.VMEM((channels, width), f32), pltpu.VMEM((depth, channels), f32)),
        2 * flops,
    )
    one, two = swap_pairs(one, "row", 0), swap_pairs(two, "row", 1)
    one, two, grad_outer = call(
        functools.partial(rim_kernel, False), (packed, packed, outer), (one, two, rims)
    )
    two, one = swap_pairs(two, "col", 1), swap_pairs(one, "col", 0)
    grad_image, token = call(
        backward_kernel,
        (shape(image.shape, bf16), shape((8, 128), f32)),
        (grads, grad_outer, one, two, backward_weight),
        (stack,),
        flops,
    )
    one, other = add_pairs(terms, "col", "row")
    grad_weight, grad_bias = call(
        finish_kernel, (shape(weight.shape, f32), shape((1, channels), f32)), (one, other, token)
    )
    return (activation, grad_image, grad_weight, grad_bias.reshape(channels))


def solution(mesh):
    return jax.shard_map(
        shards,
        mesh=mesh,
        in_specs=(P(None, "row", "col"), P(), P(), P(None, "row", "col")),
        out_specs=(P(None, "row", "col"), P(None, "row", "col"), P(), P()),
        check_vma=False,
    )
```

```python
import functools
import math

import jax
import jax.numpy as jnp
from jax import lax
from jax.experimental import pallas as pl
from jax.experimental.pallas import tpu as pltpu
from jax.sharding import PartitionSpec as P

DILATION = 16
VMEM_BYTES = 16 * 2**20


def partners(axis, first):
    count = lax.axis_size(axis)
    to = list(range(count))
    for at in range(first, count - 1, 2):
        to[at], to[at + 1] = at + 1, at
    return list(enumerate(to))


def alone(axis, first):
    places = [at for at, other in partners(axis, first) if at == other]
    at = lax.axis_index(axis)
    return functools.reduce(jnp.logical_or, [at == place for place in places]) if places else None


def clear_if(flag, ref):
    if flag is not None:
        @pl.when(flag)
        def _():
            ref[...] = jnp.zeros_like(ref)


def swap_pairs(value, axis, first):
    other_axis = "col" if axis == "row" else "row"
    columns = lax.axis_size("col")

    def place(at, other):
        row, column = (at, other) if axis == "row" else (other, at)
        return row * columns + column

    pairs = []
    for at, to in partners(axis, first):
        for other, other_to in partners(other_axis, 0):
            pairs.append((place(at, other), place(to, other if to != at else other_to)))
    return lax.ppermute(value, ("row", "col"), pairs)


def rounds_of(axis):
    bits = [2**k for k in reversed(range(lax.axis_size(axis).bit_length() - 1))]
    return [(axis, bits[at : at + 2]) for at in range(0, len(bits), 2)]


def add_pairs(value, near_axis, far_axis):
    other = jnp.zeros_like(value)
    for place, (axis, bits) in enumerate(rounds_of(near_axis) + rounds_of(far_axis)):
        value = value + other if place else value
        masks = bits[::-1] + [sum(bits)] if len(bits) == 2 else bits
        came = [
            lax.ppermute(value, axis, [(at, at ^ mask) for at in range(lax.axis_size(axis))]) for mask in masks
        ]
        if len(came) == 3:
            value, other = value + came[0], came[1] + came[2]
        else:
            other = came[0]
    return value, other


def gelu_pair(preact):
    coef, cubic = 0.7978845608, 0.7978845608 * 0.044715
    square = preact * preact
    half = 0.5 + 0.5 * jnp.tanh(preact * (coef + cubic * square))
    slope_val = half * (1.0 + (1.0 - half) * (preact * (2.0 * coef + 6.0 * cubic * square)))
    return (preact * half, slope_val)


def lane_of(shape):
    return lax.broadcasted_iota(jnp.int32, shape, len(shape) - 1)


def pack_group(rows):
    half = len(rows) // 2
    width = rows[0].shape[-1]
    lane = lane_of(rows[0].shape)
    pair = lane // (2 * DILATION)
    front = lane % (2 * DILATION) < DILATION

    def joined(part):
        total = pltpu.roll(part[0], DILATION, 1)
        for k in range(1, half):
            total = jnp.where(pair == k, pltpu.roll(part[k], DILATION + 2 * DILATION * k, 1), total)
        return total

    low, high = joined(rows[:half]), joined(rows[half:])
    first = jnp.where(front, pltpu.roll(low, width - DILATION, 1), high)
    last = jnp.where(front, low, pltpu.roll(high, DILATION, 1))
    return first, last


def unpack_group(from_left, from_right, count):
    half = count // 2
    width = from_left.shape[-1]
    front = lane_of(from_left.shape) % (2 * DILATION) < DILATION
    low = jnp.where(front, from_right, pltpu.roll(from_left, DILATION, 1))
    high = jnp.where(front, pltpu.roll(from_right, width - DILATION, 1), from_left)
    return [
        pltpu.roll(low if k < half else high, (width - DILATION - 2 * DILATION * (k % half)) % width, 1)
        for k in range(count)
    ]


def pack_rows(block, store, first_group):
    pieces = block.shape[-1] // DILATION
    for group in range(block.shape[0] // pieces):
        first, last = pack_group([block[group * pieces + k] for k in range(pieces)])
        store(first_group + group, first, last)


def rolled(rows):
    axis, width = rows.ndim - 1, rows.shape[-1]
    return pltpu.roll(rows, DILATION, axis), rows, pltpu.roll(rows, width - DILATION, axis)


def own_kernel(image_ref, cotangent_ref, rows_ref, cotangent_rows_ref, rims_ref):
    count = image_ref.shape[1] // DILATION
    groups = rims_ref.shape[1] // count

    def store(place, first, last):
        rims_ref[0, place] = first
        rims_ref[1, place] = last

    def body(block, carry):
        start = pl.multiple_of(block * DILATION, DILATION)
        rows = jnp.swapaxes(image_ref[:, pl.ds(start, DILATION), :], 0, 1)
        for index, moved in enumerate(rolled(rows)):
            rows_ref[index, pl.ds(start, DILATION)] = moved
        cotangent_rows_ref[pl.ds(start, DILATION)] = jnp.swapaxes(
            cotangent_ref[:, pl.ds(start, DILATION), :], 0, 1
        )
        pack_rows(rows, store, block * groups)
        return carry

    lax.fori_loop(0, count, body, 0)


def either(axis, body, one, two):
    odd = lax.axis_index(axis) % 2 == 1
    pl.when(odd)(lambda: body(one, two))
    pl.when(jnp.logical_not(odd))(lambda: body(two, one))


def rim_kernel(swap, one_ref, two_ref, rims_ref, send_one_ref, send_two_ref, outer_ref):
    own = rims_ref.shape[1]
    groups = (send_one_ref.shape[0] - own) // 2

    def order(upper_ref, lower_ref):
        for index, ref in enumerate((upper_ref, lower_ref)):
            outer_ref[index] = jnp.swapaxes(ref[...], 0, 1) if swap else ref[...]

    def pack(send_first_ref, send_last_ref):
        def store(place, first, last):
            send_first_ref[place] = first
            send_last_ref[place] = last

        send_first_ref[groups : groups + own] = rims_ref[0]
        send_last_ref[groups : groups + own] = rims_ref[1]
        for index in range(2):
            pack_rows(outer_ref[index], store, index * (groups + own))

    either("row", order, one_ref, two_ref)
    either("col", pack, send_one_ref, send_two_ref)
    clear_if(alone("col", 0), send_one_ref)
    clear_if(alone("col", 1), send_two_ref)


def spread(rows_of, left_ref, right_ref, stack_ref, block, group_start):
    channels, width = left_ref.shape[1:]
    pieces = width // DILATION
    lane = lane_of((channels, width))
    for group in range(DILATION // pieces):
        rims = unpack_group(left_ref[group_start + group], right_ref[group_start + group], pieces)
        for k in range(pieces):
            row = group * pieces + k
            before, value, after = rows_of(row)
            columns = slice(row * width, (row + 1) * width)
            before = jnp.where(lane < DILATION, rims[k], before)
            after = jnp.where(lane >= width - DILATION, rims[k], after)
            stack_ref[block, 0:channels, columns] = before
            stack_ref[block, channels : 2 * channels, columns] = value
            stack_ref[block, 2 * channels : 3 * channels, columns] = after


def spread_all(own_of, outer_ref, one_ref, two_ref, stack_ref):
    count = stack_ref.shape[0] - 2
    groups = one_ref.shape[0] // (count + 2)

    def every(left_ref, right_ref):
        spread(lambda row: rolled(outer_ref[0, row]), left_ref, right_ref, stack_ref, 0, 0)

        def body(block, carry):
            spread(
                lambda row: own_of(block * DILATION + row),
                left_ref, right_ref, stack_ref, block + 1, (block + 1) * groups,
            )
            return carry

        lax.fori_loop(0, count, body, 0)
        spread(lambda row: rolled(outer_ref[1, row]), left_ref, right_ref, stack_ref, count + 1, (count + 1) * groups)

    either("col", every, one_ref, two_ref)


def push_block(weight_ref, stack_ref, parts_ref, block):
    parts_ref[lax.rem(block, 3)] = jnp.dot(
        weight_ref[...], stack_ref[block], preferred_element_type=jnp.float32
    )


def pull_row(parts_ref, block, row, channels, width):
    columns = slice(row * width, (row + 1) * width)
    upper, middle, lower = (
        parts_ref[lax.rem(block + tap, 3), tap * channels : (tap + 1) * channels, columns] for tap in range(3)
    )
    return upper + middle + lower


def forward_kernel(
    scale, own_ref, outer_ref, one_ref, two_ref, cotangent_ref, weight_ref, bias_ref,
    activation_ref, grad_ref, send_one_ref, send_two_ref, rims_ref, terms_ref, stack_ref, sum_ref, taps_ref, parts_ref,
):
    height, channels, width = own_ref.shape[1:]
    count = height // DILATION
    groups = rims_ref.shape[1] // count
    spread_all(lambda at: [own_ref[k, at] for k in range(3)], outer_ref, one_ref, two_ref, stack_ref)
    taps_ref[...] = jnp.zeros_like(taps_ref)
    push_block(weight_ref, stack_ref, parts_ref, 0)
    push_block(weight_ref, stack_ref, parts_ref, 1)
    sum_ref[...] = jnp.zeros_like(sum_ref)
    depth = 9 * channels

    def store(place, first, last):
        rims_ref[0, place] = first
        rims_ref[1, place] = last

    def body(block, carry):
        start = pl.multiple_of(block * DILATION, DILATION)
        stacked = stack_ref[pl.ds(block, 3)].reshape(depth, DILATION * width)
        push_block(weight_ref, stack_ref, parts_ref, block + 2)
        bias = jnp.broadcast_to(bias_ref[...], (channels, width))
        values, grads = [], []
        total = sum_ref[...]
        for row in range(DILATION):
            value, slope_val = gelu_pair(pull_row(parts_ref, block, row, channels, width) + bias)
            values.append(value.astype(jnp.bfloat16))
            grad = (cotangent_ref[start + row].astype(jnp.float32) * slope_val).astype(jnp.bfloat16)
            grads.append(grad)
            total = total + grad.astype(jnp.float32)
            grad_ref[start + row] = grad
        sum_ref[...] = total
        activation_ref[:, pl.ds(start, DILATION), :] = jnp.swapaxes(jnp.stack(values), 0, 1)
        taps_ref[...] += lax.dot_general(
            stacked, jnp.concatenate(grads, axis=1), (((1,), (1,)), ((), ())),
            preferred_element_type=jnp.float32,
        )
        pack_rows(jnp.stack(grads), store, block * groups)
        return carry

    lax.fori_loop(0, count, body, 0)
    end = height - DILATION
    odd = lax.axis_index("row") % 2
    send_one_ref[...] = grad_ref[pl.ds((1 - odd) * end, DILATION)]
    send_two_ref[...] = grad_ref[pl.ds(odd * end, DILATION)]
    clear_if(alone("row", 0), send_one_ref)
    clear_if(alone("row", 1), send_two_ref)
    terms_ref[:, :depth] = jnp.transpose(taps_ref[...]) * scale
    sums = jnp.sum(sum_ref[...], axis=1, keepdims=True) * scale
    terms_ref[:, depth:] = jnp.broadcast_to(sums, (channels, terms_ref.shape[1] - depth))


def backward_kernel(
    own_ref, outer_ref, one_ref, two_ref, weight_ref, out_ref, token_ref, stack_ref, parts_ref
):
    height, channels, width = own_ref.shape
    token_ref[...] = jnp.zeros_like(token_ref)
    spread_all(lambda at: rolled(own_ref[at]), outer_ref, one_ref, two_ref, stack_ref)
    push_block(weight_ref, stack_ref, parts_ref, 0)
    push_block(weight_ref, stack_ref, parts_ref, 1)

    def body(block, carry):
        start = pl.multiple_of(block * DILATION, DILATION)
        push_block(weight_ref, stack_ref, parts_ref, block + 2)
        rows = [
            pull_row(parts_ref, block, row, channels, width).astype(jnp.bfloat16) for row in range(DILATION)
        ]
        out_ref[:, pl.ds(start, DILATION), :] = jnp.swapaxes(jnp.stack(rows), 0, 1)
        return carry

    lax.fori_loop(0, height // DILATION, body, 0)


def finish_kernel(one_ref, other_ref, after_ref, weight_ref, bias_ref):
    total = one_ref[...] + other_ref[...]
    channels = total.shape[0]
    for tap in range(9):
        weight_ref[tap // 3, tap % 3] = total[:, tap * channels : (tap + 1) * channels]
    flipped = jnp.transpose(total[:, total.shape[1] - 128 :])
    bias_ref[...] = flipped[127:128, :channels]


def call(kernel, out_shapes, operands, scratch=(), flops=0):
    whole = pl.BlockSpec(memory_space=pltpu.VMEM)
    size = sum(math.prod(x.shape) * jnp.dtype(x.dtype).itemsize for x in (*operands, *out_shapes))
    return pl.pallas_call(
        kernel,
        out_shape=out_shapes,
        in_specs=[whole] * len(operands),
        out_specs=[whole] * len(out_shapes),
        scratch_shapes=list(scratch),
        compiler_params=pltpu.CompilerParams(vmem_limit_bytes=VMEM_BYTES),
        cost_estimate=pl.CostEstimate(flops=flops, bytes_accessed=size, transcendentals=0),
    )(*operands)


def shards(image, weight, bias, cotangent):
    channels, height, width = image.shape
    bf16, f32 = jnp.bfloat16, jnp.float32
    scale = 1.0 / math.sqrt(height * lax.axis_size("row") * width * lax.axis_size("col"))
    shape = jax.ShapeDtypeStruct
    pieces = width // DILATION
    own_groups, all_groups = height // pieces, (height + 2 * DILATION) // pieces
    depth = 9 * channels
    stack = pltpu.VMEM((height // DILATION + 2, 3 * channels, DILATION * width), bf16)
    parts = pltpu.VMEM((3, 3 * channels, DILATION * width), f32)
    edge = shape((DILATION, channels, width), bf16)
    packed = shape((all_groups, channels, width), bf16)
    own_rims = shape((2, own_groups, channels, width), bf16)
    rows = shape((height, channels, width), bf16)
    flops = 2 * depth * channels * height * width

    odd = lax.axis_index("row") % 2
    outer = shape((2, DILATION, channels, width), bf16)
    end = height - DILATION


    def image_rim(start, first):
        rim = lax.dynamic_slice_in_dim(image, start, DILATION, 1)
        flag = alone("row", first)
        return rim if flag is None else jnp.where(flag, jnp.zeros_like(rim), rim)

    one = swap_pairs(image_rim((1 - odd) * end, 0), "row", 0)
    two = swap_pairs(image_rim(odd * end, 1), "row", 1)
    image_rows, cotangent_rows, rims = call(
        own_kernel, (shape((3, *rows.shape), bf16), rows, own_rims), (image, cotangent)
    )
    forward_weight = jnp.transpose(weight, (0, 2, 1, 3)).reshape(3 * channels, 3 * channels)
    backward_weight = jnp.transpose(weight[::-1, ::-1], (0, 3, 1, 2)).reshape(3 * channels, 3 * channels)
    one, two, image_outer = call(
        functools.partial(rim_kernel, True), (packed, packed, outer), (one, two, rims)
    )
    two, one = swap_pairs(two, "col", 1), swap_pairs(one, "col", 0)
    activation, grads, one, two, rims, terms = call(
        functools.partial(forward_kernel, scale),
        (
            shape(image.shape, bf16), rows, edge, edge, own_rims,
            shape((channels, -(-(depth + 1) // 128) * 128), f32),
        ),
        (image_rows, image_outer, one, two, cotangent_rows, forward_weight, bias[:, None]),
        (stack, pltpu.VMEM((channels, width), f32), pltpu.VMEM((depth, channels), f32), parts),
        2 * flops,
    )
    one, two = swap_pairs(one, "row", 0), swap_pairs(two, "row", 1)
    one, two, grad_outer = call(
        functools.partial(rim_kernel, False), (packed, packed, outer), (one, two, rims)
    )
    two, one = swap_pairs(two, "col", 1), swap_pairs(one, "col", 0)
    grad_image, token = call(
        backward_kernel,
        (shape(image.shape, bf16), shape((8, 128), f32)),
        (grads, grad_outer, one, two, backward_weight),
        (stack, parts),
        flops,
    )
    one, other = add_pairs(terms, "col", "row")
    grad_weight, grad_bias = call(
        finish_kernel, (shape(weight.shape, f32), shape((1, channels), f32)), (one, other, token)
    )
    return (activation, grad_image, grad_weight, grad_bias.reshape(channels))


def solution(mesh):
    return jax.shard_map(
        shards,
        mesh=mesh,
        in_specs=(P(None, "row", "col"), P(), P(), P(None, "row", "col")),
        out_specs=(P(None, "row", "col"), P(None, "row", "col"), P(), P()),
        check_vma=False,
    )
```

```python
import functools
import math

import jax
import jax.numpy as jnp
from jax import lax
from jax.experimental import pallas as pl
from jax.experimental.pallas import tpu as pltpu
from jax.sharding import PartitionSpec as P

DILATION = 16
VMEM_BYTES = 16 * 2**20


def partners(axis, first):
    count = lax.axis_size(axis)
    to = list(range(count))
    for at in range(first, count - 1, 2):
        to[at], to[at + 1] = at + 1, at
    return list(enumerate(to))


def alone(axis, first):
    places = [at for at, other in partners(axis, first) if at == other]
    at = lax.axis_index(axis)
    return functools.reduce(jnp.logical_or, [at == place for place in places]) if places else None


def clear_if(flag, ref):
    if flag is not None:
        @pl.when(flag)
        def _():
            ref[...] = jnp.zeros_like(ref)


def swap_pairs(value, axis, first):
    other_axis = "col" if axis == "row" else "row"
    columns = lax.axis_size("col")

    def place(at, other):
        row, column = (at, other) if axis == "row" else (other, at)
        return row * columns + column

    pairs = []
    for at, to in partners(axis, first):
        for other, other_to in partners(other_axis, 0):
            pairs.append((place(at, other), place(to, other if to != at else other_to)))
    return lax.ppermute(value, ("row", "col"), pairs)


def rounds_of(axis):
    bits = [2**k for k in reversed(range(lax.axis_size(axis).bit_length() - 1))]
    return [(axis, bits[at : at + 2]) for at in range(0, len(bits), 2)]


def add_pairs(value, near_axis, far_axis):
    other = jnp.zeros_like(value)
    for place, (axis, bits) in enumerate(rounds_of(near_axis) + rounds_of(far_axis)):
        value = value + other if place else value
        masks = bits[::-1] + [sum(bits)] if len(bits) == 2 else bits
        came = [
            lax.ppermute(value, axis, [(at, at ^ mask) for at in range(lax.axis_size(axis))]) for mask in masks
        ]
        if len(came) == 3:
            value, other = value + came[0], came[1] + came[2]
        else:
            other = came[0]
    return value, other


def gelu_pair(preact):
    coef, cubic = 0.7978845608, 0.7978845608 * 0.044715
    square = preact * preact
    half = 0.5 + 0.5 * jnp.tanh(preact * (coef + cubic * square))
    slope_val = half * (1.0 + (1.0 - half) * (preact * (2.0 * coef + 6.0 * cubic * square)))
    return (preact * half, slope_val)


def lane_of(shape):
    return lax.broadcasted_iota(jnp.int32, shape, len(shape) - 1)


def pack_group(rows):
    half = len(rows) // 2
    width = rows[0].shape[-1]
    lane = lane_of(rows[0].shape)
    pair = lane // (2 * DILATION)
    front = lane % (2 * DILATION) < DILATION

    def joined(part):
        total = pltpu.roll(part[0], DILATION, 1)
        for k in range(1, half):
            total = jnp.where(pair == k, pltpu.roll(part[k], DILATION + 2 * DILATION * k, 1), total)
        return total

    low, high = joined(rows[:half]), joined(rows[half:])
    first = jnp.where(front, pltpu.roll(low, width - DILATION, 1), high)
    last = jnp.where(front, low, pltpu.roll(high, DILATION, 1))
    return first, last


def unpack_group(from_left, from_right, count):
    half = count // 2
    width = from_left.shape[-1]
    front = lane_of(from_left.shape) % (2 * DILATION) < DILATION
    low = jnp.where(front, from_right, pltpu.roll(from_left, DILATION, 1))
    high = jnp.where(front, pltpu.roll(from_right, width - DILATION, 1), from_left)
    return [
        pltpu.roll(low if k < half else high, (width - DILATION - 2 * DILATION * (k % half)) % width, 1)
        for k in range(count)
    ]


def pack_rows(block, store, first_group):
    pieces = block.shape[-1] // DILATION
    for group in range(block.shape[0] // pieces):
        first, last = pack_group([block[group * pieces + k] for k in range(pieces)])
        store(first_group + group, first, last)


def rolled(rows):
    axis, width = rows.ndim - 1, rows.shape[-1]
    return pltpu.roll(rows, DILATION, axis), rows, pltpu.roll(rows, width - DILATION, axis)


def own_kernel(image_ref, cotangent_ref, rows_ref, cotangent_rows_ref, one_ref, two_ref, rims_ref):
    count = image_ref.shape[1] // DILATION
    groups = rims_ref.shape[1] // count

    def store(place, first, last):
        rims_ref[0, place] = first
        rims_ref[1, place] = last

    def body(block, carry):
        start = pl.multiple_of(block * DILATION, DILATION)
        rows = jnp.swapaxes(image_ref[:, pl.ds(start, DILATION), :], 0, 1)
        for index, moved in enumerate(rolled(rows)):
            rows_ref[index, pl.ds(start, DILATION)] = moved
        cotangent_rows_ref[pl.ds(start, DILATION)] = jnp.swapaxes(
            cotangent_ref[:, pl.ds(start, DILATION), :], 0, 1
        )
        pack_rows(rows, store, block * groups)
        return carry

    lax.fori_loop(0, count, body, 0)

    def send(first_ref, last_ref):
        first_ref[...] = rims_ref[0]
        last_ref[...] = rims_ref[1]

    either("col", send, one_ref, two_ref)
    clear_if(alone("col", 0), one_ref)
    clear_if(alone("col", 1), two_ref)


def either(axis, body, one, two):
    odd = lax.axis_index(axis) % 2 == 1
    pl.when(odd)(lambda: body(one, two))
    pl.when(jnp.logical_not(odd))(lambda: body(two, one))


def rim_kernel(swap, one_ref, two_ref, rims_ref, send_one_ref, send_two_ref, outer_ref):
    own = rims_ref.shape[1]
    groups = (send_one_ref.shape[0] - own) // 2

    def order(upper_ref, lower_ref):
        for index, ref in enumerate((upper_ref, lower_ref)):
            outer_ref[index] = jnp.swapaxes(ref[...], 0, 1) if swap else ref[...]

    def pack(send_first_ref, send_last_ref):
        def store(place, first, last):
            send_first_ref[place] = first
            send_last_ref[place] = last

        send_first_ref[groups : groups + own] = rims_ref[0]
        send_last_ref[groups : groups + own] = rims_ref[1]
        for index in range(2):
            pack_rows(outer_ref[index], store, index * (groups + own))

    either("row", order, one_ref, two_ref)
    either("col", pack, send_one_ref, send_two_ref)
    clear_if(alone("col", 0), send_one_ref)
    clear_if(alone("col", 1), send_two_ref)


def outer_kernel(one_ref, two_ref, got_one_ref, got_two_ref, send_one_ref, send_two_ref, outer_ref):
    groups = send_one_ref.shape[0] // 2

    def order(upper_ref, lower_ref):
        for index, ref in enumerate((upper_ref, lower_ref)):
            outer_ref[index] = jnp.swapaxes(ref[...], 0, 1)

    def pack(send_first_ref, send_last_ref):
        def store(place, first, last):
            send_first_ref[place] = first
            send_last_ref[place] = last

        for index in range(2):
            pack_rows(outer_ref[index], store, index * groups)

    either("row", order, one_ref, two_ref)
    either("col", pack, send_one_ref, send_two_ref)
    clear_if(alone("col", 0), send_one_ref)
    clear_if(alone("col", 1), send_two_ref)


def spread(rows_of, left_ref, right_ref, stack_ref, block, group_start):
    channels, width = left_ref.shape[1:]
    pieces = width // DILATION
    lane = lane_of((channels, width))
    for group in range(DILATION // pieces):
        rims = unpack_group(left_ref[group_start + group], right_ref[group_start + group], pieces)
        for k in range(pieces):
            row = group * pieces + k
            before, value, after = rows_of(row)
            columns = slice(row * width, (row + 1) * width)
            before = jnp.where(lane < DILATION, rims[k], before)
            after = jnp.where(lane >= width - DILATION, rims[k], after)
            stack_ref[block, 0:channels, columns] = before
            stack_ref[block, channels : 2 * channels, columns] = value
            stack_ref[block, 2 * channels : 3 * channels, columns] = after


def spread_all(own_of, outer_ref, one, two, stack_ref):
    count = stack_ref.shape[0] - 2

    def every(left, right):
        (left_ref, own_left_ref, own_start), (right_ref, own_right_ref, _) = left, right
        groups = DILATION // (stack_ref.shape[2] // DILATION // DILATION)
        end = left_ref.shape[0] - groups
        spread(lambda row: rolled(outer_ref[0, row]), left_ref, right_ref, stack_ref, 0, 0)

        def body(block, carry):
            spread(
                lambda row: own_of(block * DILATION + row),
                own_left_ref, own_right_ref, stack_ref, block + 1, own_start + block * groups,
            )
            return carry

        lax.fori_loop(0, count, body, 0)
        spread(lambda row: rolled(outer_ref[1, row]), left_ref, right_ref, stack_ref, count + 1, end)

    either("col", every, one, two)


def forward_kernel(
    scale, own_ref, outer_ref, one_ref, two_ref, own_one_ref, own_two_ref, cotangent_ref, weight_ref, bias_ref,
    activation_ref, grad_ref, send_one_ref, send_two_ref, rims_ref, terms_ref, stack_ref, sum_ref, taps_ref,
):
    height, channels, width = own_ref.shape[1:]
    count = height // DILATION
    groups = rims_ref.shape[1] // count
    spread_all(lambda at: [own_ref[k, at] for k in range(3)], outer_ref, (one_ref, own_one_ref, 0), (two_ref, own_two_ref, 0), stack_ref)
    taps_ref[...] = jnp.zeros_like(taps_ref)
    sum_ref[...] = jnp.zeros_like(sum_ref)
    depth = 9 * channels

    def store(place, first, last):
        rims_ref[0, place] = first
        rims_ref[1, place] = last

    def body(block, carry):
        start = pl.multiple_of(block * DILATION, DILATION)
        stacked = stack_ref[pl.ds(block, 3)].reshape(depth, DILATION * width)
        preact = jnp.dot(weight_ref[...], stacked, preferred_element_type=jnp.float32)
        bias = jnp.broadcast_to(bias_ref[...], (channels, width))
        values, grads = [], []
        total = sum_ref[...]
        for row in range(DILATION):
            value, slope_val = gelu_pair(preact[:, row * width : (row + 1) * width] + bias)
            values.append(value.astype(jnp.bfloat16))
            grad = (cotangent_ref[start + row].astype(jnp.float32) * slope_val).astype(jnp.bfloat16)
            grads.append(grad)
            total = total + grad.astype(jnp.float32)
            grad_ref[start + row] = grad
        sum_ref[...] = total
        activation_ref[:, pl.ds(start, DILATION), :] = jnp.swapaxes(jnp.stack(values), 0, 1)
        taps_ref[...] += lax.dot_general(
            stacked, jnp.concatenate(grads, axis=1), (((1,), (1,)), ((), ())),
            preferred_element_type=jnp.float32,
        )
        pack_rows(jnp.stack(grads), store, block * groups)
        return carry

    lax.fori_loop(0, count, body, 0)
    end = height - DILATION
    odd = lax.axis_index("row") % 2
    send_one_ref[...] = grad_ref[pl.ds((1 - odd) * end, DILATION)]
    send_two_ref[...] = grad_ref[pl.ds(odd * end, DILATION)]
    clear_if(alone("row", 0), send_one_ref)
    clear_if(alone("row", 1), send_two_ref)
    terms_ref[:, :depth] = jnp.transpose(taps_ref[...]) * scale
    sums = jnp.sum(sum_ref[...], axis=1, keepdims=True) * scale
    terms_ref[:, depth:] = jnp.broadcast_to(sums, (channels, terms_ref.shape[1] - depth))


def backward_kernel(
    own_ref, outer_ref, one_ref, two_ref, weight_ref, out_ref, token_ref, stack_ref
):
    height, channels, width = own_ref.shape
    token_ref[...] = jnp.zeros_like(token_ref)
    start = one_ref.shape[0] // (height // DILATION + 2)
    spread_all(lambda at: rolled(own_ref[at]), outer_ref, (one_ref, one_ref, start), (two_ref, two_ref, start), stack_ref)

    def body(block, carry):
        start = pl.multiple_of(block * DILATION, DILATION)
        stacked = stack_ref[pl.ds(block, 3)].reshape(9 * channels, DILATION * width)
        total = jnp.dot(weight_ref[...], stacked, preferred_element_type=jnp.float32).astype(jnp.bfloat16)
        rows = jnp.stack([total[:, row * width : (row + 1) * width] for row in range(DILATION)])
        out_ref[:, pl.ds(start, DILATION), :] = jnp.swapaxes(rows, 0, 1)
        return carry

    lax.fori_loop(0, height // DILATION, body, 0)


def finish_kernel(one_ref, other_ref, after_ref, weight_ref, bias_ref):
    total = one_ref[...] + other_ref[...]
    channels = total.shape[0]
    for tap in range(9):
        weight_ref[tap // 3, tap % 3] = total[:, tap * channels : (tap + 1) * channels]
    flipped = jnp.transpose(total[:, total.shape[1] - 128 :])
    bias_ref[...] = flipped[127:128, :channels]


def call(kernel, out_shapes, operands, scratch=(), flops=0):
    whole = pl.BlockSpec(memory_space=pltpu.VMEM)
    size = sum(math.prod(x.shape) * jnp.dtype(x.dtype).itemsize for x in (*operands, *out_shapes))
    return pl.pallas_call(
        kernel,
        out_shape=out_shapes,
        in_specs=[whole] * len(operands),
        out_specs=[whole] * len(out_shapes),
        scratch_shapes=list(scratch),
        compiler_params=pltpu.CompilerParams(vmem_limit_bytes=VMEM_BYTES),
        cost_estimate=pl.CostEstimate(flops=flops, bytes_accessed=size, transcendentals=0),
    )(*operands)


def shards(image, weight, bias, cotangent):
    channels, height, width = image.shape
    bf16, f32 = jnp.bfloat16, jnp.float32
    scale = 1.0 / math.sqrt(height * lax.axis_size("row") * width * lax.axis_size("col"))
    shape = jax.ShapeDtypeStruct
    pieces = width // DILATION
    own_groups, all_groups = height // pieces, (height + 2 * DILATION) // pieces
    depth = 9 * channels
    stack = pltpu.VMEM((height // DILATION + 2, 3 * channels, DILATION * width), bf16)
    edge = shape((DILATION, channels, width), bf16)
    packed = shape((all_groups, channels, width), bf16)
    own_rims = shape((2, own_groups, channels, width), bf16)
    rows = shape((height, channels, width), bf16)
    flops = 2 * depth * channels * height * width

    odd = lax.axis_index("row") % 2
    outer = shape((2, DILATION, channels, width), bf16)
    end = height - DILATION


    def image_rim(start, first):
        rim = lax.dynamic_slice_in_dim(image, start, DILATION, 1)
        flag = alone("row", first)
        return rim if flag is None else jnp.where(flag, jnp.zeros_like(rim), rim)

    one = swap_pairs(image_rim((1 - odd) * end, 0), "row", 0)
    two = swap_pairs(image_rim(odd * end, 1), "row", 1)
    own_packed = shape((own_groups, channels, width), bf16)
    outer_packed = shape((all_groups - own_groups, channels, width), bf16)
    image_rows, cotangent_rows, own_one, own_two = call(
        own_kernel, (shape((3, *rows.shape), bf16), rows, own_packed, own_packed), (image, cotangent),
        (pltpu.VMEM(own_rims.shape, bf16),),
    )
    own_one, own_two = swap_pairs(own_one, "col", 0), swap_pairs(own_two, "col", 1)
    forward_weight = jnp.transpose(weight, (2, 0, 1, 3)).reshape(channels, depth)
    backward_weight = jnp.transpose(weight[::-1, ::-1], (3, 0, 1, 2)).reshape(channels, depth)
    one, two, image_outer = call(
        outer_kernel, (outer_packed, outer_packed, outer), (one, two, own_one, own_two)
    )
    two, one = swap_pairs(two, "col", 1), swap_pairs(one, "col", 0)
    activation, grads, one, two, rims, terms = call(
        functools.partial(forward_kernel, scale),
        (
            shape(image.shape, bf16), rows, edge, edge, own_rims,
            shape((channels, -(-(depth + 1) // 128) * 128), f32),
        ),
        (image_rows, image_outer, one, two, own_one, own_two, cotangent_rows, forward_weight, bias[:, None]),
        (stack, pltpu.VMEM((channels, width), f32), pltpu.VMEM((depth, channels), f32)),
        2 * flops,
    )
    one, two = swap_pairs(one, "row", 0), swap_pairs(two, "row", 1)
    one, two, grad_outer = call(
        functools.partial(rim_kernel, False), (packed, packed, outer), (one, two, rims)
    )
    two, one = swap_pairs(two, "col", 1), swap_pairs(one, "col", 0)
    grad_image, token = call(
        backward_kernel,
        (shape(image.shape, bf16), shape((8, 128), f32)),
        (grads, grad_outer, one, two, backward_weight),
        (stack,),
        flops,
    )
    one, other = add_pairs(terms, "col", "row")
    grad_weight, grad_bias = call(
        finish_kernel, (shape(weight.shape, f32), shape((1, channels), f32)), (one, other, token)
    )
    return (activation, grad_image, grad_weight, grad_bias.reshape(channels))


def solution(mesh):
    return jax.shard_map(
        shards,
        mesh=mesh,
        in_specs=(P(None, "row", "col"), P(), P(), P(None, "row", "col")),
        out_specs=(P(None, "row", "col"), P(None, "row", "col"), P(), P()),
        check_vma=False,
    )
```

```python
import functools
import math

import jax
import jax.numpy as jnp
from jax import lax
from jax.experimental import pallas as pl
from jax.experimental.pallas import tpu as pltpu
from jax.sharding import PartitionSpec as P

DILATION = 16
VMEM_BYTES = 16 * 2**20


def partners(axis, first):
    count = lax.axis_size(axis)
    to = list(range(count))
    for at in range(first, count - 1, 2):
        to[at], to[at + 1] = at + 1, at
    return list(enumerate(to))


def alone(axis, first):
    places = [at for at, other in partners(axis, first) if at == other]
    at = lax.axis_index(axis)
    return functools.reduce(jnp.logical_or, [at == place for place in places]) if places else None


def clear_if(flag, ref):
    if flag is not None:
        @pl.when(flag)
        def _():
            ref[...] = jnp.zeros_like(ref)


def swap_pairs(value, axis, first):
    other_axis = "col" if axis == "row" else "row"
    columns = lax.axis_size("col")

    def place(at, other):
        row, column = (at, other) if axis == "row" else (other, at)
        return row * columns + column

    pairs = []
    for at, to in partners(axis, first):
        for other, other_to in partners(other_axis, 0):
            pairs.append((place(at, other), place(to, other if to != at else other_to)))
    return lax.ppermute(value, ("row", "col"), pairs)


def rounds_of(axis):
    bits = [2**k for k in reversed(range(lax.axis_size(axis).bit_length() - 1))]
    return [(axis, bits[at : at + 2]) for at in range(0, len(bits), 2)]


def add_pairs(value, near_axis, far_axis):
    other = jnp.zeros_like(value)
    for place, (axis, bits) in enumerate(rounds_of(near_axis) + rounds_of(far_axis)):
        value = value + other if place else value
        masks = bits[::-1] + [sum(bits)] if len(bits) == 2 else bits
        came = [
            lax.ppermute(value, axis, [(at, at ^ mask) for at in range(lax.axis_size(axis))]) for mask in masks
        ]
        if len(came) == 3:
            value, other = value + came[0], came[1] + came[2]
        else:
            other = came[0]
    return value, other


def gelu_pair(preact):
    coef, cubic = 0.7978845608, 0.7978845608 * 0.044715
    square = preact * preact
    half = 0.5 + 0.5 * jnp.tanh(preact * (coef + cubic * square))
    slope_val = half * (1.0 + (1.0 - half) * (preact * (2.0 * coef + 6.0 * cubic * square)))
    return (preact * half, slope_val)


def lane_of(shape):
    return lax.broadcasted_iota(jnp.int32, shape, len(shape) - 1)


def pack_group(rows):
    half = len(rows) // 2
    width = rows[0].shape[-1]
    lane = lane_of(rows[0].shape)
    pair = lane // (2 * DILATION)
    front = lane % (2 * DILATION) < DILATION

    def joined(part):
        total = pltpu.roll(part[0], DILATION, 1)
        for k in range(1, half):
            total = jnp.where(pair == k, pltpu.roll(part[k], DILATION + 2 * DILATION * k, 1), total)
        return total

    low, high = joined(rows[:half]), joined(rows[half:])
    first = jnp.where(front, pltpu.roll(low, width - DILATION, 1), high)
    last = jnp.where(front, low, pltpu.roll(high, DILATION, 1))
    return first, last


def unpack_group(from_left, from_right, count):
    half = count // 2
    width = from_left.shape[-1]
    front = lane_of(from_left.shape) % (2 * DILATION) < DILATION
    low = jnp.where(front, from_right, pltpu.roll(from_left, DILATION, 1))
    high = jnp.where(front, pltpu.roll(from_right, width - DILATION, 1), from_left)
    return [
        pltpu.roll(low if k < half else high, (width - DILATION - 2 * DILATION * (k % half)) % width, 1)
        for k in range(count)
    ]


def pack_rows(block, store, first_group):
    pieces = block.shape[-1] // DILATION
    for group in range(block.shape[0] // pieces):
        first, last = pack_group([block[group * pieces + k] for k in range(pieces)])
        store(first_group + group, first, last)


def rolled(rows):
    axis, width = rows.ndim - 1, rows.shape[-1]
    return pltpu.roll(rows, DILATION, axis), rows, pltpu.roll(rows, width - DILATION, axis)


def own_kernel(image_ref, cotangent_ref, rows_ref, cotangent_rows_ref, rims_ref):
    count = image_ref.shape[1] // DILATION
    groups = rims_ref.shape[1] // count

    def store(place, first, last):
        rims_ref[0, place] = first
        rims_ref[1, place] = last

    def body(block, carry):
        start = pl.multiple_of(block * DILATION, DILATION)
        rows = jnp.swapaxes(image_ref[:, pl.ds(start, DILATION), :], 0, 1)
        for index, moved in enumerate(rolled(rows)):
            rows_ref[index, pl.ds(start, DILATION)] = moved
        cotangent_rows_ref[pl.ds(start, DILATION)] = jnp.swapaxes(
            cotangent_ref[:, pl.ds(start, DILATION), :], 0, 1
        )
        pack_rows(rows, store, block * groups)
        return carry

    lax.fori_loop(0, count, body, 0)


def either(axis, body, one, two):
    odd = lax.axis_index(axis) % 2 == 1
    pl.when(odd)(lambda: body(one, two))
    pl.when(jnp.logical_not(odd))(lambda: body(two, one))


def rim_kernel(swap, one_ref, two_ref, rims_ref, send_one_ref, send_two_ref, outer_ref):
    own = rims_ref.shape[1]
    groups = (send_one_ref.shape[0] - own) // 2

    def order(upper_ref, lower_ref):
        for index, ref in enumerate((upper_ref, lower_ref)):
            outer_ref[index] = jnp.swapaxes(ref[...], 0, 1) if swap else ref[...]

    def pack(send_first_ref, send_last_ref):
        def store(place, first, last):
            send_first_ref[place] = first
            send_last_ref[place] = last

        send_first_ref[groups : groups + own] = rims_ref[0]
        send_last_ref[groups : groups + own] = rims_ref[1]
        for index in range(2):
            pack_rows(outer_ref[index], store, index * (groups + own))

    either("row", order, one_ref, two_ref)
    either("col", pack, send_one_ref, send_two_ref)
    clear_if(alone("col", 0), send_one_ref)
    clear_if(alone("col", 1), send_two_ref)


def spread(rows_of, left_ref, right_ref, stack_ref, block, group_start):
    channels, width = left_ref.shape[1:]
    pieces = width // DILATION
    lane = lane_of((channels, width))
    for group in range(DILATION // pieces):
        rims = unpack_group(left_ref[group_start + group], right_ref[group_start + group], pieces)
        for k in range(pieces):
            row = group * pieces + k
            before, value, after = rows_of(row)
            columns = slice(row * width, (row + 1) * width)
            before = jnp.where(lane < DILATION, rims[k], before)
            after = jnp.where(lane >= width - DILATION, rims[k], after)
            stack_ref[block, 0:channels, columns] = before
            stack_ref[block, channels : 2 * channels, columns] = value
            stack_ref[block, 2 * channels : 3 * channels, columns] = after


def spread_all(own_of, outer_ref, one_ref, two_ref, stack_ref):
    count = stack_ref.shape[0] - 2
    groups = one_ref.shape[0] // (count + 2)

    def every(left_ref, right_ref):
        spread(lambda row: rolled(outer_ref[0, row]), left_ref, right_ref, stack_ref, 0, 0)

        def body(block, carry):
            spread(
                lambda row: own_of(block * DILATION + row),
                left_ref, right_ref, stack_ref, block + 1, (block + 1) * groups,
            )
            return carry

        lax.fori_loop(0, count, body, 0)
        spread(lambda row: rolled(outer_ref[1, row]), left_ref, right_ref, stack_ref, count + 1, (count + 1) * groups)

    either("col", every, one_ref, two_ref)


def forward_kernel(
    own_ref, outer_ref, one_ref, two_ref, cotangent_ref, weight_ref, bias_ref,
    activation_ref, grad_ref, send_one_ref, send_two_ref, rims_ref, taps_ref, sum_ref, stack_ref,
):
    height, channels, width = own_ref.shape[1:]
    count = height // DILATION
    groups = rims_ref.shape[1] // count
    spread_all(lambda at: [own_ref[k, at] for k in range(3)], outer_ref, one_ref, two_ref, stack_ref)
    taps_ref[...] = jnp.zeros_like(taps_ref)
    sum_ref[...] = jnp.zeros_like(sum_ref)
    depth = 9 * channels

    def store(place, first, last):
        rims_ref[0, place] = first
        rims_ref[1, place] = last

    def body(block, carry):
        start = pl.multiple_of(block * DILATION, DILATION)
        stacked = stack_ref[pl.ds(block, 3)].reshape(depth, DILATION * width)
        preact = jnp.dot(weight_ref[...], stacked, preferred_element_type=jnp.float32)
        bias = jnp.broadcast_to(bias_ref[...], (channels, width))
        values, grads = [], []
        total = sum_ref[...]
        for row in range(DILATION):
            value, slope_val = gelu_pair(preact[:, row * width : (row + 1) * width] + bias)
            values.append(value.astype(jnp.bfloat16))
            grad = (cotangent_ref[start + row].astype(jnp.float32) * slope_val).astype(jnp.bfloat16)
            grads.append(grad)
            total = total + grad.astype(jnp.float32)
            grad_ref[start + row] = grad
        sum_ref[...] = total
        activation_ref[:, pl.ds(start, DILATION), :] = jnp.swapaxes(jnp.stack(values), 0, 1)
        taps_ref[...] += lax.dot_general(
            stacked, jnp.concatenate(grads, axis=1), (((1,), (1,)), ((), ())),
            preferred_element_type=jnp.float32,
        )
        pack_rows(jnp.stack(grads), store, block * groups)
        return carry

    lax.fori_loop(0, count, body, 0)
    end = height - DILATION
    odd = lax.axis_index("row") % 2
    send_one_ref[...] = grad_ref[pl.ds((1 - odd) * end, DILATION)]
    send_two_ref[...] = grad_ref[pl.ds(odd * end, DILATION)]
    clear_if(alone("row", 0), send_one_ref)
    clear_if(alone("row", 1), send_two_ref)


def terms_kernel(scale, taps_ref, sum_ref, terms_ref):
    channels, depth = sum_ref.shape[0], taps_ref.shape[0]
    terms_ref[:, :depth] = jnp.transpose(taps_ref[...]) * scale
    sums = jnp.sum(sum_ref[...], axis=1, keepdims=True) * scale
    terms_ref[:, depth:] = jnp.broadcast_to(sums, (channels, terms_ref.shape[1] - depth))


def backward_kernel(
    own_ref, outer_ref, one_ref, two_ref, weight_ref, out_ref, token_ref, stack_ref
):
    height, channels, width = own_ref.shape
    token_ref[...] = jnp.zeros_like(token_ref)
    spread_all(lambda at: rolled(own_ref[at]), outer_ref, one_ref, two_ref, stack_ref)

    def body(block, carry):
        start = pl.multiple_of(block * DILATION, DILATION)
        stacked = stack_ref[pl.ds(block, 3)].reshape(9 * channels, DILATION * width)
        total = jnp.dot(weight_ref[...], stacked, preferred_element_type=jnp.float32).astype(jnp.bfloat16)
        rows = jnp.stack([total[:, row * width : (row + 1) * width] for row in range(DILATION)])
        out_ref[:, pl.ds(start, DILATION), :] = jnp.swapaxes(rows, 0, 1)
        return carry

    lax.fori_loop(0, height // DILATION, body, 0)


def finish_kernel(one_ref, other_ref, after_ref, weight_ref, bias_ref):
    total = one_ref[...] + other_ref[...]
    channels = total.shape[0]
    for tap in range(9):
        weight_ref[tap // 3, tap % 3] = total[:, tap * channels : (tap + 1) * channels]
    flipped = jnp.transpose(total[:, total.shape[1] - 128 :])
    bias_ref[...] = flipped[127:128, :channels]


def call(kernel, out_shapes, operands, scratch=(), flops=0):
    whole = pl.BlockSpec(memory_space=pltpu.VMEM)
    size = sum(math.prod(x.shape) * jnp.dtype(x.dtype).itemsize for x in (*operands, *out_shapes))
    return pl.pallas_call(
        kernel,
        out_shape=out_shapes,
        in_specs=[whole] * len(operands),
        out_specs=[whole] * len(out_shapes),
        scratch_shapes=list(scratch),
        compiler_params=pltpu.CompilerParams(vmem_limit_bytes=VMEM_BYTES),
        cost_estimate=pl.CostEstimate(flops=flops, bytes_accessed=size, transcendentals=0),
    )(*operands)


def shards(image, weight, bias, cotangent):
    channels, height, width = image.shape
    bf16, f32 = jnp.bfloat16, jnp.float32
    scale = 1.0 / math.sqrt(height * lax.axis_size("row") * width * lax.axis_size("col"))
    shape = jax.ShapeDtypeStruct
    pieces = width // DILATION
    own_groups, all_groups = height // pieces, (height + 2 * DILATION) // pieces
    depth = 9 * channels
    stack = pltpu.VMEM((height // DILATION + 2, 3 * channels, DILATION * width), bf16)
    edge = shape((DILATION, channels, width), bf16)
    packed = shape((all_groups, channels, width), bf16)
    own_rims = shape((2, own_groups, channels, width), bf16)
    rows = shape((height, channels, width), bf16)
    flops = 2 * depth * channels * height * width

    odd = lax.axis_index("row") % 2
    outer = shape((2, DILATION, channels, width), bf16)
    end = height - DILATION


    def image_rim(start, first):
        rim = lax.dynamic_slice_in_dim(image, start, DILATION, 1)
        flag = alone("row", first)
        return rim if flag is None else jnp.where(flag, jnp.zeros_like(rim), rim)

    one = swap_pairs(image_rim((1 - odd) * end, 0), "row", 0)
    two = swap_pairs(image_rim(odd * end, 1), "row", 1)
    image_rows, cotangent_rows, rims = call(
        own_kernel, (shape((3, *rows.shape), bf16), rows, own_rims), (image, cotangent)
    )
    forward_weight = jnp.transpose(weight, (2, 0, 1, 3)).reshape(channels, depth)
    backward_weight = jnp.transpose(weight[::-1, ::-1], (3, 0, 1, 2)).reshape(channels, depth)
    one, two, image_outer = call(
        functools.partial(rim_kernel, True), (packed, packed, outer), (one, two, rims)
    )
    two, one = swap_pairs(two, "col", 1), swap_pairs(one, "col", 0)
    activation, grads, one, two, rims, taps, sums = call(
        forward_kernel,
        (
            shape(image.shape, bf16), rows, edge, edge, own_rims,
            shape((depth, channels), f32), shape((channels, width), f32),
        ),
        (image_rows, image_outer, one, two, cotangent_rows, forward_weight, bias[:, None]),
        (stack,),
        2 * flops,
    )
    (terms,) = call(
        functools.partial(terms_kernel, scale),
        (shape((channels, -(-(depth + 1) // 128) * 128), f32),),
        (taps, sums),
    )
    one, two = swap_pairs(one, "row", 0), swap_pairs(two, "row", 1)
    one, two, grad_outer = call(
        functools.partial(rim_kernel, False), (packed, packed, outer), (one, two, rims)
    )
    two, one = swap_pairs(two, "col", 1), swap_pairs(one, "col", 0)
    grad_image, token = call(
        backward_kernel,
        (shape(image.shape, bf16), shape((8, 128), f32)),
        (grads, grad_outer, one, two, backward_weight),
        (stack,),
        flops,
    )
    one, other = add_pairs(terms, "col", "row")
    grad_weight, grad_bias = call(
        finish_kernel, (shape(weight.shape, f32), shape((1, channels), f32)), (one, other, token)
    )
    return (activation, grad_image, grad_weight, grad_bias.reshape(channels))


def solution(mesh):
    return jax.shard_map(
        shards,
        mesh=mesh,
        in_specs=(P(None, "row", "col"), P(), P(), P(None, "row", "col")),
        out_specs=(P(None, "row", "col"), P(None, "row", "col"), P(), P()),
        check_vma=False,
    )
```

```python
import functools
import math

import jax
import jax.numpy as jnp
from jax import lax
from jax.experimental import pallas as pl
from jax.experimental.pallas import tpu as pltpu
from jax.sharding import PartitionSpec as P

DILATION = 16
VMEM_BYTES = 16 * 2**20


def partners(axis, first):
    count = lax.axis_size(axis)
    to = list(range(count))
    for at in range(first, count - 1, 2):
        to[at], to[at + 1] = at + 1, at
    return list(enumerate(to))


def alone(axis, first):
    places = [at for at, other in partners(axis, first) if at == other]
    at = lax.axis_index(axis)
    return functools.reduce(jnp.logical_or, [at == place for place in places]) if places else None


def clear_if(flag, ref):
    if flag is not None:
        @pl.when(flag)
        def _():
            ref[...] = jnp.zeros_like(ref)


def swap_pairs(value, axis, first):
    other_axis = "col" if axis == "row" else "row"
    columns = lax.axis_size("col")

    def place(at, other):
        row, column = (at, other) if axis == "row" else (other, at)
        return row * columns + column

    pairs = []
    for at, to in partners(axis, first):
        for other, other_to in partners(other_axis, 0):
            pairs.append((place(at, other), place(to, other if to != at else other_to)))
    return lax.ppermute(value, ("row", "col"), pairs)


def rounds_of(axis):
    bits = [2**k for k in reversed(range(lax.axis_size(axis).bit_length() - 1))]
    single = [[bits.pop(min(1, len(bits) - 1))]] if len(bits) % 2 else []
    return [(axis, part) for part in single + [bits[at : at + 2] for at in range(0, len(bits), 2)]]


def add_pairs(value, near_axis, far_axis):
    other = jnp.zeros_like(value)
    for place, (axis, bits) in enumerate(rounds_of(near_axis) + rounds_of(far_axis)):
        value = value + other if place else value
        masks = bits[::-1] + [sum(bits)] if len(bits) == 2 else bits
        came = [
            lax.ppermute(value, axis, [(at, at ^ mask) for at in range(lax.axis_size(axis))]) for mask in masks
        ]
        if len(came) == 3:
            value, other = value + came[0], came[1] + came[2]
        else:
            other = came[0]
    return value, other


def gelu_pair(preact):
    coef = 0.7978845608
    square = preact * preact
    tval = jnp.tanh(coef * (preact + 0.044715 * (square * preact)))
    half = 0.5 * (1.0 + tval)
    slope_val = half + 0.5 * preact * (1.0 - tval * tval) * coef * (1.0 + 3.0 * 0.044715 * square)
    return (preact * half, slope_val)


def lane_of(shape):
    return lax.broadcasted_iota(jnp.int32, shape, len(shape) - 1)


def pack_group(rows):
    half = len(rows) // 2
    width = rows[0].shape[-1]
    lane = lane_of(rows[0].shape)
    pair = lane // (2 * DILATION)
    front = lane % (2 * DILATION) < DILATION

    def joined(part):
        total = pltpu.roll(part[0], DILATION, 1)
        for k in range(1, half):
            total = jnp.where(pair == k, pltpu.roll(part[k], DILATION + 2 * DILATION * k, 1), total)
        return total

    low, high = joined(rows[:half]), joined(rows[half:])
    first = jnp.where(front, pltpu.roll(low, width - DILATION, 1), high)
    last = jnp.where(front, low, pltpu.roll(high, DILATION, 1))
    return first, last


def unpack_group(from_left, from_right, count):
    half = count // 2
    width = from_left.shape[-1]
    front = lane_of(from_left.shape) % (2 * DILATION) < DILATION
    low = jnp.where(front, from_right, pltpu.roll(from_left, DILATION, 1))
    high = jnp.where(front, pltpu.roll(from_right, width - DILATION, 1), from_left)
    return [
        pltpu.roll(low if k < half else high, (width - DILATION - 2 * DILATION * (k % half)) % width, 1)
        for k in range(count)
    ]


def pack_rows(block, store, first_group):
    pieces = block.shape[-1] // DILATION
    for group in range(block.shape[0] // pieces):
        first, last = pack_group([block[group * pieces + k] for k in range(pieces)])
        store(first_group + group, first, last)


def own_kernel(image_ref, rows_ref, rims_ref):
    count = image_ref.shape[1] // DILATION
    groups = rims_ref.shape[1] // count

    def store(place, first, last):
        rims_ref[0, place] = first
        rims_ref[1, place] = last

    def body(block, carry):
        start = pl.multiple_of(block * DILATION, DILATION)
        rows = jnp.swapaxes(image_ref[:, pl.ds(start, DILATION), :], 0, 1)
        rows_ref[pl.ds(start, DILATION)] = rows
        pack_rows(rows, store, block * groups)
        return carry

    lax.fori_loop(0, count, body, 0)


def either(axis, body, one, two):
    odd = lax.axis_index(axis) % 2 == 1
    pl.when(odd)(lambda: body(one, two))
    pl.when(jnp.logical_not(odd))(lambda: body(two, one))


def rim_kernel(swap, one_ref, two_ref, rims_ref, send_one_ref, send_two_ref, outer_ref):
    own = rims_ref.shape[1]
    groups = (send_one_ref.shape[0] - own) // 2

    def order(upper_ref, lower_ref):
        for index, ref in enumerate((upper_ref, lower_ref)):
            outer_ref[index] = jnp.swapaxes(ref[...], 0, 1) if swap else ref[...]

    def pack(send_first_ref, send_last_ref):
        def store(place, first, last):
            send_first_ref[place] = first
            send_last_ref[place] = last

        send_first_ref[groups : groups + own] = rims_ref[0]
        send_last_ref[groups : groups + own] = rims_ref[1]
        for index in range(2):
            pack_rows(outer_ref[index], store, index * (groups + own))

    either("row", order, one_ref, two_ref)
    either("col", pack, send_one_ref, send_two_ref)
    clear_if(alone("col", 0), send_one_ref)
    clear_if(alone("col", 1), send_two_ref)


def spread(rows_of, left_ref, right_ref, stack_ref, block, group_start):
    channels, width = left_ref.shape[1:]
    pieces = width // DILATION
    lane = lane_of((channels, width))
    for group in range(DILATION // pieces):
        rims = unpack_group(left_ref[group_start + group], right_ref[group_start + group], pieces)
        for k in range(pieces):
            row = group * pieces + k
            value = rows_of(row)
            columns = slice(row * width, (row + 1) * width)
            before = jnp.where(lane < DILATION, rims[k], pltpu.roll(value, DILATION, 1))
            after = jnp.where(lane >= width - DILATION, rims[k], pltpu.roll(value, width - DILATION, 1))
            stack_ref[block, 0:channels, columns] = before
            stack_ref[block, channels : 2 * channels, columns] = value
            stack_ref[block, 2 * channels : 3 * channels, columns] = after


def spread_all(own_ref, outer_ref, one_ref, two_ref, stack_ref):
    count = own_ref.shape[0] // DILATION
    groups = one_ref.shape[0] // (count + 2)

    def every(left_ref, right_ref):
        spread(lambda row: outer_ref[0, row], left_ref, right_ref, stack_ref, 0, 0)

        def body(block, carry):
            spread(
                lambda row: own_ref[block * DILATION + row],
                left_ref, right_ref, stack_ref, block + 1, (block + 1) * groups,
            )
            return carry

        lax.fori_loop(0, count, body, 0)
        spread(lambda row: outer_ref[1, row], left_ref, right_ref, stack_ref, count + 1, (count + 1) * groups)

    either("col", every, one_ref, two_ref)


def forward_kernel(
    scale, own_ref, outer_ref, one_ref, two_ref, cotangent_ref, weight_ref, bias_ref,
    activation_ref, grad_ref, send_one_ref, send_two_ref, rims_ref, terms_ref, stack_ref, sum_ref, taps_ref,
):
    height, channels, width = own_ref.shape
    count = height // DILATION
    groups = rims_ref.shape[1] // count
    spread_all(own_ref, outer_ref, one_ref, two_ref, stack_ref)
    taps_ref[...] = jnp.zeros_like(taps_ref)
    sum_ref[...] = jnp.zeros_like(sum_ref)
    depth = 9 * channels

    def store(place, first, last):
        rims_ref[0, place] = first
        rims_ref[1, place] = last

    def body(block, carry):
        start = pl.multiple_of(block * DILATION, DILATION)
        stacked = stack_ref[pl.ds(block, 3)].reshape(depth, DILATION * width)
        preact = jnp.dot(weight_ref[...], stacked, preferred_element_type=jnp.float32)
        cotangent = jnp.swapaxes(cotangent_ref[:, pl.ds(start, DILATION), :], 0, 1)
        bias = jnp.broadcast_to(bias_ref[...], (channels, width))
        values, grads = [], []
        total = sum_ref[...]
        for row in range(DILATION):
            value, slope_val = gelu_pair(preact[:, row * width : (row + 1) * width] + bias)
            values.append(value.astype(jnp.bfloat16))
            grad = (cotangent[row].astype(jnp.float32) * slope_val).astype(jnp.bfloat16)
            grads.append(grad)
            total = total + grad.astype(jnp.float32)
            grad_ref[start + row] = grad
        sum_ref[...] = total
        activation_ref[:, pl.ds(start, DILATION), :] = jnp.swapaxes(jnp.stack(values), 0, 1)
        taps_ref[...] += lax.dot_general(
            stacked, jnp.concatenate(grads, axis=1), (((1,), (1,)), ((), ())),
            preferred_element_type=jnp.float32,
        )
        pack_rows(jnp.stack(grads), store, block * groups)
        return carry

    lax.fori_loop(0, count, body, 0)
    end = height - DILATION
    odd = lax.axis_index("row") % 2
    send_one_ref[...] = grad_ref[pl.ds((1 - odd) * end, DILATION)]
    send_two_ref[...] = grad_ref[pl.ds(odd * end, DILATION)]
    clear_if(alone("row", 0), send_one_ref)
    clear_if(alone("row", 1), send_two_ref)
    terms_ref[:, :depth] = jnp.transpose(taps_ref[...]) * scale
    sums = jnp.sum(sum_ref[...], axis=1, keepdims=True) * scale
    terms_ref[:, depth:] = jnp.broadcast_to(sums, (channels, terms_ref.shape[1] - depth))


def backward_kernel(
    own_ref, outer_ref, one_ref, two_ref, weight_ref, out_ref, token_ref, stack_ref
):
    height, channels, width = own_ref.shape
    token_ref[...] = jnp.zeros_like(token_ref)
    spread_all(own_ref, outer_ref, one_ref, two_ref, stack_ref)

    def body(block, carry):
        start = pl.multiple_of(block * DILATION, DILATION)
        stacked = stack_ref[pl.ds(block, 3)].reshape(9 * channels, DILATION * width)
        total = jnp.dot(weight_ref[...], stacked, preferred_element_type=jnp.float32).astype(jnp.bfloat16)
        rows = jnp.stack([total[:, row * width : (row + 1) * width] for row in range(DILATION)])
        out_ref[:, pl.ds(start, DILATION), :] = jnp.swapaxes(rows, 0, 1)
        return carry

    lax.fori_loop(0, height // DILATION, body, 0)


def finish_kernel(one_ref, other_ref, after_ref, weight_ref, bias_ref):
    total = one_ref[...] + other_ref[...]
    channels = total.shape[0]
    for tap in range(9):
        weight_ref[tap // 3, tap % 3] = total[:, tap * channels : (tap + 1) * channels]
    flipped = jnp.transpose(total[:, total.shape[1] - 128 :])
    bias_ref[...] = flipped[127:128, :channels]


def call(kernel, out_shapes, operands, scratch=(), flops=0):
    whole = pl.BlockSpec(memory_space=pltpu.VMEM)
    size = sum(math.prod(x.shape) * jnp.dtype(x.dtype).itemsize for x in (*operands, *out_shapes))
    return pl.pallas_call(
        kernel,
        out_shape=out_shapes,
        in_specs=[whole] * len(operands),
        out_specs=[whole] * len(out_shapes),
        scratch_shapes=list(scratch),
        compiler_params=pltpu.CompilerParams(vmem_limit_bytes=VMEM_BYTES),
        cost_estimate=pl.CostEstimate(flops=flops, bytes_accessed=size, transcendentals=0),
    )(*operands)


def shards(image, weight, bias, cotangent):
    channels, height, width = image.shape
    bf16, f32 = jnp.bfloat16, jnp.float32
    scale = 1.0 / math.sqrt(height * lax.axis_size("row") * width * lax.axis_size("col"))
    shape = jax.ShapeDtypeStruct
    pieces = width // DILATION
    own_groups, all_groups = height // pieces, (height + 2 * DILATION) // pieces
    depth = 9 * channels
    stack = pltpu.VMEM((height // DILATION + 2, 3 * channels, DILATION * width), bf16)
    edge = shape((DILATION, channels, width), bf16)
    packed = shape((all_groups, channels, width), bf16)
    own_rims = shape((2, own_groups, channels, width), bf16)
    rows = shape((height, channels, width), bf16)
    flops = 2 * depth * channels * height * width

    odd = lax.axis_index("row") % 2
    outer = shape((2, DILATION, channels, width), bf16)
    end = height - DILATION


    def image_rim(start, first):
        rim = lax.dynamic_slice_in_dim(image, start, DILATION, 1)
        flag = alone("row", first)
        return rim if flag is None else jnp.where(flag, jnp.zeros_like(rim), rim)

    one = swap_pairs(image_rim((1 - odd) * end, 0), "row", 0)
    two = swap_pairs(image_rim(odd * end, 1), "row", 1)
    image_rows, rims = call(own_kernel, (rows, own_rims), (image,))
    forward_weight = jnp.transpose(weight, (2, 0, 1, 3)).reshape(channels, depth)
    backward_weight = jnp.transpose(weight[::-1, ::-1], (3, 0, 1, 2)).reshape(channels, depth)
    one, two, image_outer = call(
        functools.partial(rim_kernel, True), (packed, packed, outer), (one, two, rims)
    )
    two, one = swap_pairs(two, "col", 1), swap_pairs(one, "col", 0)
    activation, grads, one, two, rims, terms = call(
        functools.partial(forward_kernel, scale),
        (
            shape(image.shape, bf16), rows, edge, edge, own_rims,
            shape((channels, -(-(depth + 1) // 128) * 128), f32),
        ),
        (image_rows, image_outer, one, two, cotangent, forward_weight, bias[:, None]),
        (stack, pltpu.VMEM((channels, width), f32), pltpu.VMEM((depth, channels), f32)),
        2 * flops,
    )
    one, two = swap_pairs(one, "row", 0), swap_pairs(two, "row", 1)
    one, two, grad_outer = call(
        functools.partial(rim_kernel, False), (packed, packed, outer), (one, two, rims)
    )
    two, one = swap_pairs(two, "col", 1), swap_pairs(one, "col", 0)
    grad_image, token = call(
        backward_kernel,
        (shape(image.shape, bf16), shape((8, 128), f32)),
        (grads, grad_outer, one, two, backward_weight),
        (stack,),
        flops,
    )
    one, other = add_pairs(terms, "col", "row")
    grad_weight, grad_bias = call(
        finish_kernel, (shape(weight.shape, f32), shape((1, channels), f32)), (one, other, token)
    )
    return (activation, grad_image, grad_weight, grad_bias.reshape(channels))


def solution(mesh):
    return jax.shard_map(
        shards,
        mesh=mesh,
        in_specs=(P(None, "row", "col"), P(), P(), P(None, "row", "col")),
        out_specs=(P(None, "row", "col"), P(None, "row", "col"), P(), P()),
        check_vma=False,
    )
```

```python
import functools
import math

import jax
import jax.numpy as jnp
from jax import lax
from jax.experimental import pallas as pl
from jax.experimental.pallas import tpu as pltpu
from jax.sharding import PartitionSpec as P

DILATION = 16
VMEM_BYTES = 16 * 2**20


def partners(axis, first):
    count = lax.axis_size(axis)
    to = list(range(count))
    for at in range(first, count - 1, 2):
        to[at], to[at + 1] = at + 1, at
    return list(enumerate(to))


def alone(axis, first):
    places = [at for at, other in partners(axis, first) if at == other]
    at = lax.axis_index(axis)
    return functools.reduce(jnp.logical_or, [at == place for place in places]) if places else None


def clear_if(flag, ref):
    if flag is not None:
        @pl.when(flag)
        def _():
            ref[...] = jnp.zeros_like(ref)


def swap_pairs(value, axis, first):
    other_axis = "col" if axis == "row" else "row"
    columns = lax.axis_size("col")

    def place(at, other):
        row, column = (at, other) if axis == "row" else (other, at)
        return row * columns + column

    pairs = []
    for at, to in partners(axis, first):
        for other, other_to in partners(other_axis, 0):
            pairs.append((place(at, other), place(to, other if to != at else other_to)))
    return lax.ppermute(value, ("row", "col"), pairs)


def rounds_of(axis):
    bits = [2**k for k in reversed(range(lax.axis_size(axis).bit_length() - 1))]
    return [(axis, bits[at : at + 2]) for at in range(0, len(bits), 2)]


def add_pairs(value, near_axis, far_axis):
    other = jnp.zeros_like(value)
    for place, (axis, bits) in enumerate(rounds_of(near_axis) + rounds_of(far_axis)):
        value = value + other if place else value
        masks = bits[::-1] + [sum(bits)] if len(bits) == 2 else bits
        came = [
            lax.ppermute(value, axis, [(at, at ^ mask) for at in range(lax.axis_size(axis))]) for mask in masks
        ]
        if len(came) == 3:
            value, other = value + came[0], came[1] + came[2]
        else:
            other = came[0]
    return value, other


def gelu_pair(preact):
    coef = 0.7978845608
    square = preact * preact
    tval = jnp.tanh(coef * (preact + 0.044715 * (square * preact)))
    half = 0.5 * (1.0 + tval)
    slope_val = half + 0.5 * preact * (1.0 - tval * tval) * coef * (1.0 + 3.0 * 0.044715 * square)
    return (preact * half, slope_val)


def lane_of(shape):
    return lax.broadcasted_iota(jnp.int32, shape, len(shape) - 1)


def pack_group(rows):
    half = len(rows) // 2
    width = rows[0].shape[-1]
    lane = lane_of(rows[0].shape)
    pair = lane // (2 * DILATION)
    front = lane % (2 * DILATION) < DILATION

    def joined(part):
        total = pltpu.roll(part[0], DILATION, 1)
        for k in range(1, half):
            total = jnp.where(pair == k, pltpu.roll(part[k], DILATION + 2 * DILATION * k, 1), total)
        return total

    low, high = joined(rows[:half]), joined(rows[half:])
    first = jnp.where(front, pltpu.roll(low, width - DILATION, 1), high)
    last = jnp.where(front, low, pltpu.roll(high, DILATION, 1))
    return first, last


def unpack_group(from_left, from_right, count):
    half = count // 2
    width = from_left.shape[-1]
    front = lane_of(from_left.shape) % (2 * DILATION) < DILATION
    low = jnp.where(front, from_right, pltpu.roll(from_left, DILATION, 1))
    high = jnp.where(front, pltpu.roll(from_right, width - DILATION, 1), from_left)
    return [
        pltpu.roll(low if k < half else high, (width - DILATION - 2 * DILATION * (k % half)) % width, 1)
        for k in range(count)
    ]


def pack_rows(block, store, first_group):
    pieces = block.shape[-1] // DILATION
    for group in range(block.shape[0] // pieces):
        first, last = pack_group([block[group * pieces + k] for k in range(pieces)])
        store(first_group + group, first, last)


def own_kernel(image_ref, rows_ref, rims_ref):
    count = image_ref.shape[1] // DILATION
    groups = rims_ref.shape[1] // count

    def store(place, first, last):
        rims_ref[0, place] = first
        rims_ref[1, place] = last

    def body(block, carry):
        start = pl.multiple_of(block * DILATION, DILATION)
        rows = jnp.swapaxes(image_ref[:, pl.ds(start, DILATION), :], 0, 1)
        rows_ref[pl.ds(start, DILATION)] = rows
        pack_rows(rows, store, block * groups)
        return carry

    lax.fori_loop(0, count, body, 0)


def either(axis, body, one, two):
    odd = lax.axis_index(axis) % 2 == 1
    pl.when(odd)(lambda: body(one, two))
    pl.when(jnp.logical_not(odd))(lambda: body(two, one))


def rim_kernel(swap, one_ref, two_ref, rims_ref, send_one_ref, send_two_ref, outer_ref):
    own = rims_ref.shape[1]
    groups = (send_one_ref.shape[0] - own) // 2

    def order(upper_ref, lower_ref):
        for index, ref in enumerate((upper_ref, lower_ref)):
            outer_ref[index] = jnp.swapaxes(ref[...], 0, 1) if swap else ref[...]

    def pack(send_first_ref, send_last_ref):
        def store(place, first, last):
            send_first_ref[place] = first
            send_last_ref[place] = last

        send_first_ref[groups : groups + own] = rims_ref[0]
        send_last_ref[groups : groups + own] = rims_ref[1]
        for index in range(2):
            pack_rows(outer_ref[index], store, index * (groups + own))

    either("row", order, one_ref, two_ref)
    either("col", pack, send_one_ref, send_two_ref)
    clear_if(alone("col", 0), send_one_ref)
    clear_if(alone("col", 1), send_two_ref)


def rim_after_kernel(one_ref, two_ref, rims_ref, after_ref, send_one_ref, send_two_ref, outer_ref):
    rim_kernel(False, one_ref, two_ref, rims_ref, send_one_ref, send_two_ref, outer_ref)


def spread(rows_of, left_ref, right_ref, stack_ref, block, group_start):
    channels, width = left_ref.shape[1:]
    pieces = width // DILATION
    lane = lane_of((channels, width))
    for group in range(DILATION // pieces):
        rims = unpack_group(left_ref[group_start + group], right_ref[group_start + group], pieces)
        for k in range(pieces):
            row = group * pieces + k
            value = rows_of(row)
            columns = slice(row * width, (row + 1) * width)
            before = jnp.where(lane < DILATION, rims[k], pltpu.roll(value, DILATION, 1))
            after = jnp.where(lane >= width - DILATION, rims[k], pltpu.roll(value, width - DILATION, 1))
            stack_ref[block, 0:channels, columns] = before
            stack_ref[block, channels : 2 * channels, columns] = value
            stack_ref[block, 2 * channels : 3 * channels, columns] = after


def spread_all(own_ref, outer_ref, one_ref, two_ref, stack_ref):
    count = own_ref.shape[0] // DILATION
    groups = one_ref.shape[0] // (count + 2)

    def every(left_ref, right_ref):
        spread(lambda row: outer_ref[0, row], left_ref, right_ref, stack_ref, 0, 0)

        def body(block, carry):
            spread(
                lambda row: own_ref[block * DILATION + row],
                left_ref, right_ref, stack_ref, block + 1, (block + 1) * groups,
            )
            return carry

        lax.fori_loop(0, count, body, 0)
        spread(lambda row: outer_ref[1, row], left_ref, right_ref, stack_ref, count + 1, (count + 1) * groups)

    either("col", every, one_ref, two_ref)


def forward_kernel(
    scale, own_ref, outer_ref, one_ref, two_ref, cotangent_ref, weight_ref, bias_ref,
    activation_ref, grad_ref, send_one_ref, send_two_ref, rims_ref, terms_ref, stack_ref, sum_ref, taps_ref,
):
    height, channels, width = own_ref.shape
    count = height // DILATION
    groups = rims_ref.shape[1] // count
    spread_all(own_ref, outer_ref, one_ref, two_ref, stack_ref)
    taps_ref[...] = jnp.zeros_like(taps_ref)
    sum_ref[...] = jnp.zeros_like(sum_ref)
    depth = 9 * channels

    def store(place, first, last):
        rims_ref[0, place] = first
        rims_ref[1, place] = last

    def body(block, carry):
        start = pl.multiple_of(block * DILATION, DILATION)
        stacked = stack_ref[pl.ds(block, 3)].reshape(depth, DILATION * width)
        preact = jnp.dot(weight_ref[...], stacked, preferred_element_type=jnp.float32)
        cotangent = jnp.swapaxes(cotangent_ref[:, pl.ds(start, DILATION), :], 0, 1)
        bias = jnp.broadcast_to(bias_ref[...], (channels, width))
        values, grads = [], []
        total = sum_ref[...]
        for row in range(DILATION):
            value, slope_val = gelu_pair(preact[:, row * width : (row + 1) * width] + bias)
            values.append(value.astype(jnp.bfloat16))
            grad = (cotangent[row].astype(jnp.float32) * slope_val).astype(jnp.bfloat16)
            grads.append(grad)
            total = total + grad.astype(jnp.float32)
            grad_ref[start + row] = grad
        sum_ref[...] = total
        activation_ref[:, pl.ds(start, DILATION), :] = jnp.swapaxes(jnp.stack(values), 0, 1)
        taps_ref[...] += lax.dot_general(
            stacked, jnp.concatenate(grads, axis=1), (((1,), (1,)), ((), ())),
            preferred_element_type=jnp.float32,
        )
        pack_rows(jnp.stack(grads), store, block * groups)
        return carry

    lax.fori_loop(0, count, body, 0)
    end = height - DILATION
    odd = lax.axis_index("row") % 2
    send_one_ref[...] = grad_ref[pl.ds((1 - odd) * end, DILATION)]
    send_two_ref[...] = grad_ref[pl.ds(odd * end, DILATION)]
    clear_if(alone("row", 0), send_one_ref)
    clear_if(alone("row", 1), send_two_ref)
    terms_ref[:, :depth] = jnp.transpose(taps_ref[...]) * scale
    sums = jnp.sum(sum_ref[...], axis=1, keepdims=True) * scale
    terms_ref[:, depth:] = jnp.broadcast_to(sums, (channels, terms_ref.shape[1] - depth))


def backward_kernel(
    own_ref, outer_ref, one_ref, two_ref, weight_ref, out_ref, token_ref, stack_ref
):
    height, channels, width = own_ref.shape
    token_ref[...] = jnp.zeros_like(token_ref)
    spread_all(own_ref, outer_ref, one_ref, two_ref, stack_ref)

    def body(block, carry):
        start = pl.multiple_of(block * DILATION, DILATION)
        stacked = stack_ref[pl.ds(block, 3)].reshape(9 * channels, DILATION * width)
        total = jnp.dot(weight_ref[...], stacked, preferred_element_type=jnp.float32).astype(jnp.bfloat16)
        rows = jnp.stack([total[:, row * width : (row + 1) * width] for row in range(DILATION)])
        out_ref[:, pl.ds(start, DILATION), :] = jnp.swapaxes(rows, 0, 1)
        return carry

    lax.fori_loop(0, height // DILATION, body, 0)


def finish_kernel(one_ref, other_ref, after_ref, weight_ref, bias_ref):
    total = one_ref[...] + other_ref[...]
    channels = total.shape[0]
    for tap in range(9):
        weight_ref[tap // 3, tap % 3] = total[:, tap * channels : (tap + 1) * channels]
    flipped = jnp.transpose(total[:, total.shape[1] - 128 :])
    bias_ref[...] = flipped[127:128, :channels]


def call(kernel, out_shapes, operands, scratch=(), flops=0, after=()):
    whole = pl.BlockSpec(memory_space=pltpu.VMEM)
    size = sum(math.prod(x.shape) * jnp.dtype(x.dtype).itemsize for x in (*operands, *out_shapes))
    return pl.pallas_call(
        kernel,
        out_shape=out_shapes,
        in_specs=[whole] * len(operands) + [pl.BlockSpec(memory_space=pl.ANY)] * len(after),
        out_specs=[whole] * len(out_shapes),
        scratch_shapes=list(scratch),
        compiler_params=pltpu.CompilerParams(vmem_limit_bytes=VMEM_BYTES),
        cost_estimate=pl.CostEstimate(flops=flops, bytes_accessed=size, transcendentals=0),
    )(*operands, *after)


def shards(image, weight, bias, cotangent):
    channels, height, width = image.shape
    bf16, f32 = jnp.bfloat16, jnp.float32
    scale = 1.0 / math.sqrt(height * lax.axis_size("row") * width * lax.axis_size("col"))
    shape = jax.ShapeDtypeStruct
    pieces = width // DILATION
    own_groups, all_groups = height // pieces, (height + 2 * DILATION) // pieces
    depth = 9 * channels
    stack = pltpu.VMEM((height // DILATION + 2, 3 * channels, DILATION * width), bf16)
    edge = shape((DILATION, channels, width), bf16)
    packed = shape((all_groups, channels, width), bf16)
    own_rims = shape((2, own_groups, channels, width), bf16)
    rows = shape((height, channels, width), bf16)
    flops = 2 * depth * channels * height * width

    odd = lax.axis_index("row") % 2
    outer = shape((2, DILATION, channels, width), bf16)
    end = height - DILATION


    def image_rim(start, first):
        rim = lax.dynamic_slice_in_dim(image, start, DILATION, 1)
        flag = alone("row", first)
        return rim if flag is None else jnp.where(flag, jnp.zeros_like(rim), rim)

    one = swap_pairs(image_rim((1 - odd) * end, 0), "row", 0)
    two = swap_pairs(image_rim(odd * end, 1), "row", 1)
    image_rows, rims = call(own_kernel, (rows, own_rims), (image,))
    forward_weight = jnp.transpose(weight, (2, 0, 1, 3)).reshape(channels, depth)
    backward_weight = jnp.transpose(weight[::-1, ::-1], (3, 0, 1, 2)).reshape(channels, depth)
    one, two, image_outer = call(
        functools.partial(rim_kernel, True), (packed, packed, outer), (one, two, rims)
    )
    two, one = swap_pairs(two, "col", 1), swap_pairs(one, "col", 0)
    activation, grads, one, two, rims, terms = call(
        functools.partial(forward_kernel, scale),
        (
            shape(image.shape, bf16), rows, edge, edge, own_rims,
            shape((channels, -(-(depth + 1) // 128) * 128), f32),
        ),
        (image_rows, image_outer, one, two, cotangent, forward_weight, bias[:, None]),
        (stack, pltpu.VMEM((channels, width), f32), pltpu.VMEM((depth, channels), f32)),
        2 * flops,
    )
    one, two = swap_pairs(one, "row", 0), swap_pairs(two, "row", 1)
    one, two, grad_outer = call(
        rim_after_kernel, (packed, packed, outer), (one, two, rims), after=(activation,)
    )
    two, one = swap_pairs(two, "col", 1), swap_pairs(one, "col", 0)
    grad_image, token = call(
        backward_kernel,
        (shape(image.shape, bf16), shape((8, 128), f32)),
        (grads, grad_outer, one, two, backward_weight),
        (stack,),
        flops,
    )
    one, other = add_pairs(terms, "col", "row")
    grad_weight, grad_bias = call(
        finish_kernel, (shape(weight.shape, f32), shape((1, channels), f32)), (one, other, token)
    )
    return (activation, grad_image, grad_weight, grad_bias.reshape(channels))


def solution(mesh):
    return jax.shard_map(
        shards,
        mesh=mesh,
        in_specs=(P(None, "row", "col"), P(), P(), P(None, "row", "col")),
        out_specs=(P(None, "row", "col"), P(None, "row", "col"), P(), P()),
        check_vma=False,
    )
```
